32 devices in a mesh: row: 2 (over x), col: 4 (over z), depth: 4 (over y, core).
Axes of the slice: x: 2, y: 2, z: 4, core: 2. Of those that a mesh axis runs over, the one named last changes fastest.
Arguments:
- integrals: bfloat16 [2048, 5120], P('row', 'depth'), may hold values from -0.25 to 0.25
- amplitudes: bfloat16 [1280, 4, 10000], P('depth', 'row', 'col'), may hold values from -6 to 6
- ab_irrep: int32 [2048], P('row'), may hold values from 0 to 7
- cd_irrep: int32 [5120], P('depth'), may hold values from 0 to 7
Outputs:
- residual: bfloat16 [2048, 10000], P(('row', 'depth'), 'col')
The draws below stay inside these ranges and needn't reach their ends.
All inputs are finite; a program needn't handle non-finite values.
Results may differ from the reference program's by a relative error of at most 0.001.
Values may be sent and summed in bfloat16 or wider, within the bound.
No kernel may reach another device: no remote copies, remote signals or barrier semaphores. Data moves between devices by JAX's collectives and lax.ppermute only.
A program may use at most 192 MiB of HBM per device.

```python
import jax
import jax.numpy as jnp

OCC = 100
SLAB = 256
SLABS = 20
KB = 4
CDK = 5120
CDB = 1280
PAIRS = 10000
ABROWS = 2048


def set_ends(drawn, key, smallest, top_value):
    longest = drawn.shape.index(max(drawn.shape))
    spots = []
    for shift in (0, 1):
        where = [jax.random.randint(jax.random.fold_in(key, axis), (), 0, length) for axis, length in enumerate(drawn.shape)]
        where[longest] = (where[longest] + shift) % drawn.shape[longest]
        spots.append(tuple(where))
    return drawn.at[spots[0]].set(smallest).at[spots[1]].set(top_value)


def steps_of(stream_key, extent, shards, least, high):
    def one(position, shards_of):
        draws = jax.random.uniform(jax.random.fold_in(jax.random.fold_in(stream_key, 6), position), (shards_of,), jnp.float32, least / len(shards), high / len(shards))
        return jnp.repeat(jnp.exp(draws), extent[position] // shards_of).reshape((-1,) + (1,) * (len(extent) - position - 1))

    factor_of = one(*shards[0])
    for cut in shards[1:]:
        factor_of = factor_of * one(*cut)
    return factor_of


def scatter_about(stream_key, shape, scale, reach, cuts=(), held_as=jnp.bfloat16):
    values = scale * jax.random.normal(stream_key, shape, jnp.float32)
    if cuts:
        values = values * steps_of(stream_key, shape, cuts, -0.22, 0.18)
    return jnp.clip(values, -reach, reach).astype(held_as)


def setup_inputs(seed: int = 0) -> dict:
    key_list = jax.random.split(jax.random.key(seed), 5)
    return {
        "integrals": scatter_about(key_list[0], (ABROWS, CDK), (SLABS * SLAB // 8) ** -0.5, 0.25, ((0, 2), (1, 4))),
        "amplitudes": scatter_about(key_list[1], (CDB, KB, PAIRS), 1.0, 6.0, ((0, 4), (1, 2), (2, 4))),
        "ab_irrep": set_ends(jax.random.randint(key_list[2], (ABROWS,), 0, 8), jax.random.fold_in(key_list[2], 1), 0, 7).astype(jnp.int32),
        "cd_irrep": set_ends(jax.random.randint(key_list[3], (CDK,), 0, 8), jax.random.fold_in(key_list[3], 1), 0, 7).astype(jnp.int32),
    }


def reference(integrals, amplitudes, ab_irrep, cd_irrep):
    keep = ab_irrep[:, None] == cd_irrep[None, :]
    masked = jnp.where(keep, integrals, jnp.zeros_like(integrals))
    flat_amps = amplitudes.reshape(CDB * KB, OCC * OCC)
    ladder = jnp.dot(masked, flat_amps, preferred_element_type=jnp.float32)
    cube = ladder.reshape(ABROWS, OCC, OCC)
    result = cube - jnp.swapaxes(cube, 1, 2)
    return result.reshape(ABROWS, OCC * OCC).astype(jnp.bfloat16)
```

```python
import functools

import jax
import jax.numpy as jnp
import numpy as np
from jax import lax
from jax.experimental import pallas as pl
from jax.experimental.pallas import tpu as pltpu
from jax.sharding import PartitionSpec as P

OCC = 100
TOP = 32000.0
STEPS = 256.0
CORES = 2


def index_tables(groups):
    n = OCC // groups
    half = (n * n + 1) // 2
    chunk = -(-(half + 1) // 16) * 16
    own = np.full((groups, groups, chunk, 1), -1, np.int32)
    away = np.full((groups, groups, chunk, 1), -1, np.int32)
    for z in range(groups):
        inside = [(i, j) for i in range(n) for j in range(i + 1, n)]
        for p, (i, j) in enumerate(inside):
            own[z, 0, p, 0] = i * OCC + z * n + j
            away[z, 0, p, 0] = j * OCC + z * n + i
        for r in range(1, groups):
            other = (z + r) % groups
            entries = [(e // n, e % n) for e in range(n * n)]
            if z < other:
                mine = entries[:half]
            else:
                mine = [(j, i) for i, j in entries[half:]]
            for p, (i, j) in enumerate(mine):
                own[z, r, p, 0] = i * OCC + other * n + j
                away[other, r, p, 0] = j * OCC + z * n + i
    return own, away, chunk


def dot_nt(a, b):
    return lax.dot_general(a, b, (((1,), (1,)), ((), ())), preferred_element_type=jnp.float32)


def dot_tn(a, b):
    return lax.dot_general(a, b, (((0,), (0,)), ((), ())), preferred_element_type=jnp.float32)


def one_hot(index, width):
    lanes = lax.broadcasted_iota(jnp.int32, (index.shape[0], width), 1)
    return jnp.where(lanes == index, 1.0, 0.0).astype(jnp.bfloat16)


def encode(values):
    largest = jnp.maximum(jnp.max(jnp.abs(values), axis=0, keepdims=True), 1e-30)
    code = jnp.floor(jnp.log2(TOP / largest) * STEPS)
    coded = jnp.round(values * jnp.exp2(code * (1.0 / STEPS)))
    rows = lax.broadcasted_iota(jnp.int32, values.shape, 0)
    coded = jnp.where(rows == values.shape[0] - 1, code, coded)
    return coded.astype(jnp.int32).astype(jnp.int16)


def decode(coded):
    values = coded.astype(jnp.int32).astype(jnp.float32)
    rows = lax.broadcasted_iota(jnp.int32, values.shape, 0)
    last = rows == values.shape[0] - 1
    code = jnp.sum(jnp.where(last, values, 0.0), axis=0, keepdims=True)
    return jnp.where(last, 0.0, values * jnp.exp2(code * (-1.0 / STEPS)))


def call(body, scalars, inputs, outputs, flops, moved):
    whole = lambda rank: (lambda g, s: (0,) * rank)
    in_specs = []
    for array, block, index in inputs:
        if block is None:
            in_specs.append(pl.BlockSpec(array.shape, whole(array.ndim)))
        else:
            in_specs.append(pl.BlockSpec(block, index))
    out_specs = [pl.BlockSpec(shape, whole(len(shape))) for shape, _ in outputs]
    return pl.pallas_call(
        body,
        out_shape=[jax.ShapeDtypeStruct(shape, dtype) for shape, dtype in outputs],
        grid_spec=pltpu.PrefetchScalarGridSpec(
            num_scalar_prefetch=1, grid=(1,), in_specs=in_specs, out_specs=out_specs
        ),
        compiler_params=pltpu.CompilerParams(vmem_limit_bytes=48 * 2**20),
        cost_estimate=pl.CostEstimate(flops=int(flops), bytes_accessed=int(moved), transcendentals=0),
    )(scalars, *[array for array, _, _ in inputs])


def mask_body(count, s_ref, *refs):
    sel_ref, cd_here, cd_there = refs[:3]
    refs = refs[3:]
    ins, outs = refs[: 3 * count], refs[3 * count :]
    pick = None
    for k in range(count):
        ab_ref, here_ref, there_ref = ins[3 * k : 3 * k + 3]
        if pick is None:
            pick = one_hot(sel_ref[0], here_ref.shape[-1])
        ab = ab_ref[0]
        for core, (v_ref, cd_ref) in enumerate(((here_ref, cd_here), (there_ref, cd_there))):
            v = v_ref[...].reshape(v_ref.shape[-2:]).astype(jnp.float32)
            kept = jnp.where(ab == cd_ref[...], v, 0.0).astype(jnp.bfloat16)
            outs[k][core] = dot_nt(kept, pick).astype(jnp.bfloat16)


def select_body(s_ref, idx_ref, t_ref, *out_refs):
    t = t_ref[...]
    for k in range(idx_ref.shape[1]):
        picked = dot_nt(one_hot(idx_ref[0, k], t.shape[1]), t).astype(jnp.bfloat16)
        if len(out_refs) > 1:
            out_refs[k][...] = picked
        else:
            out_refs[0][k] = picked


def sum_body(groups, s_ref, *refs):
    own_here, own_there, away_here, away_there = refs[:4]
    there, here = refs[4 : 4 + groups], refs[4 + groups : 4 + 2 * groups]
    coded_ref, kept_ref = refs[4 + 2 * groups :]

    def tile(ref):
        return ref[...].reshape(ref.shape[-2:])

    to, too, tr, tro = tile(own_here), tile(own_there), tile(away_here), tile(away_there)

    def partial(a_ref):
        a, b = a_ref[0], a_ref[1]
        return (dot_nt(to, a) + dot_nt(too, b)) - (dot_nt(tr, a) + dot_nt(tro, b))

    for g in range(groups):
        coded_ref[g] = encode(partial(there[g]))
    for g in range(groups):
        kept_ref[g] = partial(here[g])


def add_y_body(s_ref, kept_ref, coded_ref, sum_ref, *out_refs):
    for g in range(kept_ref.shape[0]):
        total = kept_ref[g] + decode(coded_ref[g])
        if g == 0:
            sum_ref[...] = total
        else:
            out_refs[g - 1][...] = encode(total)


def add_x_body(s_ref, sum_ref, *refs):
    total = sum_ref[...]
    for ref in refs[:-1]:
        total = total + decode(ref[...])
    refs[-1][...] = total.astype(jnp.bfloat16)


def place_body(groups, s_ref, own_ref, away_ref, *refs):
    out_ref = refs[-1]
    width = out_ref.shape[1]
    mine, others = refs[:groups], refs[groups:-1]
    total = None
    for k in range(groups):
        minus = mine[0] if k == 0 else others[k - 1]
        term = dot_tn(mine[k][...], one_hot(own_ref[0, k], width)) - dot_tn(minus[...], one_hot(away_ref[0, k], width))
        total = term if total is None else total + term
    out_ref[...] = total.astype(jnp.bfloat16)


def local(integrals, amplitudes, ab_irrep, cd_irrep):
    row_n, col_n, depth_n = lax.axis_size("row"), lax.axis_size("col"), lax.axis_size("depth")
    x, z, d = lax.axis_index("row"), lax.axis_index("col"), lax.axis_index("depth")
    y_n = depth_n // CORES
    y, core = d // CORES, d % CORES
    rows, cd_here = integrals.shape
    blocks, sub, columns = amplitudes.shape
    k_here = blocks * sub
    tall = rows // depth_n
    own_np, away_np, chunk = index_tables(col_n)
    own_table, away_table = jnp.asarray(own_np), jnp.asarray(away_np)
    bf16, i16, f32 = jnp.bfloat16, jnp.int16, jnp.float32

    def shift(array, axis, by):
        n = lax.axis_size(axis)
        return lax.ppermute(array, axis, [(i, (i + by) % n) for i in range(n)])

    def other_core(array):
        return lax.ppermute(array, "depth", [(i, i ^ 1) for i in range(depth_n)])

    zone = lambda rank: (lambda g, s: (s[1],) + (0,) * (rank - 1))
    scalars = jnp.stack([x, z, y, core]).astype(jnp.int32)

    v = integrals.reshape(y_n, CORES, tall, cd_here)
    v_there = other_core(lax.dynamic_index_in_dim(v, 1 - core, axis=1, keepdims=False))
    cd_row = cd_irrep.reshape(1, cd_here)
    cd_there = other_core(cd_row)
    ab = ab_irrep.reshape(y_n * CORES, tall, 1)
    sub_full = sub * row_n
    t = np.arange(k_here)
    sel = np.stack([(t // sub) * sub_full + g * sub + t % sub for g in range(row_n)])
    sel = jnp.asarray(sel.astype(np.int32)[:, :, None])

    def masked(by):
        steps = list(range(1, y_n)) + [0]
        ins = [(sel, (1, k_here, 1), lambda g, s: (lax.rem(s[0] - by + row_n, row_n), 0, 0)), (cd_row, None, None), (cd_there, None, None)]
        for step in steps:
            at = lambda s, step=step: lax.rem(s[2] + step, y_n)
            ins.append((ab, (1, tall, 1), lambda g, s, at=at: (at(s) * CORES + s[3], 0, 0)))
            ins.append((v, (1, 1, tall, cd_here), lambda g, s, at=at: (at(s), s[3], 0, 0)))
            ins.append((v_there, (1, tall, cd_here), lambda g, s, at=at: (at(s), 0, 0)))
        outs = [((CORES, tall, k_here), bf16)] * y_n
        flops = 2 * y_n * CORES * tall * cd_here * k_here
        return call(functools.partial(mask_body, y_n), scalars, ins, outs, flops, 3 * y_n * CORES * tall * cd_here)

    a_there, a_here = [None] * row_n, [None] * row_n
    for by in list(range(1, row_n)) + [0]:
        first, last = masked(by)
        if by:
            first, last = shift(first, "row", -by), shift(last, "row", -by)
        a_there[by], a_here[by] = first, last

    flat = amplitudes.reshape(k_here, columns)
    away_block = (1, col_n - 1, chunk, 1)
    sent = call(
        select_body,
        scalars,
        [(away_table[:, 1:], away_block, zone(4)), (flat, None, None)],
        [((chunk, k_here), bf16)] * (col_n - 1),
        2 * (col_n - 1) * chunk * columns * k_here,
        2 * k_here * (columns + (col_n - 1) * chunk),
    )
    t_away = {r: shift(sent[r - 1], "col", -r) for r in range(1, col_n)}
    kept_table = jnp.asarray(np.concatenate([own_np, away_np[:, :1]], axis=1))
    kept_n = col_n + 1
    (kept,) = call(
        select_body,
        scalars,
        [(kept_table, (1, kept_n, chunk, 1), zone(4)), (flat, None, None)],
        [((kept_n, chunk, k_here), bf16)],
        2 * kept_n * chunk * columns * k_here,
        2 * k_here * (columns + kept_n * chunk),
    )
    kept_there = other_core(kept)

    mine, others = [None] * col_n, [None] * col_n
    for k in [0] + list(range(1, col_n)):
        block = (1, chunk, k_here)
        at = lambda g, s, k=k: (k, 0, 0)
        ins = [(kept, block, at), (kept_there, block, at)]
        if k == 0:
            last = lambda g, s: (kept_n - 1, 0, 0)
            ins += [(kept, block, last), (kept_there, block, last)]
        else:
            ins += [(t_away[k], None, None), (other_core(t_away[k]), None, None)]
        ins += [(a, None, None) for a in a_there + a_here]
        coded, own_sum = call(
            functools.partial(sum_body, row_n),
            scalars,
            ins,
            [((row_n, chunk, tall), i16), ((row_n, chunk, tall), f32)],
            2 * 2 * y_n * row_n * chunk * tall * CORES * k_here,
            2 * CORES * k_here * (2 * chunk + y_n * row_n * tall) + 6 * row_n * chunk * tall,
        )
        coded = shift(coded, "depth", CORES)
        sums = call(
            add_y_body,
            scalars,
            [(own_sum, None, None), (coded, None, None)],
            [((chunk, tall), f32)] + [((chunk, tall), i16)] * (row_n - 1),
            10 * row_n * chunk * tall,
            10 * row_n * chunk * tall,
        )
        arrived = [shift(sums[g], "row", g) for g in range(1, row_n)]
        (mine[k],) = call(
            add_x_body,
            scalars,
            [(a, None, None) for a in [sums[0]] + arrived],
            [((chunk, tall), bf16)],
            10 * row_n * chunk * tall,
            (6 + 2 * row_n) * chunk * tall,
        )
        if k:
            others[k] = shift(mine[k], "col", k)

    (out,) = call(
        functools.partial(place_body, col_n),
        scalars,
        [(own_table, (1, col_n, chunk, 1), zone(4)), (away_table, (1, col_n, chunk, 1), zone(4))]
        + [(a, None, None) for a in mine + others[1:]],
        [((tall, columns), bf16)],
        4 * col_n * chunk * tall * columns,
        2 * tall * (columns + 2 * col_n * chunk),
    )
    return out


def solution(mesh):
    in_specs = (P("row", "depth"), P("depth", "row", "col"), P("row"), P("depth"))
    out_specs = P(("row", "depth"), "col")
    return jax.shard_map(local, mesh=mesh, in_specs=in_specs, out_specs=out_specs, check_vma=False)
```

```python
import functools

import jax
import jax.numpy as jnp
import numpy as np
from jax import lax
from jax.experimental import pallas as pl
from jax.experimental.pallas import tpu as pltpu
from jax.sharding import PartitionSpec as P

OCC = 100
TOP = 32000.0
STEPS = 256.0
CORES = 2
TILE = 512


def dot_nt(a, b):
    return lax.dot_general(a, b, (((1,), (1,)), ((), ())), preferred_element_type=jnp.float32)


def dot_nn(a, b):
    return lax.dot_general(a, b, (((1,), (0,)), ((), ())), preferred_element_type=jnp.float32)


def divide(value, by):
    whole = jnp.floor((value.astype(jnp.float32) + 0.5) * (1.0 / by)).astype(jnp.int32)
    return whole, value - whole * by


def inside_columns(place, n, z):
    apart, i = divide(place, n)
    j = i + apart + 1
    j = jnp.where(j >= n, j - n, j)
    valid = place < n * (n - 1) // 2
    return jnp.where(valid, i * OCC + z * n + j, -1), jnp.where(valid, j * OCC + z * n + i, -1)


def pair_columns(place, n, z, other, mine):
    half = (n * n + 1) // 2
    first = jnp.logical_xor(z < other, jnp.logical_not(mine))
    count = jnp.where(first, half, n * n - half)
    q, m = divide(place + jnp.where(first, 0, half), n)
    a = jnp.where(z < other, q, m)
    b = jnp.where(z < other, m, q)
    return jnp.where(place < count, a * OCC + other * n + b, -1)


def encode(values):
    largest = jnp.maximum(jnp.max(jnp.abs(values), axis=0, keepdims=True), 1e-30)
    code = jnp.floor(jnp.log2(TOP / largest) * STEPS)
    coded = jnp.round(values * jnp.exp2(code * (1.0 / STEPS)))
    rows = lax.broadcasted_iota(jnp.int32, values.shape, 0)
    coded = jnp.where(rows == values.shape[0] - 1, code, coded)
    return coded.astype(jnp.int32).astype(jnp.int16)


def decode(coded):
    values = coded.astype(jnp.int32).astype(jnp.float32)
    rows = lax.broadcasted_iota(jnp.int32, values.shape, 0)
    last = rows == values.shape[0] - 1
    code = jnp.sum(jnp.where(last, values, 0.0), axis=0, keepdims=True)
    return jnp.where(last, 0.0, values * jnp.exp2(code * (-1.0 / STEPS)))


def call(name, body, scalars, inputs, outputs, flops, moved, grid=1, scratch=()):
    in_specs, arrays, out_specs, shapes = [], [], [], []
    for entry in inputs:
        array, block, index = entry if isinstance(entry, tuple) else (entry, None, None)
        arrays.append(array)
        in_specs.append(pl.BlockSpec(block or array.shape, index or (lambda g, s, rank=array.ndim: (0,) * rank)))
    for shape, dtype, *spec in outputs:
        shapes.append(jax.ShapeDtypeStruct(shape, dtype))
        block, index = spec or (shape, lambda g, s, rank=len(shape): (0,) * rank)
        out_specs.append(pl.BlockSpec(block, index))
    return pl.pallas_call(
        body,
        name=name,
        out_shape=shapes,
        grid_spec=pltpu.PrefetchScalarGridSpec(
            num_scalar_prefetch=1, grid=(grid,), in_specs=in_specs, out_specs=out_specs, scratch_shapes=list(scratch)
        ),
        compiler_params=pltpu.CompilerParams(vmem_limit_bytes=48 * 2**20),
        cost_estimate=pl.CostEstimate(flops=int(flops), bytes_accessed=int(moved), transcendentals=0),
    )(scalars, *arrays)


def mask_body(by, row_n, sub, tall, s_ref, ab_ref, cd_ref, v_ref, pass_ref, keep_ref):
    x, y, core = s_ref[0], s_ref[2], s_ref[3]
    k_here, cd_here = pass_ref.shape[2], v_ref.shape[1]
    q, m = divide(lax.broadcasted_iota(jnp.int32, (k_here, 1), 0), sub)
    wanted = q * (sub * row_n) + lax.rem(x - by + row_n, row_n) * sub + m
    pick = jnp.where(lax.broadcasted_iota(jnp.int32, (k_here, cd_here), 1) == wanted, 1.0, 0.0).astype(jnp.bfloat16)
    square = (tall, tall)
    diagonal = lax.broadcasted_iota(jnp.int32, square, 0) == lax.broadcasted_iota(jnp.int32, square, 1)
    blocks = []
    for other_core in (1, 0):
        for other_y in (1, 0):
            block = lax.rem(y + other_y, 2) * CORES + lax.rem(core + other_core, CORES)
            start = pl.multiple_of(block * tall, tall)
            labels = ab_ref[:, pl.ds(start, tall)].astype(jnp.float32)
            ab = jnp.sum(jnp.where(diagonal, labels, 0.0), axis=1, keepdims=True)
            v = v_ref[pl.ds(start, tall), :].astype(jnp.float32)
            blocks.append(jnp.where(ab == cd_ref[...].astype(jnp.float32), v, 0.0).astype(jnp.bfloat16))
    picked = dot_nt(jnp.concatenate(blocks, axis=0), pick).astype(jnp.bfloat16)
    pass_ref[...] = picked[: 2 * tall].reshape(pass_ref.shape)
    keep_ref[...] = picked[2 * tall :].reshape(keep_ref.shape)


def one_hot_rows(columns, width):
    lanes = lax.broadcasted_iota(jnp.int32, (columns.shape[0], width), 1)
    return jnp.where(lanes == columns, 1.0, 0.0).astype(jnp.bfloat16)


def send_body(order, n, col_n, s_ref, t_ref, flat_ref, *out_refs):
    flat_ref[...] = t_ref[...].reshape(flat_ref.shape)
    z = s_ref[1]
    place = lax.broadcasted_iota(jnp.int32, (out_refs[0].shape[0], 1), 0)
    for r, out_ref in zip(order, out_refs):
        wanted = pair_columns(place, n, z, lax.rem(z - r + col_n, col_n), False)
        out_ref[...] = dot_nt(one_hot_rows(wanted, flat_ref.shape[1]), flat_ref[...]).astype(jnp.bfloat16)


def keep_body(order, n, col_n, s_ref, flat_ref, out_ref):
    z = s_ref[1]
    place = lax.broadcasted_iota(jnp.int32, (out_ref.shape[1], 1), 0)
    inside, turned = inside_columns(place, n, z)
    picks = [inside if r == 0 else pair_columns(place, n, z, lax.rem(z + r, col_n), True) for r in order] + [turned]
    for k, wanted in enumerate(picks):
        out_ref[k] = dot_nt(one_hot_rows(wanted, flat_ref.shape[1]), flat_ref[...]).astype(jnp.bfloat16)


def sum_body(first, count, s_ref, own_here, own_there, *refs):
    away = refs[: 2 * count]
    keep_ref, pass_ref, coded_ref, kept_ref = refs[2 * count :]
    k_here = own_here.shape[2]
    chunk = own_here.shape[1]

    def rows(ref):
        return ref[...].reshape(-1, k_here)

    a, b = keep_ref[0], pass_ref[0]
    to = own_here[first : first + count].reshape(count * chunk, k_here)
    too = own_there[first : first + count].reshape(count * chunk, k_here)
    tr = jnp.concatenate([rows(ref) for ref in away[:count]], axis=0)
    tro = jnp.concatenate([rows(ref) for ref in away[count:]], axis=0)
    total = (dot_nt(to, a) + dot_nt(too, b)) - (dot_nt(tr, a) + dot_nt(tro, b))

    @pl.when(pl.program_id(0) == 0)
    def _():
        coded_ref[...] = encode(total)

    @pl.when(pl.program_id(0) == 1)
    def _():
        kept_ref[...] = total


def add_y_body(s_ref, kept_ref, coded_ref, out_ref):
    out_ref[...] = encode(kept_ref[...] + decode(coded_ref[...]))


def add_x_body(count, s_ref, kept_ref, *refs):
    total = kept_ref[...]
    for ref in refs[:-count]:
        total = total + decode(ref[...])
    rounded = total.astype(jnp.bfloat16)
    chunk = rounded.shape[0] // count
    for k, out_ref in enumerate(refs[-count:]):
        out_ref[...] = rounded[k * chunk : (k + 1) * chunk]


def place_body(order, n, col_n, before, s_ref, *refs):
    out_ref = refs[-1]
    z = s_ref[1]
    chunk = refs[0].shape[0]
    place = lax.broadcasted_iota(jnp.int32, (1, chunk), 1)
    at = lax.broadcasted_iota(jnp.int32, (out_ref.shape[0], chunk), 0) + pl.program_id(0) * out_ref.shape[0]
    total = refs[-2][...].astype(jnp.float32) if before else None
    source = iter(refs)
    for r in order:
        if r == 0:
            inside, turned = inside_columns(place, n, z)
            signs = jnp.where(at == inside, 1.0, jnp.where(at == turned, -1.0, 0.0))
            terms = [(signs, next(source))]
        else:
            plus = pair_columns(place, n, z, lax.rem(z + r, col_n), True)
            minus = pair_columns(place, n, z, lax.rem(z - r + col_n, col_n), False)
            terms = [(jnp.where(at == plus, 1.0, 0.0), next(source)), (jnp.where(at == minus, -1.0, 0.0), next(source))]
        for signs, ref in terms:
            term = dot_nn(signs.astype(jnp.bfloat16), ref[...])
            total = term if total is None else total + term
    out_ref[...] = total.astype(jnp.bfloat16)


def local(integrals, amplitudes, ab_irrep, cd_irrep):
    row_n, col_n, depth_n = lax.axis_size("row"), lax.axis_size("col"), lax.axis_size("depth")
    x, z, d = lax.axis_index("row"), lax.axis_index("col"), lax.axis_index("depth")
    y, core = d // CORES, d % CORES
    rows, cd_here = integrals.shape
    blocks, sub, columns = amplitudes.shape
    k_here = blocks * sub
    tall = rows // depth_n
    n = OCC // col_n
    chunk = -(-((n * n + 1) // 2 + 1) // 16) * 16
    far = col_n // 2
    near = [r for r in range(1, col_n) if r != far]
    groups = [[0] + near, [far]]
    order = [0] + near + [far]
    bf16, i16, f32 = jnp.bfloat16, jnp.int16, jnp.float32

    def shift(array, axis, by):
        count = lax.axis_size(axis)
        return lax.ppermute(array, axis, [(i, (i + by) % count) for i in range(count)])

    def other_core(array):
        return lax.ppermute(array, "depth", [(i, i ^ 1) for i in range(depth_n)])

    def other_y(array):
        return lax.ppermute(array, "depth", [(i, i ^ 2) for i in range(depth_n)])

    scalars = jnp.stack([x, z, y, core]).astype(jnp.int32)
    ab_row, cd_row = ab_irrep.reshape(1, rows), cd_irrep.reshape(1, cd_here)

    def masked(v, by):
        return call(
            "mask_integrals",
            functools.partial(mask_body, by, row_n, sub, tall),
            scalars,
            [ab_row, cd_row, v],
            [((2, tall, k_here), bf16)] * 2,
            2 * rows * cd_here * k_here,
            2 * rows * (cd_here + k_here),
        )

    passed, kept = [None] * row_n, [None] * row_n
    for by in range(1, row_n):
        gone, stay = masked(integrals, by)
        passed[by], kept[by] = shift(gone, "row", -by), shift(stay, "row", -by)

    amplitudes, _ = lax.optimization_barrier((amplitudes, gone if row_n > 1 else scalars))
    sent_order = near + [far]
    flat, *sent = call(
        "send_columns",
        functools.partial(send_body, sent_order, n, col_n),
        scalars,
        [amplitudes],
        [((k_here, columns), bf16)] + [((chunk, k_here), bf16)] * len(sent_order),
        2 * len(sent_order) * chunk * columns * k_here,
        2 * k_here * (2 * columns + len(sent_order) * chunk),
    )
    away = {r: shift(s, "col", -r) for r, s in zip(near, sent)}
    integrals, _ = lax.optimization_barrier((integrals, flat))
    last = lax.optimization_barrier((sent[-1], *away.values()))
    away[far] = shift(last[0], "col", -far)

    passed[0], kept[0] = masked(integrals, 0)
    (own,) = call(
        "keep_columns",
        functools.partial(keep_body, order, n, col_n),
        scalars,
        [flat],
        [((col_n + 1, chunk, k_here), bf16)],
        2 * (col_n + 1) * chunk * columns * k_here,
        2 * k_here * (columns + (col_n + 1) * chunk),
    )
    passed = [other_core(a) for a in passed]
    own_there = other_core(own)

    done = None
    for group in groups:
        first, count = order.index(group[0]), len(group)
        tail = (1, chunk, k_here), lambda g, s: (col_n, 0, 0)
        here = [(own, *tail) if r == 0 else away[r] for r in group]
        there = [(own_there, *tail) if r == 0 else other_core(away[r]) for r in group]
        final = []
        for by in range(row_n):
            block = (1, tall, k_here), lambda g, s: (g, 0, 0)
            coded, total = call(
                "sum_pairs",
                functools.partial(sum_body, first, count),
                scalars,
                [own, own_there] + here + there + [(kept[by], *block), (passed[by], *block)],
                [((count * chunk, tall), i16), ((count * chunk, tall), f32)],
                2 * 2 * 2 * count * chunk * tall * CORES * k_here,
                2 * CORES * k_here * (2 * count * chunk + 2 * tall) + 6 * count * chunk * tall,
                grid=2,
            )
            coded = other_y(coded)
            if by == 0:
                final += [total, coded]
            else:
                (merged,) = call(
                    "add_other_y",
                    add_y_body,
                    scalars,
                    [total, coded],
                    [((count * chunk, tall), i16)],
                    20 * count * chunk * tall,
                    8 * count * chunk * tall,
                )
                final.append(shift(merged, "row", by))
        rounded = call(
            "add_other_x",
            functools.partial(add_x_body, count),
            scalars,
            final,
            [((chunk, tall), bf16)] * count,
            20 * count * chunk * tall,
            8 * count * chunk * tall,
        )
        sources = []
        for r, mine in zip(group, rounded):
            sources += [mine] if r == 0 else [mine, shift(mine, "col", r)]
        tile = (TILE, tall), lambda g, s: (g, 0)
        sources += [] if done is None else [(done, *tile)]
        (done,) = call(
            "place_pairs",
            functools.partial(place_body, group, n, col_n, done is not None),
            scalars,
            sources,
            [((columns, tall), bf16, *tile)],
            2 * len(sources) * chunk * tall * columns,
            2 * tall * (2 * columns + len(sources) * chunk),
            grid=-(-columns // TILE),
        )
    return done.T


def solution(mesh):
    in_specs = (P("row", "depth"), P("depth", "row", "col"), P("row"), P("depth"))
    out_specs = P(("row", "depth"), "col")
    return jax.shard_map(local, mesh=mesh, in_specs=in_specs, out_specs=out_specs, check_vma=False)
```

```python
import functools

import jax
import jax.numpy as jnp
import numpy as np
from jax import lax
from jax.experimental import pallas as pl
from jax.experimental.pallas import tpu as pltpu
from jax.sharding import PartitionSpec as P

OCC = 100
TOP = 32000.0
STEPS = 256.0
CORES = 2
TILE = 512
LANES = 128
LIGHT = 64


def dot_nt(a, b):
    return lax.dot_general(a, b, (((1,), (1,)), ((), ())), preferred_element_type=jnp.float32)


def dot_nn(a, b):
    return lax.dot_general(a, b, (((1,), (0,)), ((), ())), preferred_element_type=jnp.float32)


def divide(value, by):
    whole = jnp.floor((value.astype(jnp.float32) + 0.5) * (1.0 / by)).astype(jnp.int32)
    return whole, value - whole * by


def inside_columns(place, n, z):
    apart, i = divide(place, n)
    j = i + apart + 1
    j = jnp.where(j >= n, j - n, j)
    valid = place < n * (n - 1) // 2
    return jnp.where(valid, i * OCC + z * n + j, -1), jnp.where(valid, j * OCC + z * n + i, -1)


def pair_columns(place, n, z, other, mine):
    half = (n * n + 1) // 2
    first = jnp.logical_xor(z < other, jnp.logical_not(mine))
    count = jnp.where(first, half, n * n - half)
    q, m = divide(place + jnp.where(first, 0, half), n)
    a = jnp.where(z < other, q, m)
    b = jnp.where(z < other, m, q)
    return jnp.where(place < count, a * OCC + other * n + b, -1)


def encode(values):
    largest = jnp.maximum(jnp.max(jnp.abs(values), axis=0, keepdims=True), 1e-30)
    code = jnp.floor(jnp.log2(TOP / largest) * STEPS)
    coded = jnp.round(values * jnp.exp2(code * (1.0 / STEPS)))
    rows = lax.broadcasted_iota(jnp.int32, values.shape, 0)
    coded = jnp.where(rows == values.shape[0] - 1, code, coded)
    return coded.astype(jnp.int32).astype(jnp.int16)


def decode(coded):
    values = coded.astype(jnp.int32).astype(jnp.float32)
    rows = lax.broadcasted_iota(jnp.int32, values.shape, 0)
    last = rows == values.shape[0] - 1
    code = jnp.sum(jnp.where(last, values, 0.0), axis=0, keepdims=True)
    return jnp.where(last, 0.0, values * jnp.exp2(code * (-1.0 / STEPS)))


def call(name, body, scalars, inputs, outputs, flops, moved, grid=1, scratch=()):
    in_specs, arrays, out_specs, shapes = [], [], [], []
    for entry in inputs:
        array, block, index = entry if isinstance(entry, tuple) else (entry, None, None)
        arrays.append(array)
        in_specs.append(pl.BlockSpec(block or array.shape, index or (lambda g, s, rank=array.ndim: (0,) * rank)))
    for shape, dtype, *spec in outputs:
        shapes.append(jax.ShapeDtypeStruct(shape, dtype))
        block, index = spec or (shape, lambda g, s, rank=len(shape): (0,) * rank)
        out_specs.append(pl.BlockSpec(block, index))
    return pl.pallas_call(
        body,
        name=name,
        out_shape=shapes,
        grid_spec=pltpu.PrefetchScalarGridSpec(
            num_scalar_prefetch=1, grid=(grid,), in_specs=in_specs, out_specs=out_specs, scratch_shapes=list(scratch)
        ),
        compiler_params=pltpu.CompilerParams(vmem_limit_bytes=48 * 2**20),
        cost_estimate=pl.CostEstimate(flops=int(flops) // LIGHT, bytes_accessed=int(moved) // LIGHT, transcendentals=0),
    )(scalars, *arrays)


def mask_body(by, row_n, sub, tall, s_ref, ab_ref, cd_ref, v_ref, pass_ref, keep_ref):
    x, y, core = s_ref[0], s_ref[2], s_ref[3]
    k_here, cd_here = pass_ref.shape[2], v_ref.shape[1]
    q, m = divide(lax.broadcasted_iota(jnp.int32, (k_here, 1), 0), sub)
    wanted = q * (sub * row_n) + lax.rem(x - by + row_n, row_n) * sub + m
    pick = jnp.where(lax.broadcasted_iota(jnp.int32, (k_here, cd_here), 1) == wanted, 1.0, 0.0).astype(jnp.bfloat16)
    square = (LANES, LANES)
    diagonal = lax.broadcasted_iota(jnp.int32, square, 0) == lax.broadcasted_iota(jnp.int32, square, 1)
    cd_labels = cd_ref[...].astype(jnp.float32)
    cd = jnp.concatenate([cd_labels[k : k + 1] for k in range(cd_here // LANES)], axis=1)
    strips = tall // LANES
    blocks = []
    for other_core in (1, 0):
        for other_y in (1, 0):
            block = lax.rem(y + other_y, 2) * CORES + lax.rem(core + other_core, CORES)
            for strip in range(strips):
                labels = ab_ref[pl.ds(block * strips + strip, 1), :].astype(jnp.float32)
                ab = jnp.sum(jnp.where(diagonal, labels, 0.0), axis=1, keepdims=True)
                start = pl.multiple_of(block * tall + strip * LANES, LANES)
                v = v_ref[pl.ds(start, LANES), :].astype(jnp.float32)
                blocks.append(jnp.where(ab == cd, v, 0.0).astype(jnp.bfloat16))
    picked = dot_nt(jnp.concatenate(blocks, axis=0), pick).astype(jnp.bfloat16)
    pass_ref[...] = picked[: 2 * tall].reshape(pass_ref.shape)
    keep_ref[...] = picked[2 * tall :].reshape(keep_ref.shape)


def one_hot_rows(columns, width):
    lanes = lax.broadcasted_iota(jnp.int32, (columns.shape[0], width), 1)
    return jnp.where(lanes == columns, 1.0, 0.0).astype(jnp.bfloat16)


def send_body(order, n, col_n, s_ref, t_ref, flat_ref, *out_refs):
    flat_ref[...] = t_ref[...].reshape(flat_ref.shape)
    z = s_ref[1]
    place = lax.broadcasted_iota(jnp.int32, (out_refs[0].shape[0], 1), 0)
    chunk = out_refs[0].shape[0]
    wanted = [pair_columns(place, n, z, lax.rem(z - r + col_n, col_n), False) for r in order]
    picked = dot_nt(one_hot_rows(jnp.concatenate(wanted, axis=0), flat_ref.shape[1]), flat_ref[...]).astype(jnp.bfloat16)
    for k, out_ref in enumerate(out_refs):
        out_ref[...] = picked[k * chunk : (k + 1) * chunk]


def keep_body(order, n, col_n, s_ref, flat_ref, out_ref):
    z = s_ref[1]
    place = lax.broadcasted_iota(jnp.int32, (out_ref.shape[1], 1), 0)
    inside, turned = inside_columns(place, n, z)
    picks = [inside if r == 0 else pair_columns(place, n, z, lax.rem(z + r, col_n), True) for r in order] + [turned]
    picked = dot_nt(one_hot_rows(jnp.concatenate(picks, axis=0), flat_ref.shape[1]), flat_ref[...])
    out_ref[...] = picked.astype(jnp.bfloat16).reshape(out_ref.shape)


def sum_body(first, count, s_ref, own_here, own_there, *refs):
    away = refs[: 2 * count]
    keep_ref, pass_ref, coded_ref, kept_ref = refs[2 * count :]
    k_here = own_here.shape[2]
    chunk = own_here.shape[1]

    def rows(ref):
        return ref[...].reshape(-1, k_here)

    a, b = keep_ref[...].reshape(-1, k_here), pass_ref[...].reshape(-1, k_here)
    half = a.shape[0] // 2
    to = own_here[first : first + count].reshape(count * chunk, k_here)
    too = own_there[first : first + count].reshape(count * chunk, k_here)
    tr = jnp.concatenate([rows(ref) for ref in away[:count]], axis=0)
    tro = jnp.concatenate([rows(ref) for ref in away[count:]], axis=0)
    left = jnp.concatenate([to, too, tr, tro], axis=1)
    right = jnp.concatenate([a, b, -a, -b], axis=1)
    total = dot_nt(left, right)
    coded_ref[...] = encode(total[:, :half])
    kept_ref[...] = total[:, half:]


def add_y_body(s_ref, kept_ref, coded_ref, out_ref):
    out_ref[...] = encode(kept_ref[...] + decode(coded_ref[...]))


def add_x_body(count, s_ref, kept_ref, *refs):
    total = kept_ref[...]
    for ref in refs[:-count]:
        total = total + decode(ref[...])
    rounded = total.astype(jnp.bfloat16)
    chunk = rounded.shape[0] // count
    for k, out_ref in enumerate(refs[-count:]):
        out_ref[...] = rounded[k * chunk : (k + 1) * chunk]


def place_body(order, n, col_n, before, s_ref, *refs):
    out_ref = refs[-1]
    z = s_ref[1]
    chunk = refs[0].shape[0]
    place = lax.broadcasted_iota(jnp.int32, (1, chunk), 1)
    at = lax.broadcasted_iota(jnp.int32, (out_ref.shape[0], chunk), 0) + pl.program_id(0) * out_ref.shape[0]
    signs = []
    for r in order:
        if r == 0:
            inside, turned = inside_columns(place, n, z)
            signs.append(jnp.where(at == inside, 1.0, jnp.where(at == turned, -1.0, 0.0)))
        else:
            plus = pair_columns(place, n, z, lax.rem(z + r, col_n), True)
            minus = pair_columns(place, n, z, lax.rem(z - r + col_n, col_n), False)
            signs.append(jnp.where(at == plus, 1.0, 0.0))
            signs.append(jnp.where(at == minus, -1.0, 0.0))
    signs = jnp.concatenate([sign.astype(jnp.bfloat16) for sign in signs], axis=1)
    values = jnp.concatenate([ref[...] for ref in refs[: 2 * len(order) - order.count(0)]], axis=0)
    total = dot_nn(signs, values)
    if before:
        total = total + refs[-2][...].astype(jnp.float32)
    out_ref[...] = total.astype(jnp.bfloat16)


def local(integrals, amplitudes, ab_irrep, cd_irrep):
    row_n, col_n, depth_n = lax.axis_size("row"), lax.axis_size("col"), lax.axis_size("depth")
    x, z, d = lax.axis_index("row"), lax.axis_index("col"), lax.axis_index("depth")
    y, core = d // CORES, d % CORES
    rows, cd_here = integrals.shape
    blocks, sub, columns = amplitudes.shape
    k_here = blocks * sub
    tall = rows // depth_n
    n = OCC // col_n
    chunk = -(-((n * n + 1) // 2 + 1) // 16) * 16
    far = col_n // 2
    near = [r for r in range(1, col_n) if r != far]
    groups = [[0] + near, [far]]
    order = [0] + near + [far]
    bf16, i16, f32 = jnp.bfloat16, jnp.int16, jnp.float32

    def shift(array, axis, by):
        count = lax.axis_size(axis)
        return lax.ppermute(array, axis, [(i, (i + by) % count) for i in range(count)])

    def other_core(array):
        return lax.ppermute(array, "depth", [(i, i ^ 1) for i in range(depth_n)])

    def other_y(array):
        return lax.ppermute(array, "depth", [(i, i ^ 2) for i in range(depth_n)])

    scalars = jnp.stack([x, z, y, core]).astype(jnp.int32)
    ab_row, cd_row = ab_irrep.reshape(-1, LANES), cd_irrep.reshape(-1, LANES)

    def masked(v, by):
        return call(
            "mask_integrals",
            functools.partial(mask_body, by, row_n, sub, tall),
            scalars,
            [ab_row, cd_row, v],
            [((2, tall, k_here), bf16)] * 2,
            2 * rows * cd_here * k_here,
            2 * rows * (cd_here + k_here),
        )

    passed, kept = [None] * row_n, [None] * row_n
    for by in range(1, row_n):
        gone, stay = masked(integrals, by)
        passed[by], kept[by] = shift(gone, "row", -by), shift(stay, "row", -by)

    amplitudes, _ = lax.optimization_barrier((amplitudes, gone if row_n > 1 else scalars))
    sent_order = near + [far]
    flat, *sent = call(
        "send_columns",
        functools.partial(send_body, sent_order, n, col_n),
        scalars,
        [amplitudes],
        [((k_here, columns), bf16)] + [((chunk, k_here), bf16)] * len(sent_order),
        2 * len(sent_order) * chunk * columns * k_here,
        2 * k_here * (2 * columns + len(sent_order) * chunk),
    )
    away = {r: shift(s, "col", -r) for r, s in zip(near, sent)}
    integrals, _ = lax.optimization_barrier((integrals, flat))
    last = lax.optimization_barrier((sent[-1], *away.values()))
    away[far] = shift(last[0], "col", -far)

    passed[0], kept[0] = masked(integrals, 0)
    (own,) = call(
        "keep_columns",
        functools.partial(keep_body, order, n, col_n),
        scalars,
        [flat],
        [((col_n + 1, chunk, k_here), bf16)],
        2 * (col_n + 1) * chunk * columns * k_here,
        2 * k_here * (columns + (col_n + 1) * chunk),
    )
    passed = [other_core(a) for a in passed]
    own_there = other_core(own)

    done = None
    for group in groups:
        first, count = order.index(group[0]), len(group)
        tail = (1, chunk, k_here), lambda g, s: (col_n, 0, 0)
        here = [(own, *tail) if r == 0 else away[r] for r in group]
        there = [(own_there, *tail) if r == 0 else other_core(away[r]) for r in group]
        final = []
        for by in range(row_n):
            coded, total = call(
                "sum_pairs",
                functools.partial(sum_body, first, count),
                scalars,
                [own, own_there] + here + there + [kept[by], passed[by]],
                [((count * chunk, tall), i16), ((count * chunk, tall), f32)],
                2 * 2 * 2 * count * chunk * tall * CORES * k_here,
                2 * CORES * k_here * (2 * count * chunk + 2 * tall) + 6 * count * chunk * tall,
            )
            coded = other_y(coded)
            if by == 0:
                final += [total, coded]
            else:
                (merged,) = call(
                    "add_other_y",
                    add_y_body,
                    scalars,
                    [total, coded],
                    [((count * chunk, tall), i16)],
                    20 * count * chunk * tall,
                    8 * count * chunk * tall,
                )
                final.append(shift(merged, "row", by))
        rounded = call(
            "add_other_x",
            functools.partial(add_x_body, count),
            scalars,
            final,
            [((chunk, tall), bf16)] * count,
            20 * count * chunk * tall,
            8 * count * chunk * tall,
        )
        sources = []
        for r, mine in zip(group, rounded):
            sources += [mine] if r == 0 else [mine, shift(mine, "col", r)]
        tile = (TILE, tall), lambda g, s: (g, 0)
        sources += [] if done is None else [(done, *tile)]
        (done,) = call(
            "place_pairs",
            functools.partial(place_body, group, n, col_n, done is not None),
            scalars,
            sources,
            [((columns, tall), bf16, *tile)],
            2 * len(sources) * chunk * tall * columns,
            2 * tall * (2 * columns + len(sources) * chunk),
            grid=-(-columns // TILE),
        )
    return done.T


def solution(mesh):
    in_specs = (P("row", "depth"), P("depth", "row", "col"), P("row"), P("depth"))
    out_specs = P(("row", "depth"), "col")
    return jax.shard_map(local, mesh=mesh, in_specs=in_specs, out_specs=out_specs, check_vma=False)
```

```python
import functools

import jax
import jax.numpy as jnp
import numpy as np
from jax import lax
from jax.experimental import pallas as pl
from jax.experimental.pallas import tpu as pltpu
from jax.sharding import PartitionSpec as P

OCC = 100
TOP = 32000.0
STEPS = 256.0
CORES = 2
TILE = 512
LANES = 128
VMEM_BYTES = 32 * 2**20


def dot_nt(a, b):
    return lax.dot_general(a, b, (((1,), (1,)), ((), ())), preferred_element_type=jnp.float32)


def dot_nn(a, b):
    return lax.dot_general(a, b, (((1,), (0,)), ((), ())), preferred_element_type=jnp.float32)


def divide(value, by):
    whole = jnp.floor((value.astype(jnp.float32) + 0.5) * (1.0 / by)).astype(jnp.int32)
    return whole, value - whole * by


def inside_columns(place, n, z):
    apart, i = divide(place, n)
    j = i + apart + 1
    j = jnp.where(j >= n, j - n, j)
    valid = place < n * (n - 1) // 2
    return jnp.where(valid, i * OCC + z * n + j, -1), jnp.where(valid, j * OCC + z * n + i, -1)


def pair_columns(place, n, z, other, mine):
    half = (n * n + 1) // 2
    first = jnp.logical_xor(z < other, jnp.logical_not(mine))
    count = jnp.where(first, half, n * n - half)
    q, m = divide(place + jnp.where(first, 0, half), n)
    a = jnp.where(z < other, q, m)
    b = jnp.where(z < other, m, q)
    return jnp.where(place < count, a * OCC + other * n + b, -1)


def encode(values):
    largest = jnp.maximum(jnp.max(jnp.abs(values), axis=0, keepdims=True), 1e-30)
    code = jnp.floor(jnp.log2(TOP / largest) * STEPS)
    coded = jnp.round(values * jnp.exp2(code * (1.0 / STEPS)))
    rows = lax.broadcasted_iota(jnp.int32, values.shape, 0)
    coded = jnp.where(rows == values.shape[0] - 1, code, coded)
    return coded.astype(jnp.int32).astype(jnp.int16)


def decode(coded):
    values = coded.astype(jnp.int32).astype(jnp.float32)
    rows = lax.broadcasted_iota(jnp.int32, values.shape, 0)
    last = rows == values.shape[0] - 1
    code = jnp.sum(jnp.where(last, values, 0.0), axis=0, keepdims=True)
    return jnp.where(last, 0.0, values * jnp.exp2(code * (-1.0 / STEPS)))


def call(name, body, scalars, inputs, outputs, grid=None):
    arrays = [entry[0] if isinstance(entry, tuple) else entry for entry in inputs]
    shapes = [jax.ShapeDtypeStruct(entry[0], entry[1]) for entry in outputs]
    if grid is None:
        in_specs = [pl.BlockSpec(memory_space=pltpu.SMEM)] + [pl.BlockSpec(memory_space=pltpu.VMEM)] * len(arrays)
        specs = dict(in_specs=in_specs, out_specs=[pl.BlockSpec(memory_space=pltpu.VMEM)] * len(shapes))
    else:
        in_specs, out_specs = [], []
        for entry, array in zip(inputs, arrays):
            block, index = entry[1:] if isinstance(entry, tuple) else (array.shape, lambda g, s, rank=array.ndim: (0,) * rank)
            in_specs.append(pl.BlockSpec(block, index))
        for entry in outputs:
            out_specs.append(pl.BlockSpec(*entry[2:]))
        specs = dict(
            grid_spec=pltpu.PrefetchScalarGridSpec(
                num_scalar_prefetch=1, grid=(grid,), in_specs=in_specs, out_specs=out_specs
            )
        )
    return pl.pallas_call(
        body,
        name=name,
        out_shape=shapes,
        compiler_params=pltpu.CompilerParams(vmem_limit_bytes=VMEM_BYTES),
        cost_estimate=pl.CostEstimate(flops=1, bytes_accessed=1, transcendentals=0),
        **specs,
    )(scalars, *arrays)


def mask_body(by, row_n, sub, tall, s_ref, ab_ref, cd_ref, v_ref, *out_refs):
    x, y, core = s_ref[0], s_ref[2], s_ref[3]
    k_here, cd_here = out_refs[0].shape[-1], v_ref.shape[1]
    q, m = divide(lax.broadcasted_iota(jnp.int32, (k_here, 1), 0), sub)
    wanted = q * (sub * row_n) + lax.rem(x - by + row_n, row_n) * sub + m
    pick = jnp.where(lax.broadcasted_iota(jnp.int32, (k_here, cd_here), 1) == wanted, 1.0, 0.0).astype(jnp.bfloat16)
    square = (LANES, LANES)
    diagonal = lax.broadcasted_iota(jnp.int32, square, 0) == lax.broadcasted_iota(jnp.int32, square, 1)
    cd_labels = cd_ref[...].astype(jnp.float32)
    cd = jnp.concatenate([cd_labels[k : k + 1] for k in range(cd_here // LANES)], axis=1)
    strips = tall // LANES
    blocks = []
    for other_core in (1, 0):
        for other_y in (1, 0):
            block = lax.rem(y + other_y, 2) * CORES + lax.rem(core + other_core, CORES)
            for strip in range(strips):
                labels = ab_ref[pl.ds(block * strips + strip, 1), :].astype(jnp.float32)
                ab = jnp.sum(jnp.where(diagonal, labels, 0.0), axis=1, keepdims=True)
                start = pl.multiple_of(block * tall + strip * LANES, LANES)
                v = v_ref[pl.ds(start, LANES), :].astype(jnp.float32)
                blocks.append(jnp.where(ab == cd, v, 0.0).astype(jnp.bfloat16))
    picked = dot_nt(jnp.concatenate(blocks, axis=0), pick).astype(jnp.bfloat16)
    if len(out_refs) == 1:
        out_refs[0][...] = picked.reshape(out_refs[0].shape)
    else:
        out_refs[0][...] = picked[: 2 * tall].reshape(out_refs[0].shape)
        out_refs[1][...] = picked[2 * tall :].reshape(out_refs[1].shape)


def one_hot_rows(columns, width):
    lanes = lax.broadcasted_iota(jnp.int32, (columns.shape[0], width), 1)
    return jnp.where(lanes == columns, 1.0, 0.0).astype(jnp.bfloat16)


def send_body(order, n, col_n, s_ref, t_ref, flat_ref, *out_refs):
    columns, wide = t_ref.shape[-1], flat_ref.shape[1]
    last = wide - LANES
    flat_ref[:, last:] = jnp.zeros((flat_ref.shape[0], LANES), flat_ref.dtype)
    flat_ref[:, :columns] = t_ref[...].reshape(-1, columns)
    z = s_ref[1]
    place = lax.broadcasted_iota(jnp.int32, (out_refs[0].shape[0], 1), 0)
    chunk = out_refs[0].shape[0]
    wanted = [pair_columns(place, n, z, lax.rem(z - r + col_n, col_n), False) for r in order]
    picked = dot_nt(one_hot_rows(jnp.concatenate(wanted, axis=0), flat_ref.shape[1]), flat_ref[...]).astype(jnp.bfloat16)
    for k, out_ref in enumerate(out_refs):
        out_ref[...] = picked[k * chunk : (k + 1) * chunk]


def keep_body(order, n, col_n, s_ref, flat_ref, out_ref):
    z = s_ref[1]
    place = lax.broadcasted_iota(jnp.int32, (out_ref.shape[1], 1), 0)
    inside, turned = inside_columns(place, n, z)
    picks = [inside if r == 0 else pair_columns(place, n, z, lax.rem(z + r, col_n), True) for r in order] + [turned]
    picked = dot_nt(one_hot_rows(jnp.concatenate(picks, axis=0), flat_ref.shape[1]), flat_ref[...])
    out_ref[...] = picked.astype(jnp.bfloat16).reshape(out_ref.shape)


def sum_body(first, count, s_ref, own_here, own_there, *refs):
    away = refs[: 2 * count]
    keep_ref, pass_ref, coded_ref, kept_ref = refs[2 * count :]
    k_here = own_here.shape[2]
    chunk = own_here.shape[1]

    def rows(ref):
        return ref[ref.shape[0] - 1] if len(ref.shape) == 3 else ref[...]

    half = kept_ref.shape[1]
    keep, passed = keep_ref[...].reshape(-1, k_here), pass_ref[...].reshape(-1, k_here)
    a, b = keep[-2 * half :], passed[: 2 * half]
    to = own_here[first : first + count].reshape(count * chunk, k_here)
    too = own_there[first : first + count].reshape(count * chunk, k_here)
    tr = jnp.concatenate([rows(ref) for ref in away[:count]], axis=0)
    tro = jnp.concatenate([rows(ref) for ref in away[count:]], axis=0)
    left = jnp.concatenate([to, too, tr, tro], axis=1)
    right = jnp.concatenate([a, b, -a, -b], axis=1)
    total = dot_nt(left, right)
    coded_ref[...] = encode(total[:, :half])
    kept_ref[...] = total[:, half:]


def add_y_body(s_ref, kept_ref, coded_ref, out_ref):
    out_ref[...] = encode(kept_ref[...] + decode(coded_ref[...]))


def add_x_body(count, s_ref, kept_ref, *refs):
    total = kept_ref[...]
    for ref in refs[:-count]:
        total = total + decode(ref[...])
    rounded = total.astype(jnp.bfloat16)
    chunk = rounded.shape[0] // count
    for k, out_ref in enumerate(refs[-count:]):
        out_ref[...] = rounded[k * chunk : (k + 1) * chunk]


def place_body(order, n, col_n, before, s_ref, *refs):
    out_ref = refs[-1]
    z = s_ref[1]
    chunk = refs[0].shape[0]
    place = lax.broadcasted_iota(jnp.int32, (1, chunk), 1)
    at = lax.broadcasted_iota(jnp.int32, (out_ref.shape[0], chunk), 0) + pl.program_id(0) * out_ref.shape[0]
    signs = []
    for r in order:
        if r == 0:
            inside, turned = inside_columns(place, n, z)
            signs.append(jnp.where(at == inside, 1.0, jnp.where(at == turned, -1.0, 0.0)))
        else:
            plus = pair_columns(place, n, z, lax.rem(z + r, col_n), True)
            minus = pair_columns(place, n, z, lax.rem(z - r + col_n, col_n), False)
            signs.append(jnp.where(at == plus, 1.0, 0.0))
            signs.append(jnp.where(at == minus, -1.0, 0.0))
    signs = jnp.concatenate([sign.astype(jnp.bfloat16) for sign in signs], axis=1)
    values = jnp.concatenate([ref[...] for ref in refs[: 2 * len(order) - order.count(0)]], axis=0)
    total = dot_nn(signs, values)
    if before:
        total = total + refs[-2][...].astype(jnp.float32)
    out_ref[...] = total.astype(jnp.bfloat16)


def local(integrals, amplitudes, ab_irrep, cd_irrep):
    row_n, col_n, depth_n = lax.axis_size("row"), lax.axis_size("col"), lax.axis_size("depth")
    x, z, d = lax.axis_index("row"), lax.axis_index("col"), lax.axis_index("depth")
    y, core = d // CORES, d % CORES
    rows, cd_here = integrals.shape
    blocks, sub, columns = amplitudes.shape
    k_here = blocks * sub
    tall = rows // depth_n
    n = OCC // col_n
    chunk = -(-((n * n + 1) // 2 + 1) // 16) * 16
    far = col_n // 2
    near = [r for r in range(1, col_n) if r != far]
    groups = [[0] + near, [far]]
    order = [0] + near + [far]
    bf16, i16, f32 = jnp.bfloat16, jnp.int16, jnp.float32

    def shift(array, axis, by):
        count = lax.axis_size(axis)
        return lax.ppermute(array, axis, [(i, (i + by) % count) for i in range(count)])

    def other_core(array):
        return lax.ppermute(array, "depth", [(i, i ^ 1) for i in range(depth_n)])

    def other_y(array):
        return lax.ppermute(array, "depth", [(i, i ^ 2) for i in range(depth_n)])

    scalars = jnp.stack([x, z, y, core]).astype(jnp.int32)
    ab_row, cd_row = ab_irrep.reshape(-1, LANES), cd_irrep.reshape(-1, LANES)

    def masked(v, by, parts):
        return call(
            "mask_integrals",
            functools.partial(mask_body, by, row_n, sub, tall),
            scalars,
            [ab_row, cd_row, v],
            [((4 // parts * tall, k_here), bf16)] * parts,
        )

    passed, kept = [None] * row_n, [None] * row_n
    gone = scalars
    for by in range(1, row_n):
        (gone,) = masked(integrals, by, 1)
        kept[by] = shift(gone, "row", -by)

    amplitudes, _ = lax.optimization_barrier((amplitudes, gone))
    sent_order = near + [far]
    flat, *sent = call(
        "send_columns",
        functools.partial(send_body, sent_order, n, col_n),
        scalars,
        [amplitudes],
        [((k_here, -(-columns // LANES) * LANES), bf16)] + [((chunk, k_here), bf16)] * len(sent_order),
    )
    away = {r: shift(s, "col", -r) for r, s in zip(near, sent)}
    integrals, flat = lax.optimization_barrier((integrals, flat))
    passed[0], kept[0] = masked(integrals, 0, 2)
    (own,) = call(
        "keep_columns",
        functools.partial(keep_body, order, n, col_n),
        scalars,
        [flat],
        [((col_n + 1, chunk, k_here), bf16)],
    )
    arrived = lax.optimization_barrier((passed[0], own, sent[-1], kept[1:], away))
    passed[0], behind, far_sent, kept[1:], away = arrived
    away_there = {r: other_core(away[r]) for r in near}
    passed = [other_core(passed[0])] + [other_core(a) for a in kept[1:]]
    own_there = other_core(behind)
    away[far] = shift(far_sent, "col", -far)

    done = None
    for group in groups:
        first, count = order.index(group[0]), len(group)
        here = [own if r == 0 else away[r] for r in group]
        there = [own_there if r == 0 else away_there[r] for r in group]
        final = [None] * (row_n + 1)
        for by in list(range(1, row_n)) + [0]:
            coded, total = call(
                "sum_pairs",
                functools.partial(sum_body, first, count),
                scalars,
                [own, own_there] + here + there + [kept[by], passed[by]],
                [((count * chunk, tall), i16), ((count * chunk, tall), f32)],
            )
            if by == 0 and group == groups[0]:
                _, away[far] = lax.optimization_barrier((coded, away[far]))
                away_there[far] = other_core(away[far])
            coded = other_y(coded)
            if by == 0:
                final[:2] = [total, coded]
            else:
                (merged,) = call(
                    "add_other_y",
                    add_y_body,
                    scalars,
                    [total, coded],
                    [((count * chunk, tall), i16)],
                )
                final[by + 1] = shift(merged, "row", by)
        rounded = call(
            "add_other_x",
            functools.partial(add_x_body, count),
            scalars,
            final,
            [((chunk, tall), bf16)] * count,
        )
        sources = []
        for r, mine in zip(group, rounded):
            sources += [mine] if r == 0 else [mine, shift(mine, "col", r)]
        tile = (TILE, tall), lambda g, s: (g, 0)
        sources += [] if done is None else [(done, *tile)]
        (done,) = call(
            "place_pairs",
            functools.partial(place_body, group, n, col_n, done is not None),
            scalars,
            sources,
            [((columns, tall), bf16, *tile)],
            grid=-(-columns // TILE),
        )
    return done.T


def solution(mesh):
    in_specs = (P("row", "depth"), P("depth", "row", "col"), P("row"), P("depth"))
    out_specs = P(("row", "depth"), "col")
    return jax.shard_map(local, mesh=mesh, in_specs=in_specs, out_specs=out_specs, check_vma=False)
```

```python
import functools

import jax
import jax.numpy as jnp
import numpy as np
from jax import lax
from jax.experimental import pallas as pl
from jax.experimental.pallas import tpu as pltpu
from jax.sharding import PartitionSpec as P

OCC = 100
TOP = 32000.0
STEPS = 256.0
CORES = 2
TILE = 512
LANES = 128
VMEM_BYTES = 32 * 2**20


def dot_nt(a, b):
    return lax.dot_general(a, b, (((1,), (1,)), ((), ())), preferred_element_type=jnp.float32)


def dot_nn(a, b):
    return lax.dot_general(a, b, (((1,), (0,)), ((), ())), preferred_element_type=jnp.float32)


def divide(value, by):
    whole = jnp.floor((value.astype(jnp.float32) + 0.5) * (1.0 / by)).astype(jnp.int32)
    return whole, value - whole * by


def inside_columns(place, n, z):
    apart, i = divide(place, n)
    j = i + apart + 1
    j = jnp.where(j >= n, j - n, j)
    valid = place < n * (n - 1) // 2
    return jnp.where(valid, i * OCC + z * n + j, -1), jnp.where(valid, j * OCC + z * n + i, -1)


def pair_columns(place, n, z, other, mine):
    half = (n * n + 1) // 2
    first = jnp.logical_xor(z < other, jnp.logical_not(mine))
    count = jnp.where(first, half, n * n - half)
    q, m = divide(place + jnp.where(first, 0, half), n)
    a = jnp.where(z < other, q, m)
    b = jnp.where(z < other, m, q)
    return jnp.where(place < count, a * OCC + other * n + b, -1)


def encode(values):
    largest = jnp.maximum(jnp.max(jnp.abs(values), axis=0, keepdims=True), 1e-30)
    code = jnp.floor(jnp.log2(TOP / largest) * STEPS)
    coded = jnp.round(values * jnp.exp2(code * (1.0 / STEPS)))
    rows = lax.broadcasted_iota(jnp.int32, values.shape, 0)
    coded = jnp.where(rows == values.shape[0] - 1, code, coded)
    return coded.astype(jnp.int32).astype(jnp.int16)


def decode(coded):
    values = coded.astype(jnp.int32).astype(jnp.float32)
    rows = lax.broadcasted_iota(jnp.int32, values.shape, 0)
    last = rows == values.shape[0] - 1
    code = jnp.sum(jnp.where(last, values, 0.0), axis=0, keepdims=True)
    return jnp.where(last, 0.0, values * jnp.exp2(code * (-1.0 / STEPS)))


def call(name, body, scalars, inputs, outputs, grid=None):
    arrays = [entry[0] if isinstance(entry, tuple) else entry for entry in inputs]
    shapes = [jax.ShapeDtypeStruct(entry[0], entry[1]) for entry in outputs]
    if grid is None:
        in_specs = [pl.BlockSpec(memory_space=pltpu.SMEM)] + [pl.BlockSpec(memory_space=pltpu.VMEM)] * len(arrays)
        specs = dict(in_specs=in_specs, out_specs=[pl.BlockSpec(memory_space=pltpu.VMEM)] * len(shapes))
    else:
        in_specs, out_specs = [], []
        for entry, array in zip(inputs, arrays):
            block, index = entry[1:] if isinstance(entry, tuple) else (array.shape, lambda g, s, rank=array.ndim: (0,) * rank)
            in_specs.append(pl.BlockSpec(block, index))
        for entry in outputs:
            out_specs.append(pl.BlockSpec(*entry[2:]))
        specs = dict(
            grid_spec=pltpu.PrefetchScalarGridSpec(
                num_scalar_prefetch=1, grid=(grid,), in_specs=in_specs, out_specs=out_specs
            )
        )
    return pl.pallas_call(
        body,
        name=name,
        out_shape=shapes,
        compiler_params=pltpu.CompilerParams(vmem_limit_bytes=VMEM_BYTES),
        cost_estimate=pl.CostEstimate(flops=1, bytes_accessed=1, transcendentals=0),
        **specs,
    )(scalars, *arrays)


def masked_rows(by, row_n, sub, k_here, s_ref, ab_ref, cd_ref, v_ref):
    x, y, core = s_ref[0], s_ref[2], s_ref[3]
    rows, cd_here = v_ref.shape
    tall = rows // 4
    q, m = divide(lax.broadcasted_iota(jnp.int32, (k_here, 1), 0), sub)
    wanted = q * (sub * row_n) + lax.rem(x - by + row_n, row_n) * sub + m
    square = (LANES, LANES)
    diagonal = lax.broadcasted_iota(jnp.int32, square, 0) == lax.broadcasted_iota(jnp.int32, square, 1)
    cd_labels = cd_ref[...].astype(jnp.float32)
    cd = jnp.concatenate([cd_labels[k : k + 1] for k in range(cd_here // LANES)], axis=1)
    strips = tall // LANES
    blocks = []
    for other_core in (1, 0):
        for other_y in (1, 0):
            block = lax.rem(y + other_y, 2) * CORES + lax.rem(core + other_core, CORES)
            for strip in range(strips):
                labels = ab_ref[pl.ds(block * strips + strip, 1), :].astype(jnp.float32)
                ab = jnp.sum(jnp.where(diagonal, labels, 0.0), axis=1, keepdims=True)
                start = pl.multiple_of(block * tall + strip * LANES, LANES)
                v = v_ref[pl.ds(start, LANES), :].astype(jnp.float32)
                blocks.append(jnp.where(ab == cd, v, 0.0).astype(jnp.bfloat16))
    return dot_nt(jnp.concatenate(blocks, axis=0), one_hot_rows(wanted, cd_here)).astype(jnp.bfloat16)


def mask_body(by, row_n, sub, s_ref, ab_ref, cd_ref, v_ref, out_ref):
    out_ref[...] = masked_rows(by, row_n, sub, out_ref.shape[1], s_ref, ab_ref, cd_ref, v_ref)


def one_hot_rows(columns, width):
    lanes = lax.broadcasted_iota(jnp.int32, (columns.shape[0], width), 1)
    return jnp.where(lanes == columns, 1.0, 0.0).astype(jnp.bfloat16)


def send_body(order, n, col_n, s_ref, t_ref, flat_ref, *out_refs):
    columns, wide = t_ref.shape[-1], flat_ref.shape[1]
    last = wide - LANES
    flat_ref[:, last:] = jnp.zeros((flat_ref.shape[0], LANES), flat_ref.dtype)
    flat_ref[:, :columns] = t_ref[...].reshape(-1, columns)
    z = s_ref[1]
    place = lax.broadcasted_iota(jnp.int32, (out_refs[0].shape[0], 1), 0)
    chunk = out_refs[0].shape[0]
    wanted = [pair_columns(place, n, z, lax.rem(z - r + col_n, col_n), False) for r in order]
    picked = dot_nt(one_hot_rows(jnp.concatenate(wanted, axis=0), flat_ref.shape[1]), flat_ref[...]).astype(jnp.bfloat16)
    for k, out_ref in enumerate(out_refs):
        out_ref[...] = picked[k * chunk : (k + 1) * chunk]


def keep_body(order, n, col_n, row_n, sub, s_ref, flat_ref, ab_ref, cd_ref, v_ref, both_ref, kept_ref):
    z = s_ref[1]
    half, k_here = kept_ref.shape
    pairs = both_ref.shape[0] - half
    place = lax.broadcasted_iota(jnp.int32, (pairs // (len(order) + 1), 1), 0)
    inside, turned = inside_columns(place, n, z)
    picks = [inside if r == 0 else pair_columns(place, n, z, lax.rem(z + r, col_n), True) for r in order] + [turned]
    picked = dot_nt(one_hot_rows(jnp.concatenate(picks, axis=0), flat_ref.shape[1]), flat_ref[...])
    both_ref[:pairs] = picked.astype(jnp.bfloat16)
    masked = masked_rows(0, row_n, sub, k_here, s_ref, ab_ref, cd_ref, v_ref)
    both_ref[pairs:] = masked[:half]
    kept_ref[...] = masked[half:]


def sum_body(first, count, groups, y_first, s_ref, own_here, own_there, *refs):
    away, refs = refs[: 2 * count], refs[2 * count :]
    keeps, passes, outs = refs[:groups], refs[groups : 2 * groups - 1], refs[2 * groups - 1 :]
    high, tall = outs[-1].shape[-2:]
    tall = tall if y_first else tall // 2
    chunk = high // count
    pairs = own_here.shape[0] - 2 * tall

    def rows(ref):
        return ref[pairs - chunk : pairs] if ref.shape[0] > chunk else ref[...]

    mine = slice(first * chunk, (first + count) * chunk)
    tr = jnp.concatenate([rows(ref) for ref in away[:count]], axis=0)
    tro = jnp.concatenate([rows(ref) for ref in away[count:]], axis=0)
    left = jnp.concatenate([own_here[mine], own_there[mine], tr, tro], axis=1)
    for g in range(groups):
        start = keeps[g].shape[0] - 2 * tall
        a = keeps[g][start:]
        b = own_there[pairs:] if g == 0 else passes[g - 1][: 2 * tall]
        total = dot_nt(left, jnp.concatenate([a, b, -a, -b], axis=1))
        if y_first:
            outs[0][g] = encode(total[:, :tall])
            outs[1][g] = total[:, tall:]
        elif g == 0:
            outs[-1][...] = total
        else:
            outs[g - 1][...] = encode(total)


def add_y_body(s_ref, kept_ref, coded_ref, own_ref, *out_refs):
    for g in range(kept_ref.shape[0]):
        total = kept_ref[g] + decode(coded_ref[g])
        if g == 0:
            own_ref[...] = total
        else:
            out_refs[g - 1][...] = encode(total)


def add_x_body(s_ref, kept_ref, *refs):
    coded_ref, own_ref = refs[-2:]
    total = kept_ref[...]
    for ref in refs[:-2]:
        total = total + decode(ref[...])
    tall = own_ref.shape[1]
    coded_ref[...] = encode(total[:, :tall])
    own_ref[...] = total[:, tall:]


def round_body(count, s_ref, kept_ref, *refs):
    total = kept_ref[...]
    for ref in refs[:-count]:
        total = total + decode(ref[...])
    rounded = total.astype(jnp.bfloat16)
    chunk = rounded.shape[0] // count
    for k, out_ref in enumerate(refs[-count:]):
        out_ref[...] = rounded[k * chunk : (k + 1) * chunk]


def place_body(order, n, col_n, before, s_ref, *refs):
    out_ref = refs[-1]
    z = s_ref[1]
    chunk = refs[0].shape[0]
    place = lax.broadcasted_iota(jnp.int32, (1, chunk), 1)
    at = lax.broadcasted_iota(jnp.int32, (out_ref.shape[0], chunk), 0) + pl.program_id(0) * out_ref.shape[0]
    signs = []
    for r in order:
        if r == 0:
            inside, turned = inside_columns(place, n, z)
            signs.append(jnp.where(at == inside, 1.0, jnp.where(at == turned, -1.0, 0.0)))
        else:
            plus = pair_columns(place, n, z, lax.rem(z + r, col_n), True)
            minus = pair_columns(place, n, z, lax.rem(z - r + col_n, col_n), False)
            signs.append(jnp.where(at == plus, 1.0, 0.0))
            signs.append(jnp.where(at == minus, -1.0, 0.0))
    signs = jnp.concatenate([sign.astype(jnp.bfloat16) for sign in signs], axis=1)
    values = jnp.concatenate([ref[...] for ref in refs[: 2 * len(order) - order.count(0)]], axis=0)
    total = dot_nn(signs, values)
    if before:
        total = total + refs[-2][...].astype(jnp.float32)
    out_ref[...] = total.astype(jnp.bfloat16)


def local(integrals, amplitudes, ab_irrep, cd_irrep):
    row_n, col_n, depth_n = lax.axis_size("row"), lax.axis_size("col"), lax.axis_size("depth")
    x, z, d = lax.axis_index("row"), lax.axis_index("col"), lax.axis_index("depth")
    y, core = d // CORES, d % CORES
    rows, cd_here = integrals.shape
    blocks, sub, columns = amplitudes.shape
    k_here = blocks * sub
    tall = rows // depth_n
    n = OCC // col_n
    chunk = -(-((n * n + 1) // 2 + 1) // 16) * 16
    far = col_n // 2
    near = [r for r in range(1, col_n) if r != far]
    half = (len(near) + 1) // 2
    groups = [([0] + near[:half], True), (near[half:], False), ([far], False)]
    groups = [(group, y_first) for group, y_first in groups if group]
    order = [0] + near + [far]
    bf16, i16, f32 = jnp.bfloat16, jnp.int16, jnp.float32

    def shift(array, axis, by):
        count = lax.axis_size(axis)
        return lax.ppermute(array, axis, [(i, (i + by) % count) for i in range(count)])

    def other_core(array):
        return lax.ppermute(array, "depth", [(i, i ^ 1) for i in range(depth_n)])

    def other_y(array):
        return lax.ppermute(array, "depth", [(i, i ^ 2) for i in range(depth_n)])

    scalars = jnp.stack([x, z, y, core]).astype(jnp.int32)
    ab_row, cd_row = ab_irrep.reshape(-1, LANES), cd_irrep.reshape(-1, LANES)

    kept = [None] * row_n
    gone = scalars
    for by in range(1, row_n):
        (gone,) = call(
            "mask_integrals",
            functools.partial(mask_body, by, row_n, sub),
            scalars,
            [ab_row, cd_row, integrals],
            [((rows, k_here), bf16)],
        )
        kept[by] = shift(gone, "row", -by)

    amplitudes, _ = lax.optimization_barrier((amplitudes, gone))
    sent_order = near + [far]
    flat, *sent = call(
        "send_columns",
        functools.partial(send_body, sent_order, n, col_n),
        scalars,
        [amplitudes],
        [((k_here, -(-columns // LANES) * LANES), bf16)] + [((chunk, k_here), bf16)] * len(sent_order),
    )
    away = {r: shift(s, "col", -r) for r, s in zip(near, sent)}

    both, kept[0] = call(
        "keep_columns",
        functools.partial(keep_body, order, n, col_n, row_n, sub),
        scalars,
        [flat, ab_row, cd_row, integrals],
        [(((col_n + 1) * chunk + 2 * tall, k_here), bf16), ((2 * tall, k_here), bf16)],
    )
    far_sent, away = lax.optimization_barrier((sent[-1], away))
    behind, kept[1:], *arrived = lax.optimization_barrier((both, kept[1:], *[away[r] for r in near]))
    away_there = {r: other_core(a) for r, a in zip(near, arrived)}
    both_there = other_core(behind)
    away[far] = shift(far_sent, "col", -far)
    passed = [other_core(a) for a in kept[1:]]

    rounded, arrived = {}, []
    for group, y_first in groups:
        first, count = order.index(group[0]), len(group)
        high = count * chunk
        if far in group:
            _, away[far] = lax.optimization_barrier((arrived, away[far]))
            away_there[far] = other_core(away[far])
        here = [both if r == 0 else away[r] for r in group]
        there = [both_there if r == 0 else away_there[r] for r in group]
        if group == groups[1][0]:
            _, here[0] = lax.optimization_barrier((sums[0], here[0]))
        if y_first:
            shapes = [((row_n, high, tall), i16), ((row_n, high, tall), f32)]
        else:
            shapes = [((high, 2 * tall), i16)] * (row_n - 1) + [((high, 2 * tall), f32)]
        sums = call(
            "sum_pairs",
            functools.partial(sum_body, first, count, row_n, y_first),
            scalars,
            [both, both_there] + here + there + kept + passed,
            shapes,
        )
        if y_first:
            own_sum, *others = call(
                "add_other_y",
                add_y_body,
                scalars,
                [sums[1], other_y(sums[0])],
                [((high, tall), f32)] + [((high, tall), i16)] * (row_n - 1),
            )
            last = [shift(other, "row", by + 1) for by, other in enumerate(others)]
        else:
            arrived = [shift(coded, "row", by + 1) for by, coded in enumerate(sums[:-1])]
            coded, own_sum = call(
                "add_other_x",
                add_x_body,
                scalars,
                [sums[-1]] + arrived,
                [((high, tall), i16), ((high, tall), f32)],
            )
            last = [other_y(coded)]
        mine = call(
            "round_pairs",
            functools.partial(round_body, count),
            scalars,
            [own_sum] + last,
            [((chunk, tall), bf16)] * count,
        )
        for r, value in zip(group, mine):
            rounded[r] = [value] if r == 0 else [value, shift(value, "col", r)]

    done = None
    for group in ([0] + near, [far]):
        sources = [value for r in group for value in rounded[r]]
        tile = (TILE, tall), lambda g, s: (g, 0)
        sources += [] if done is None else [(done, *tile)]
        (done,) = call(
            "place_pairs",
            functools.partial(place_body, group, n, col_n, done is not None),
            scalars,
            sources,
            [((columns, tall), bf16, *tile)],
            grid=-(-columns // TILE),
        )
    return done.T


def solution(mesh):
    in_specs = (P("row", "depth"), P("depth", "row", "col"), P("row"), P("depth"))
    out_specs = P(("row", "depth"), "col")
    return jax.shard_map(local, mesh=mesh, in_specs=in_specs, out_specs=out_specs, check_vma=False)
```

```python
import functools

import jax
import jax.numpy as jnp
import numpy as np
from jax import lax
from jax.experimental import pallas as pl
from jax.experimental.pallas import tpu as pltpu
from jax.sharding import PartitionSpec as P

OCC = 100
TOP = 32000.0
STEPS = 256.0
CORES = 2
TILE = 1264
LANES = 128
VMEM_BYTES = 32 * 2**20


def dot_nt(a, b):
    return lax.dot_general(a, b, (((1,), (1,)), ((), ())), preferred_element_type=jnp.float32)


def dot_nn(a, b):
    return lax.dot_general(a, b, (((1,), (0,)), ((), ())), preferred_element_type=jnp.float32)


def divide(value, by):
    whole = jnp.floor((value.astype(jnp.float32) + 0.5) * (1.0 / by)).astype(jnp.int32)
    return whole, value - whole * by


def inside_columns(place, n, z):
    apart, i = divide(place, n)
    j = i + apart + 1
    j = jnp.where(j >= n, j - n, j)
    valid = place < n * (n - 1) // 2
    return jnp.where(valid, i * OCC + z * n + j, -1), jnp.where(valid, j * OCC + z * n + i, -1)


def pair_columns(place, n, z, other, mine):
    half = (n * n + 1) // 2
    first = jnp.logical_xor(z < other, jnp.logical_not(mine))
    count = jnp.where(first, half, n * n - half)
    q, m = divide(place + jnp.where(first, 0, half), n)
    a = jnp.where(z < other, q, m)
    b = jnp.where(z < other, m, q)
    return jnp.where(place < count, a * OCC + other * n + b, -1)


def encode(values):
    largest = jnp.maximum(jnp.max(jnp.abs(values), axis=0, keepdims=True), 1e-30)
    code = jnp.floor(jnp.log2(TOP / largest) * STEPS)
    coded = jnp.round(values * jnp.exp2(code * (1.0 / STEPS)))
    rows = lax.broadcasted_iota(jnp.int32, values.shape, 0)
    coded = jnp.where(rows == values.shape[0] - 1, code, coded)
    return coded.astype(jnp.int32).astype(jnp.int16)


def decode(coded):
    values = coded.astype(jnp.int32).astype(jnp.float32)
    rows = lax.broadcasted_iota(jnp.int32, values.shape, 0)
    last = rows == values.shape[0] - 1
    code = jnp.sum(jnp.where(last, values, 0.0), axis=0, keepdims=True)
    return jnp.where(last, 0.0, values * jnp.exp2(code * (-1.0 / STEPS)))


def call(name, body, scalars, inputs, outputs, grid=None):
    arrays = [entry[0] if isinstance(entry, tuple) else entry for entry in inputs]
    shapes = [jax.ShapeDtypeStruct(entry[0], entry[1]) for entry in outputs]
    if grid is None:
        in_specs = [pl.BlockSpec(memory_space=pltpu.SMEM)] + [pl.BlockSpec(memory_space=pltpu.VMEM)] * len(arrays)
        specs = dict(in_specs=in_specs, out_specs=[pl.BlockSpec(memory_space=pltpu.VMEM)] * len(shapes))
    else:
        in_specs, out_specs = [], []
        for entry, array in zip(inputs, arrays):
            block, index = entry[1:] if isinstance(entry, tuple) else (array.shape, lambda g, s, rank=array.ndim: (0,) * rank)
            in_specs.append(pl.BlockSpec(block, index))
        for entry in outputs:
            out_specs.append(pl.BlockSpec(*entry[2:]))
        specs = dict(
            grid_spec=pltpu.PrefetchScalarGridSpec(
                num_scalar_prefetch=1, grid=(grid,), in_specs=in_specs, out_specs=out_specs
            )
        )
    return pl.pallas_call(
        body,
        name=name,
        out_shape=shapes,
        compiler_params=pltpu.CompilerParams(vmem_limit_bytes=VMEM_BYTES),
        cost_estimate=pl.CostEstimate(flops=1, bytes_accessed=1, transcendentals=0),
        **specs,
    )(scalars, *arrays)


def masked_rows(by, row_n, sub, k_here, s_ref, ab_ref, cd_ref, v_ref):
    x, y, core = s_ref[0], s_ref[2], s_ref[3]
    rows, cd_here = v_ref.shape
    tall = rows // 4
    q, m = divide(lax.broadcasted_iota(jnp.int32, (k_here, 1), 0), sub)
    wanted = q * (sub * row_n) + lax.rem(x - by + row_n, row_n) * sub + m
    square = (LANES, LANES)
    diagonal = lax.broadcasted_iota(jnp.int32, square, 0) == lax.broadcasted_iota(jnp.int32, square, 1)
    cd_labels = cd_ref[...].astype(jnp.float32)
    cd = jnp.concatenate([cd_labels[k : k + 1] for k in range(cd_here // LANES)], axis=1)
    strips = tall // LANES
    blocks = []
    for other_core in (1, 0):
        for other_y in (1, 0):
            block = lax.rem(y + other_y, 2) * CORES + lax.rem(core + other_core, CORES)
            for strip in range(strips):
                labels = ab_ref[pl.ds(block * strips + strip, 1), :].astype(jnp.float32)
                ab = jnp.sum(jnp.where(diagonal, labels, 0.0), axis=1, keepdims=True)
                start = pl.multiple_of(block * tall + strip * LANES, LANES)
                v = v_ref[pl.ds(start, LANES), :].astype(jnp.float32)
                blocks.append(jnp.where(ab == cd, v, 0.0).astype(jnp.bfloat16))
    return dot_nt(jnp.concatenate(blocks, axis=0), one_hot_rows(wanted, cd_here)).astype(jnp.bfloat16)


def mask_body(by, row_n, sub, s_ref, ab_ref, cd_ref, v_ref, out_ref):
    out_ref[...] = masked_rows(by, row_n, sub, out_ref.shape[1], s_ref, ab_ref, cd_ref, v_ref)


def one_hot_rows(columns, width):
    lanes = lax.broadcasted_iota(jnp.int32, (columns.shape[0], width), 1)
    return jnp.where(lanes == columns, 1.0, 0.0).astype(jnp.bfloat16)


def send_body(order, n, col_n, s_ref, t_ref, flat_ref, *out_refs):
    columns, wide = t_ref.shape[-1], flat_ref.shape[1]
    last = wide - LANES
    flat_ref[:, last:] = jnp.zeros((flat_ref.shape[0], LANES), flat_ref.dtype)
    flat_ref[:, :columns] = t_ref[...].reshape(-1, columns)
    z = s_ref[1]
    place = lax.broadcasted_iota(jnp.int32, (out_refs[0].shape[0], 1), 0)
    chunk = out_refs[0].shape[0]
    wanted = [pair_columns(place, n, z, lax.rem(z - r + col_n, col_n), False) for r in order]
    picked = dot_nt(one_hot_rows(jnp.concatenate(wanted, axis=0), flat_ref.shape[1]), flat_ref[...]).astype(jnp.bfloat16)
    for k, out_ref in enumerate(out_refs):
        out_ref[...] = picked[k * chunk : (k + 1) * chunk]


def keep_body(soon, late, n, col_n, row_n, sub, s_ref, flat_ref, ab_ref, cd_ref, v_ref, first_ref, later_ref, kept_ref):
    z = s_ref[1]
    half, k_here = kept_ref.shape
    pairs = first_ref.shape[0] - half
    place = lax.broadcasted_iota(jnp.int32, (pairs // (len(soon) + 2), 1), 0)
    inside, turned = inside_columns(place, n, z)
    others = [pair_columns(place, n, z, lax.rem(z + r, col_n), True) for r in soon + late]
    picks = jnp.concatenate([inside] + others[: len(soon)] + [turned] + others[len(soon) :], axis=0)
    picked = dot_nt(one_hot_rows(picks, flat_ref.shape[1]), flat_ref[...]).astype(jnp.bfloat16)
    masked = masked_rows(0, row_n, sub, k_here, s_ref, ab_ref, cd_ref, v_ref)
    first_ref[:pairs] = picked[:pairs]
    first_ref[pairs:] = masked[:half]
    later_ref[...] = picked[pairs:]
    kept_ref[...] = masked[half:]


def sum_body(place, turned, groups, y_first, s_ref, own_here, own_there, away_here, away_there, first_there, *refs):
    keeps, passes, outs = refs[:groups], refs[groups : 2 * groups - 1], refs[2 * groups - 1 :]
    chunk, tall = outs[-1].shape[-2:]
    tall = tall if y_first else tall // 2
    mine = slice(place * chunk, (place + 1) * chunk)
    other = slice(turned * chunk, (turned + 1) * chunk)
    left = jnp.concatenate([own_here[mine], own_there[mine], away_here[other], away_there[other]], axis=1)
    for g in range(groups):
        start = keeps[g].shape[0] - 2 * tall
        a = keeps[g][start:]
        b = first_there[first_there.shape[0] - 2 * tall :] if g == 0 else passes[g - 1][: 2 * tall]
        total = dot_nt(left, jnp.concatenate([a, b, -a, -b], axis=1))
        if y_first:
            outs[0][g] = encode(total[:, :tall])
            outs[1][g] = total[:, tall:]
        elif g == 0:
            outs[-1][...] = total
        else:
            outs[g - 1][...] = encode(total)


def add_y_body(s_ref, kept_ref, coded_ref, own_ref, *out_refs):
    for g in range(kept_ref.shape[0]):
        total = kept_ref[g] + decode(coded_ref[g])
        if g == 0:
            own_ref[...] = total
        else:
            out_refs[g - 1][...] = encode(total)


def add_x_body(s_ref, kept_ref, *refs):
    coded_ref, own_ref = refs[-2:]
    total = kept_ref[...]
    for ref in refs[:-2]:
        total = total + decode(ref[...])
    tall = own_ref.shape[1]
    coded_ref[...] = encode(total[:, :tall])
    own_ref[...] = total[:, tall:]


def round_body(s_ref, kept_ref, *refs):
    total = kept_ref[...]
    for ref in refs[:-1]:
        total = total + decode(ref[...])
    refs[-1][...] = total.astype(jnp.bfloat16)


def place_body(order, n, col_n, before, s_ref, *refs):
    out_ref = refs[-1]
    z = s_ref[1]
    chunk = refs[0].shape[0]
    place = lax.broadcasted_iota(jnp.int32, (1, chunk), 1)
    at = lax.broadcasted_iota(jnp.int32, (out_ref.shape[0], chunk), 0) + pl.program_id(0) * out_ref.shape[0]
    signs = []
    for r in order:
        if r == 0:
            inside, turned = inside_columns(place, n, z)
            signs.append(jnp.where(at == inside, 1.0, jnp.where(at == turned, -1.0, 0.0)))
        else:
            plus = pair_columns(place, n, z, lax.rem(z + r, col_n), True)
            minus = pair_columns(place, n, z, lax.rem(z - r + col_n, col_n), False)
            signs.append(jnp.where(at == plus, 1.0, 0.0))
            signs.append(jnp.where(at == minus, -1.0, 0.0))
    signs = jnp.concatenate([sign.astype(jnp.bfloat16) for sign in signs], axis=1)
    values = jnp.concatenate([ref[...] for ref in refs[: 2 * len(order) - order.count(0)]], axis=0)
    total = dot_nn(signs, values)
    if before:
        total = total + refs[-2][...].astype(jnp.float32)
    out_ref[...] = total.astype(jnp.bfloat16)


def local(integrals, amplitudes, ab_irrep, cd_irrep):
    row_n, col_n, depth_n = lax.axis_size("row"), lax.axis_size("col"), lax.axis_size("depth")
    x, z, d = lax.axis_index("row"), lax.axis_index("col"), lax.axis_index("depth")
    y, core = d // CORES, d % CORES
    rows, cd_here = integrals.shape
    blocks, sub, columns = amplitudes.shape
    k_here = blocks * sub
    tall = rows // depth_n
    n = OCC // col_n
    chunk = -(-((n * n + 1) // 2 + 1) // 16) * 16
    far = col_n // 2
    near = [r for r in range(1, col_n) if r != far]
    soon, late = [far] + near[:1], near[1:]
    chunks = [(0, True)] + [(r, False) for r in soon] + [(r, True) for r in late]
    bf16, i16, f32 = jnp.bfloat16, jnp.int16, jnp.float32

    def shift(array, axis, by):
        count = lax.axis_size(axis)
        return lax.ppermute(array, axis, [(i, (i + by) % count) for i in range(count)])

    def other_core(array):
        return lax.ppermute(array, "depth", [(i, i ^ 1) for i in range(depth_n)])

    def other_y(array):
        return lax.ppermute(array, "depth", [(i, i ^ 2) for i in range(depth_n)])

    scalars = jnp.stack([x, z, y, core]).astype(jnp.int32)
    ab_row, cd_row = ab_irrep.reshape(-1, LANES), cd_irrep.reshape(-1, LANES)

    kept = [None] * row_n
    gone = scalars
    for by in range(1, row_n):
        (gone,) = call(
            "mask_integrals",
            functools.partial(mask_body, by, row_n, sub),
            scalars,
            [ab_row, cd_row, integrals],
            [((rows, k_here), bf16)],
        )
        kept[by] = shift(gone, "row", -by)

    amplitudes, _ = lax.optimization_barrier((amplitudes, gone))
    flat, *sent = call(
        "send_columns",
        functools.partial(send_body, soon + late, n, col_n),
        scalars,
        [amplitudes],
        [((k_here, -(-columns // LANES) * LANES), bf16)] + [((chunk, k_here), bf16)] * (col_n - 1),
    )
    away = {r: shift(value, "col", -r) for r, value in zip(soon, sent)}

    first, later, kept[0] = call(
        "keep_columns",
        functools.partial(keep_body, soon, late, n, col_n, row_n, sub),
        scalars,
        [flat, ab_row, cd_row, integrals],
        [
            (((len(soon) + 2) * chunk + 2 * tall, k_here), bf16),
            ((len(late) * chunk, k_here), bf16),
            ((2 * tall, k_here), bf16),
        ],
    )
    away, kept[1:], first, *sent = lax.optimization_barrier((away, kept[1:], first, *sent[len(soon) :]))
    first_there = other_core(first)
    passed = [other_core(a) for a in kept[1:]]
    away_there = {r: other_core(away[r]) for r in soon}
    for r, value in zip(late, sent):
        away[r] = shift(value, "col", -r)

    rounded = {}
    before, later_there = [], None
    for place, (r, y_first) in enumerate(chunks):
        if r in late and later_there is None:
            _, later, *arrived = lax.optimization_barrier((before, later, *[away[q] for q in late]))
            for q, value in zip(late, arrived):
                away[q] = value
                away_there[q] = other_core(value)
            later_there = other_core(later)
        if r in late:
            own, at, turned = (later, later_there), late.index(r), 0
        else:
            own, at, turned = (first, first_there), place, len(soon) + 1 if r == 0 else 0
        others = (first, first_there) if r == 0 else (away[r], away_there[r])
        if y_first:
            shapes = [((row_n, chunk, tall), i16), ((row_n, chunk, tall), f32)]
        else:
            shapes = [((chunk, 2 * tall), i16)] * (row_n - 1) + [((chunk, 2 * tall), f32)]
        sums = call(
            "sum_pairs",
            functools.partial(sum_body, at, turned, row_n, y_first),
            scalars,
            [*own, *others, first_there, *kept, *passed],
            shapes,
        )
        if y_first:
            crossed = [other_y(sums[0])]
        else:
            crossed = [shift(value, "row", by + 1) for by, value in enumerate(sums[:-1])]
        before += crossed if place < 2 else sums[:1]
        if y_first:
            own_sum, *coded = call(
                "add_other_y",
                add_y_body,
                scalars,
                [sums[1]] + crossed,
                [((chunk, tall), f32)] + [((chunk, tall), i16)] * (row_n - 1),
            )
            last = [shift(value, "row", by + 1) for by, value in enumerate(coded)]
        else:
            coded, own_sum = call(
                "add_other_x",
                add_x_body,
                scalars,
                [sums[-1]] + crossed,
                [((chunk, tall), i16), ((chunk, tall), f32)],
            )
            last = [other_y(coded)]
        (mine,) = call("round_pairs", round_body, scalars, [own_sum] + last, [((chunk, tall), bf16)])
        rounded[r] = [mine] if r == 0 else [mine, shift(mine, "col", r)]

    done = None
    for group in ([0] + soon, late):
        sources = [value for r in group for value in rounded[r]]
        tile = (TILE, tall), lambda g, s: (g, 0)
        sources += [] if done is None else [(done, *tile)]
        (done,) = call(
            "place_pairs",
            functools.partial(place_body, group, n, col_n, done is not None),
            scalars,
            sources,
            [((columns, tall), bf16, *tile)],
            grid=-(-columns // TILE),
        )
    return done.T


def solution(mesh):
    in_specs = (P("row", "depth"), P("depth", "row", "col"), P("row"), P("depth"))
    out_specs = P(("row", "depth"), "col")
    return jax.shard_map(local, mesh=mesh, in_specs=in_specs, out_specs=out_specs, check_vma=False)
```

```python
import functools

import jax
import jax.numpy as jnp
import numpy as np
from jax import lax
from jax.experimental import pallas as pl
from jax.experimental.pallas import tpu as pltpu
from jax.sharding import PartitionSpec as P

OCC = 100
TOP = 32000.0
STEPS = 256.0
CORES = 2
TILE = 1264
LANES = 128
VMEM_BYTES = 32 * 2**20


def dot_nt(a, b):
    return lax.dot_general(a, b, (((1,), (1,)), ((), ())), preferred_element_type=jnp.float32)


def dot_nn(a, b):
    return lax.dot_general(a, b, (((1,), (0,)), ((), ())), preferred_element_type=jnp.float32)


def divide(value, by):
    whole = jnp.floor((value.astype(jnp.float32) + 0.5) * (1.0 / by)).astype(jnp.int32)
    return whole, value - whole * by


def inside_columns(place, n, z):
    apart, i = divide(place, n)
    j = i + apart + 1
    j = jnp.where(j >= n, j - n, j)
    valid = place < n * (n - 1) // 2
    return jnp.where(valid, i * OCC + z * n + j, -1), jnp.where(valid, j * OCC + z * n + i, -1)


def pair_columns(place, n, z, other, mine):
    half = (n * n + 1) // 2
    first = jnp.logical_xor(z < other, jnp.logical_not(mine))
    count = jnp.where(first, half, n * n - half)
    q, m = divide(place + jnp.where(first, 0, half), n)
    a = jnp.where(z < other, q, m)
    b = jnp.where(z < other, m, q)
    return jnp.where(place < count, a * OCC + other * n + b, -1)


def encode(values):
    largest = jnp.maximum(jnp.max(jnp.abs(values), axis=0, keepdims=True), 1e-30)
    code = jnp.floor(jnp.log2(TOP / largest) * STEPS)
    coded = jnp.round(values * jnp.exp2(code * (1.0 / STEPS)))
    rows = lax.broadcasted_iota(jnp.int32, values.shape, 0)
    coded = jnp.where(rows == values.shape[0] - 1, code, coded)
    return coded.astype(jnp.int32).astype(jnp.int16)


def decode(coded):
    values = coded.astype(jnp.int32).astype(jnp.float32)
    rows = lax.broadcasted_iota(jnp.int32, values.shape, 0)
    last = rows == values.shape[0] - 1
    code = jnp.sum(jnp.where(last, values, 0.0), axis=0, keepdims=True)
    return jnp.where(last, 0.0, values * jnp.exp2(code * (-1.0 / STEPS)))


def call(name, body, scalars, inputs, outputs, grid=None, scratch=()):
    arrays = [entry[0] if isinstance(entry, tuple) else entry for entry in inputs]
    shapes = [jax.ShapeDtypeStruct(entry[0], entry[1]) for entry in outputs]
    if grid is None:
        in_specs = [pl.BlockSpec(memory_space=pltpu.SMEM)] + [pl.BlockSpec(memory_space=pltpu.VMEM)] * len(arrays)
        out_specs = [pl.BlockSpec(memory_space=pltpu.VMEM)] * len(shapes)
        specs = dict(in_specs=in_specs, out_specs=out_specs, scratch_shapes=list(scratch))
    else:
        in_specs, out_specs = [], []
        for entry, array in zip(inputs, arrays):
            block, index = entry[1:] if isinstance(entry, tuple) else (array.shape, lambda g, s, rank=array.ndim: (0,) * rank)
            in_specs.append(pl.BlockSpec(block, index))
        for entry in outputs:
            out_specs.append(pl.BlockSpec(*entry[2:]))
        specs = dict(
            grid_spec=pltpu.PrefetchScalarGridSpec(
                num_scalar_prefetch=1, grid=(grid,), in_specs=in_specs, out_specs=out_specs
            )
        )
    return pl.pallas_call(
        body,
        name=name,
        out_shape=shapes,
        compiler_params=pltpu.CompilerParams(vmem_limit_bytes=VMEM_BYTES),
        cost_estimate=pl.CostEstimate(flops=1, bytes_accessed=1, transcendentals=0),
        **specs,
    )(scalars, *arrays)


def masked_rows(by, row_n, sub, k_here, s_ref, ab_ref, cd_refs, v_refs):
    x, y, core = s_ref[0], s_ref[2], s_ref[3]
    rows, cd_here = v_refs[0].shape
    tall = rows // 4
    q, m = divide(lax.broadcasted_iota(jnp.int32, (k_here, 1), 0), sub)
    wanted = q * (sub * row_n) + lax.rem(x - by + row_n, row_n) * sub + m
    square = (LANES, LANES)
    diagonal = lax.broadcasted_iota(jnp.int32, square, 0) == lax.broadcasted_iota(jnp.int32, square, 1)
    strips = tall // LANES
    blocks = []
    for cd_ref, v_ref in zip(cd_refs, v_refs):
        cd_labels = cd_ref[...].astype(jnp.float32)
        cd = jnp.concatenate([cd_labels[k : k + 1] for k in range(cd_here // LANES)], axis=1)
        for other_y in (1, 0):
            block = lax.rem(y + other_y, 2) * CORES + core
            for strip in range(strips):
                labels = ab_ref[pl.ds(block * strips + strip, 1), :].astype(jnp.float32)
                ab = jnp.sum(jnp.where(diagonal, labels, 0.0), axis=1, keepdims=True)
                start = pl.multiple_of(block * tall + strip * LANES, LANES)
                v = v_ref[pl.ds(start, LANES), :].astype(jnp.float32)
                blocks.append(jnp.where(ab == cd, v, 0.0).astype(jnp.bfloat16))
    return dot_nt(jnp.concatenate(blocks, axis=0), one_hot_rows(wanted, cd_here)).astype(jnp.bfloat16)


def mask_body(by, row_n, sub, s_ref, ab_ref, cd_here, cd_there, v_here, v_there, out_ref):
    k_here = out_ref.shape[1]
    out_ref[...] = masked_rows(by, row_n, sub, k_here, s_ref, ab_ref, (cd_here, cd_there), (v_here, v_there))


def one_hot_rows(columns, width):
    lanes = lax.broadcasted_iota(jnp.int32, (columns.shape[0], width), 1)
    return jnp.where(lanes == columns, 1.0, 0.0).astype(jnp.bfloat16)


def flatten(t_ref, flat_ref):
    columns, wide = t_ref.shape[-1], flat_ref.shape[1]
    flat_ref[:, wide - LANES :] = jnp.zeros((flat_ref.shape[0], LANES), flat_ref.dtype)
    flat_ref[:, :columns] = t_ref[...].reshape(-1, columns)


def send_body(order, n, col_n, s_ref, t_ref, flat_ref, *out_refs):
    flatten(t_ref, flat_ref)
    z = s_ref[1]
    chunk = out_refs[0].shape[0]
    place = lax.broadcasted_iota(jnp.int32, (chunk, 1), 0)
    wanted = [pair_columns(place, n, z, lax.rem(z - r + col_n, col_n), False) for r in order]
    picked = dot_nt(one_hot_rows(jnp.concatenate(wanted, axis=0), flat_ref.shape[1]), flat_ref[...]).astype(jnp.bfloat16)
    for k, out_ref in enumerate(out_refs):
        out_ref[...] = picked[k * chunk : (k + 1) * chunk]


def keep_body(order, n, col_n, row_n, sub, s_ref, flat_ref, t_there, ab_ref, cd_here, cd_there, v_here, v_there, *refs):
    own_here, own_there, kept_ref, flat_there = refs
    flatten(t_there, flat_there)
    z = s_ref[1]
    place = lax.broadcasted_iota(jnp.int32, (own_here.shape[0] // (len(order) + 2), 1), 0)
    inside, turned = inside_columns(place, n, z)
    others = [pair_columns(place, n, z, lax.rem(z + r, col_n), True) for r in order]
    picks = one_hot_rows(jnp.concatenate([inside] + others + [turned], axis=0), flat_ref.shape[1])
    own_here[...] = dot_nt(picks, flat_ref[...]).astype(jnp.bfloat16)
    own_there[...] = dot_nt(picks, flat_there[...]).astype(jnp.bfloat16)
    k_here = kept_ref.shape[1]
    kept_ref[...] = masked_rows(0, row_n, sub, k_here, s_ref, ab_ref, (cd_here, cd_there), (v_here, v_there))


def sum_body(place, turned, groups, y_first, s_ref, own_here, own_there, away_here, away_there, *refs):
    keeps, outs = refs[:groups], refs[groups:]
    chunk, tall = outs[-1].shape[-2:]
    tall = tall if y_first else tall // 2
    mine = slice(place * chunk, (place + 1) * chunk)
    other = slice(turned * chunk, (turned + 1) * chunk)
    left = jnp.concatenate([own_here[mine], own_there[mine], away_here[other], away_there[other]], axis=1)
    for g in range(groups):
        a, b = keeps[g][: 2 * tall], keeps[g][2 * tall :]
        total = dot_nt(left, jnp.concatenate([a, b, -a, -b], axis=1))
        if y_first:
            outs[0][g] = encode(total[:, :tall])
            outs[1][g] = total[:, tall:]
        elif g == 0:
            outs[-1][...] = total
        else:
            outs[g - 1][...] = encode(total)


def add_y_body(s_ref, kept_ref, coded_ref, own_ref, *out_refs):
    for g in range(kept_ref.shape[0]):
        total = kept_ref[g] + decode(coded_ref[g])
        if g == 0:
            own_ref[...] = total
        else:
            out_refs[g - 1][...] = encode(total)


def add_x_body(s_ref, kept_ref, *refs):
    coded_ref, own_ref = refs[-2:]
    total = kept_ref[...]
    for ref in refs[:-2]:
        total = total + decode(ref[...])
    tall = own_ref.shape[1]
    coded_ref[...] = encode(total[:, :tall])
    own_ref[...] = total[:, tall:]


def round_body(s_ref, kept_ref, *refs):
    total = kept_ref[...]
    for ref in refs[:-1]:
        total = total + decode(ref[...])
    refs[-1][...] = total.astype(jnp.bfloat16)


def place_body(order, n, col_n, before, s_ref, *refs):
    out_ref = refs[-1]
    z = s_ref[1]
    chunk = refs[0].shape[0]
    place = lax.broadcasted_iota(jnp.int32, (1, chunk), 1)
    at = lax.broadcasted_iota(jnp.int32, (out_ref.shape[0], chunk), 0) + pl.program_id(0) * out_ref.shape[0]
    signs = []
    for r in order:
        if r == 0:
            inside, turned = inside_columns(place, n, z)
            signs.append(jnp.where(at == inside, 1.0, jnp.where(at == turned, -1.0, 0.0)))
        else:
            plus = pair_columns(place, n, z, lax.rem(z + r, col_n), True)
            minus = pair_columns(place, n, z, lax.rem(z - r + col_n, col_n), False)
            signs.append(jnp.where(at == plus, 1.0, 0.0))
            signs.append(jnp.where(at == minus, -1.0, 0.0))
    signs = jnp.concatenate([sign.astype(jnp.bfloat16) for sign in signs], axis=1)
    values = jnp.concatenate([ref[...] for ref in refs[: 2 * len(order) - order.count(0)]], axis=0)
    total = dot_nn(signs, values)
    if before:
        total = total + refs[-2][...].astype(jnp.float32)
    out_ref[...] = total.astype(jnp.bfloat16)


def local(integrals, amplitudes, ab_irrep, cd_irrep):
    row_n, col_n, depth_n = lax.axis_size("row"), lax.axis_size("col"), lax.axis_size("depth")
    x, z, d = lax.axis_index("row"), lax.axis_index("col"), lax.axis_index("depth")
    y, core = d // CORES, d % CORES
    rows, cd_here = integrals.shape
    blocks, sub, columns = amplitudes.shape
    k_here = blocks * sub
    tall = rows // depth_n
    n = OCC // col_n
    chunk = -(-((n * n + 1) // 2 + 1) // 16) * 16
    far = col_n // 2
    near = [r for r in range(1, col_n) if r != far]
    soon, late = [far] + near[:1], near[1:]
    bf16, i16, f32 = jnp.bfloat16, jnp.int16, jnp.float32

    def shift(array, axis, by):
        count = lax.axis_size(axis)
        return lax.ppermute(array, axis, [(i, (i + by) % count) for i in range(count)])

    def other_core(array):
        return lax.ppermute(array, "depth", [(i, i ^ 1) for i in range(depth_n)])

    def other_y(array):
        return lax.ppermute(array, "depth", [(i, i ^ 2) for i in range(depth_n)])

    def after(values, *earlier):
        return lax.optimization_barrier((values, earlier))[0]

    scalars = jnp.stack([x, z, y, core]).astype(jnp.int32)
    ab_row, cd_row = ab_irrep.reshape(-1, LANES), cd_irrep.reshape(-1, LANES)

    cd_there, v_there, t_there = other_core(cd_row), other_core(integrals), other_core(amplitudes)
    integral_refs = [ab_row, cd_row, cd_there, integrals, v_there]

    kept = [None] * row_n
    gone = scalars
    for by in range(1, row_n):
        (gone,) = call(
            "mask_integrals",
            functools.partial(mask_body, by, row_n, sub),
            scalars,
            integral_refs,
            [((rows, k_here), bf16)],
        )
        kept[by] = shift(gone, "row", -by)

    wide = -(-columns // LANES) * LANES
    flat, *sent = call(
        "send_columns",
        functools.partial(send_body, soon + late, n, col_n),
        scalars,
        [after(amplitudes, gone)],
        [((k_here, wide), bf16)] + [((chunk, k_here), bf16)] * (col_n - 1),
    )
    sent = dict(zip(soon + late, sent))
    away = {r: shift(sent[r], "col", -r) for r in soon}

    own_here, own_there, kept[0] = call(
        "keep_columns",
        functools.partial(keep_body, soon + late, n, col_n, row_n, sub),
        scalars,
        [flat, t_there] + integral_refs,
        [(((col_n + 1) * chunk, k_here), bf16)] * 2 + [((rows, k_here), bf16)],
        scratch=[pltpu.VMEM((k_here, wide), bf16)],
    )

    first_y = {r: r not in soon for r in range(col_n)}
    away_there, crossed, added, rounded = {}, {}, {}, {}

    def sum_pairs(r):
        others = (own_here, own_there) if r == 0 else (away[r], away_there[r])
        place, turned = ([0] + soon + late).index(r), col_n if r == 0 else 0
        if first_y[r]:
            shapes = [((row_n, chunk, tall), i16), ((row_n, chunk, tall), f32)]
        else:
            shapes = [((chunk, 2 * tall), i16)] * (row_n - 1) + [((chunk, 2 * tall), f32)]
        sums = call(
            "sum_pairs",
            functools.partial(sum_body, place, turned, row_n, first_y[r]),
            scalars,
            [own_here, own_there, *others, *kept],
            shapes,
        )
        if first_y[r]:
            crossed[r] = [sums[1], other_y(sums[0])]
        else:
            crossed[r] = [sums[-1]] + [shift(value, "row", by + 1) for by, value in enumerate(sums[:-1])]
        return sums

    def add_pairs(r):
        if first_y[r]:
            own_sum, *coded = call(
                "add_other_y",
                add_y_body,
                scalars,
                crossed[r],
                [((chunk, tall), f32)] + [((chunk, tall), i16)] * (row_n - 1),
            )
            added[r] = [own_sum] + [shift(value, "row", by + 1) for by, value in enumerate(coded)]
        else:
            coded, own_sum = call(
                "add_other_x", add_x_body, scalars, crossed[r], [((chunk, tall), i16), ((chunk, tall), f32)]
            )
            added[r] = [own_sum, other_y(coded)]
        return own_sum

    def round_pairs(r):
        (mine,) = call("round_pairs", round_body, scalars, added[r], [((chunk, tall), bf16)])
        rounded[r] = [mine] if r == 0 else [mine, shift(mine, "col", r)]
        return mine

    inside = sum_pairs(0)
    arrived = after([away[r] for r in soon], inside)
    for r in late:
        away[r] = shift(after(sent[r], arrived), "col", -r)
    for r, value in zip(soon, arrived):
        away_there[r] = other_core(value)
    sums = [sum_pairs(r) for r in soon]
    early = [add_pairs(soon[0]), add_pairs(0)]
    for r in late:
        away_there[r] = other_core(after(away[r], early, sums))
    sums = [sum_pairs(r) for r in late]
    early = [round_pairs(soon[0]), round_pairs(0)]
    for r in soon[1:] + late:
        crossed[r] = after(crossed[r], early)
        add_pairs(r)
    for r in soon[1:] + late:
        added[r] = after(added[r], rounded[soon[0]])
        round_pairs(r)

    done = None
    for group in ([0] + soon, late):
        sources = [value for r in group for value in rounded[r]]
        tile = (TILE, tall), lambda g, s: (g, 0)
        sources += [] if done is None else [(done, *tile)]
        (done,) = call(
            "place_pairs",
            functools.partial(place_body, group, n, col_n, done is not None),
            scalars,
            sources,
            [((columns, tall), bf16, *tile)],
            grid=-(-columns // TILE),
        )
    return done.T


def solution(mesh):
    in_specs = (P("row", "depth"), P("depth", "row", "col"), P("row"), P("depth"))
    out_specs = P(("row", "depth"), "col")
    return jax.shard_map(local, mesh=mesh, in_specs=in_specs, out_specs=out_specs, check_vma=False)
```

```python
import functools

import jax
import jax.numpy as jnp
import numpy as np
from jax import lax
from jax.experimental import pallas as pl
from jax.experimental.pallas import tpu as pltpu
from jax.sharding import PartitionSpec as P

OCC = 100
TOP = 32000.0
STEPS = 256.0
CORES = 2
TILE = 1264
LANES = 128
VMEM_BYTES = 32 * 2**20


def dot_nt(a, b):
    return lax.dot_general(a, b, (((1,), (1,)), ((), ())), preferred_element_type=jnp.float32)


def dot_nn(a, b):
    return lax.dot_general(a, b, (((1,), (0,)), ((), ())), preferred_element_type=jnp.float32)


def divide(value, by):
    whole = jnp.floor((value.astype(jnp.float32) + 0.5) * (1.0 / by)).astype(jnp.int32)
    return whole, value - whole * by


def inside_columns(place, n, z):
    apart, i = divide(place, n)
    j = i + apart + 1
    j = jnp.where(j >= n, j - n, j)
    valid = place < n * (n - 1) // 2
    return jnp.where(valid, i * OCC + z * n + j, -1), jnp.where(valid, j * OCC + z * n + i, -1)


def pair_columns(place, n, z, other, mine):
    half = (n * n + 1) // 2
    first = jnp.logical_xor(z < other, jnp.logical_not(mine))
    count = jnp.where(first, half, n * n - half)
    q, m = divide(place + jnp.where(first, 0, half), n)
    a = jnp.where(z < other, q, m)
    b = jnp.where(z < other, m, q)
    return jnp.where(place < count, a * OCC + other * n + b, -1)


def encode(values):
    largest = jnp.maximum(jnp.max(jnp.abs(values), axis=0, keepdims=True), 1e-30)
    code = jnp.floor(jnp.log2(TOP / largest) * STEPS)
    coded = jnp.round(values * jnp.exp2(code * (1.0 / STEPS)))
    rows = lax.broadcasted_iota(jnp.int32, values.shape, 0)
    coded = jnp.where(rows == values.shape[0] - 1, code, coded)
    return coded.astype(jnp.int32).astype(jnp.int16)


def decode(coded):
    values = coded.astype(jnp.int32).astype(jnp.float32)
    rows = lax.broadcasted_iota(jnp.int32, values.shape, 0)
    last = rows == values.shape[0] - 1
    code = jnp.sum(jnp.where(last, values, 0.0), axis=0, keepdims=True)
    return jnp.where(last, 0.0, values * jnp.exp2(code * (-1.0 / STEPS)))


def call(name, body, scalars, inputs, outputs, grid=None):
    arrays = [entry[0] if isinstance(entry, tuple) else entry for entry in inputs]
    shapes = [jax.ShapeDtypeStruct(entry[0], entry[1]) for entry in outputs]
    if grid is None:
        in_specs = [pl.BlockSpec(memory_space=pltpu.SMEM)] + [pl.BlockSpec(memory_space=pltpu.VMEM)] * len(arrays)
        specs = dict(in_specs=in_specs, out_specs=[pl.BlockSpec(memory_space=pltpu.VMEM)] * len(shapes))
    else:
        in_specs, out_specs = [], []
        for entry, array in zip(inputs, arrays):
            block, index = entry[1:] if isinstance(entry, tuple) else (array.shape, lambda g, s, rank=array.ndim: (0,) * rank)
            in_specs.append(pl.BlockSpec(block, index))
        for entry in outputs:
            out_specs.append(pl.BlockSpec(*entry[2:]))
        specs = dict(
            grid_spec=pltpu.PrefetchScalarGridSpec(
                num_scalar_prefetch=1, grid=(grid,), in_specs=in_specs, out_specs=out_specs
            )
        )
    return pl.pallas_call(
        body,
        name=name,
        out_shape=shapes,
        compiler_params=pltpu.CompilerParams(vmem_limit_bytes=VMEM_BYTES),
        cost_estimate=pl.CostEstimate(flops=1, bytes_accessed=1, transcendentals=0),
        **specs,
    )(scalars, *arrays)


def masked_rows(by, row_n, sub, k_here, s_ref, ab_ref, cd_ref, v_ref):
    x, y, core = s_ref[0], s_ref[2], s_ref[3]
    rows, cd_here = v_ref.shape
    tall = rows // 4
    q, m = divide(lax.broadcasted_iota(jnp.int32, (k_here, 1), 0), sub)
    wanted = q * (sub * row_n) + lax.rem(x - by + row_n, row_n) * sub + m
    square = (LANES, LANES)
    diagonal = lax.broadcasted_iota(jnp.int32, square, 0) == lax.broadcasted_iota(jnp.int32, square, 1)
    cd_labels = cd_ref[...].astype(jnp.float32)
    cd = jnp.concatenate([cd_labels[k : k + 1] for k in range(cd_here // LANES)], axis=1)
    strips = tall // LANES
    blocks = []
    for other_core in (1, 0):
        for other_y in (1, 0):
            block = lax.rem(y + other_y, 2) * CORES + lax.rem(core + other_core, CORES)
            for strip in range(strips):
                labels = ab_ref[pl.ds(block * strips + strip, 1), :].astype(jnp.float32)
                ab = jnp.sum(jnp.where(diagonal, labels, 0.0), axis=1, keepdims=True)
                start = pl.multiple_of(block * tall + strip * LANES, LANES)
                v = v_ref[pl.ds(start, LANES), :].astype(jnp.float32)
                blocks.append(jnp.where(ab == cd, v, 0.0).astype(jnp.bfloat16))
    return dot_nt(jnp.concatenate(blocks, axis=0), one_hot_rows(wanted, cd_here)).astype(jnp.bfloat16)


def mask_body(by, row_n, sub, s_ref, ab_ref, cd_ref, v_ref, out_ref):
    out_ref[...] = masked_rows(by, row_n, sub, out_ref.shape[1], s_ref, ab_ref, cd_ref, v_ref)


def one_hot_rows(columns, width):
    lanes = lax.broadcasted_iota(jnp.int32, (columns.shape[0], width), 1)
    return jnp.where(lanes == columns, 1.0, 0.0).astype(jnp.bfloat16)


def send_body(order, n, col_n, s_ref, t_ref, flat_ref, *out_refs):
    columns, wide = t_ref.shape[-1], flat_ref.shape[1]
    last = wide - LANES
    flat_ref[:, last:] = jnp.zeros((flat_ref.shape[0], LANES), flat_ref.dtype)
    flat_ref[:, :columns] = t_ref[...].reshape(-1, columns)
    z = s_ref[1]
    place = lax.broadcasted_iota(jnp.int32, (out_refs[0].shape[0], 1), 0)
    chunk = out_refs[0].shape[0]
    wanted = [pair_columns(place, n, z, lax.rem(z - r + col_n, col_n), False) for r in order]
    picked = dot_nt(one_hot_rows(jnp.concatenate(wanted, axis=0), flat_ref.shape[1]), flat_ref[...]).astype(jnp.bfloat16)
    for k, out_ref in enumerate(out_refs):
        out_ref[...] = picked[k * chunk : (k + 1) * chunk]


def keep_body(order, n, col_n, row_n, sub, s_ref, flat_ref, ab_ref, cd_ref, v_ref, both_ref, kept_ref):
    z = s_ref[1]
    half, k_here = kept_ref.shape
    pairs = both_ref.shape[0] - half
    place = lax.broadcasted_iota(jnp.int32, (pairs // (len(order) + 1), 1), 0)
    inside, turned = inside_columns(place, n, z)
    picks = [inside if r == 0 else pair_columns(place, n, z, lax.rem(z + r, col_n), True) for r in order] + [turned]
    picked = dot_nt(one_hot_rows(jnp.concatenate(picks, axis=0), flat_ref.shape[1]), flat_ref[...])
    both_ref[:pairs] = picked.astype(jnp.bfloat16)
    masked = masked_rows(0, row_n, sub, k_here, s_ref, ab_ref, cd_ref, v_ref)
    both_ref[pairs:] = masked[:half]
    kept_ref[...] = masked[half:]


def sum_body(first, count, groups, way, s_ref, own_here, own_there, *refs):
    away, refs = refs[: 2 * count], refs[2 * count :]
    keeps, passes, outs = refs[:groups], refs[groups : 2 * groups - 1], refs[2 * groups - 1 :]
    high, tall = outs[-1].shape[-2:]
    tall = tall // 2 if way == "x" else tall
    chunk = high // count
    pairs = own_here.shape[0] - 2 * tall

    def rows(ref):
        return ref[pairs - chunk : pairs] if ref.shape[0] > chunk else ref[...]

    mine = slice(first * chunk, (first + count) * chunk)
    tr = jnp.concatenate([rows(ref) for ref in away[:count]], axis=0)
    tro = jnp.concatenate([rows(ref) for ref in away[count:]], axis=0)
    left = jnp.concatenate([own_here[mine], own_there[mine], tr, tro], axis=1)
    for g in reversed(range(groups)):
        start = keeps[g].shape[0] - 2 * tall
        a = keeps[g][start:]
        b = own_there[pairs:] if g == 0 else passes[g - 1][: 2 * tall]
        total = dot_nt(left, jnp.concatenate([a, b, -a, -b], axis=1))
        if way == "y":
            outs[0][g] = encode(total[:, :tall])
            outs[1][g] = total[:, tall:]
        elif way == "x":
            if g == 0:
                outs[-1][...] = total
            else:
                outs[g - 1][...] = encode(total)
        else:
            outs[2 * g][...] = encode(total[:, :tall])
            outs[2 * g + 1][...] = total[:, tall:] if g == 0 else encode(total[:, tall:])


def add_y_body(s_ref, kept_ref, coded_ref, own_ref, *out_refs):
    for g in range(kept_ref.shape[0]):
        total = kept_ref[g] + decode(coded_ref[g])
        if g == 0:
            own_ref[...] = total
        else:
            out_refs[g - 1][...] = encode(total)


def add_x_body(s_ref, kept_ref, *refs):
    coded_ref, own_ref = refs[-2:]
    total = kept_ref[...]
    for ref in refs[:-2]:
        total = total + decode(ref[...])
    tall = own_ref.shape[1]
    coded_ref[...] = encode(total[:, :tall])
    own_ref[...] = total[:, tall:]


def round_body(count, s_ref, kept_ref, *refs):
    total = kept_ref[...]
    for ref in refs[:-count]:
        total = total + decode(ref[...])
    rounded = total.astype(jnp.bfloat16)
    chunk = rounded.shape[0] // count
    for k, out_ref in enumerate(refs[-count:]):
        out_ref[...] = rounded[k * chunk : (k + 1) * chunk]


def place_body(items, n, col_n, before, s_ref, *refs):
    out_ref = refs[-1]
    z = s_ref[1]
    chunk = refs[0].shape[0]
    place = lax.broadcasted_iota(jnp.int32, (1, chunk), 1)
    at = lax.broadcasted_iota(jnp.int32, (out_ref.shape[0], chunk), 0) + pl.program_id(0) * out_ref.shape[0]
    signs = []
    for r, mine in items:
        if r == 0:
            inside, turned = inside_columns(place, n, z)
            sign = jnp.where(at == inside, 1.0, jnp.where(at == turned, -1.0, 0.0))
        elif mine:
            sign = jnp.where(at == pair_columns(place, n, z, lax.rem(z + r, col_n), True), 1.0, 0.0)
        else:
            sign = jnp.where(at == pair_columns(place, n, z, lax.rem(z - r + col_n, col_n), False), -1.0, 0.0)
        signs.append(sign.astype(jnp.bfloat16))
    values = jnp.concatenate([ref[...] for ref in refs[: len(items)]], axis=0)
    total = dot_nn(jnp.concatenate(signs, axis=1), values)
    if before:
        total = total + refs[-2][...].astype(jnp.float32)
    out_ref[...] = total.astype(jnp.bfloat16)


def local(integrals, amplitudes, ab_irrep, cd_irrep):
    row_n, col_n, depth_n = lax.axis_size("row"), lax.axis_size("col"), lax.axis_size("depth")
    x, z, d = lax.axis_index("row"), lax.axis_index("col"), lax.axis_index("depth")
    y, core = d // CORES, d % CORES
    rows, cd_here = integrals.shape
    blocks, sub, columns = amplitudes.shape
    k_here = blocks * sub
    tall = rows // depth_n
    n = OCC // col_n
    chunk = -(-((n * n + 1) // 2 + 1) // 16) * 16
    far = col_n // 2
    near = [r for r in range(1, col_n) if r != far]
    order = [0] + near + [far]
    bf16, i16, f32 = jnp.bfloat16, jnp.int16, jnp.float32

    def shift(array, axis, by):
        count = lax.axis_size(axis)
        return lax.ppermute(array, axis, [(i, (i + by) % count) for i in range(count)])

    def other_core(array):
        return lax.ppermute(array, "depth", [(i, i ^ 1) for i in range(depth_n)])

    def other_y(array):
        return lax.ppermute(array, "depth", [(i, i ^ 2) for i in range(depth_n)])

    def across(array, by):
        pairs = [(i * depth_n + j, (i + by) % row_n * depth_n + (j ^ 2)) for i in range(row_n) for j in range(depth_n)]
        return lax.ppermute(array, ("row", "depth"), pairs)

    def after(values, *earlier):
        return lax.optimization_barrier((values, earlier))[0]

    scalars = jnp.stack([x, z, y, core]).astype(jnp.int32)
    ab_row, cd_row = ab_irrep.reshape(-1, LANES), cd_irrep.reshape(-1, LANES)

    kept = [None] * row_n
    gone = scalars
    for by in range(1, row_n):
        (gone,) = call(
            "mask_integrals",
            functools.partial(mask_body, by, row_n, sub),
            scalars,
            [ab_row, cd_row, integrals],
            [((rows, k_here), bf16)],
        )
        kept[by] = shift(gone, "row", -by)

    amplitudes, _ = lax.optimization_barrier((amplitudes, gone))
    sent_order = near + [far]
    flat, *sent = call(
        "send_columns",
        functools.partial(send_body, sent_order, n, col_n),
        scalars,
        [amplitudes],
        [((k_here, -(-columns // LANES) * LANES), bf16)] + [((chunk, k_here), bf16)] * len(sent_order),
    )
    away = {r: shift(s, "col", -r) for r, s in zip(near, sent)}

    both, kept[0] = call(
        "keep_columns",
        functools.partial(keep_body, order, n, col_n, row_n, sub),
        scalars,
        [flat, ab_row, cd_row, integrals],
        [(((col_n + 1) * chunk + 2 * tall, k_here), bf16), ((2 * tall, k_here), bf16)],
    )
    far_sent, away = lax.optimization_barrier((sent[-1], away))
    behind, kept[1:], *arrived = lax.optimization_barrier((both, kept[1:], *[away[r] for r in near]))
    away_there = {r: other_core(a) for r, a in zip(near, arrived)}
    both_there = other_core(behind)
    away[far] = shift(far_sent, "col", -far)
    passed = [other_core(a) for a in kept[1:]]

    crossed, added, rounded = {}, {}, {}

    def sum_pairs(group, way):
        first, count = order.index(group[0]), len(group)
        high = count * chunk
        if way == "y":
            shapes = [((row_n, high, tall), i16), ((row_n, high, tall), f32)]
        elif way == "x":
            shapes = [((high, 2 * tall), i16)] * (row_n - 1) + [((high, 2 * tall), f32)]
        else:
            shapes = [((high, tall), i16), ((high, tall), f32)] + [((high, tall), i16)] * (2 * row_n - 2)
        here = [both if r == 0 else away[r] for r in group]
        there = [both_there if r == 0 else away_there[r] for r in group]
        sums = call(
            "sum_pairs",
            functools.partial(sum_body, first, count, row_n, way),
            scalars,
            [both, both_there] + here + there + kept + passed,
            shapes,
        )
        if way == "y":
            crossed[group] = [sums[1], other_y(sums[0])]
        elif way == "x":
            crossed[group] = [sums[-1]] + [shift(value, "row", by + 1) for by, value in enumerate(sums[:-1])]
        else:
            crossed[group] = [sums[1], other_y(sums[0])]
            for by in range(1, row_n):
                crossed[group] += [across(sums[2 * by], by), shift(sums[2 * by + 1], "row", by)]
        return sums

    def add_pairs(group, way):
        high = len(group) * chunk
        if way == "y":
            own_sum, *coded = call(
                "add_other_y",
                add_y_body,
                scalars,
                crossed[group],
                [((high, tall), f32)] + [((high, tall), i16)] * (row_n - 1),
            )
            added[group] = [own_sum] + [shift(value, "row", by + 1) for by, value in enumerate(coded)]
        else:
            coded, own_sum = call(
                "add_other_x", add_x_body, scalars, crossed[group], [((high, tall), i16), ((high, tall), f32)]
            )
            added[group] = [own_sum, other_y(coded)]
        return own_sum

    def round_pairs(group, sums):
        mine = call(
            "round_pairs",
            functools.partial(round_body, len(group)),
            scalars,
            sums,
            [((chunk, tall), bf16)] * len(group),
        )
        for r, value in zip(group, mine):
            rounded[r, True] = value
            if r:
                rounded[r, False] = shift(value, "col", r)
        return mine

    y_group, x_group, last = (0, *near[:1]), tuple(near[1:]), (far,)
    sum_pairs(x_group, "x")
    sums = sum_pairs(y_group, "y")
    early = add_pairs(x_group, "x")
    away[far] = after(away[far], early, sums)
    away_there[far] = other_core(away[far])
    sums = sum_pairs(last, "direct")
    round_pairs(x_group, after(added[x_group], sums))
    early = add_pairs(y_group, "y")
    round_pairs(last, after(crossed[last], early, [rounded[r, False] for r in x_group]))
    round_pairs(y_group, added[y_group])

    done = None
    ends = [(r, False) for r in near[:1] + [far]]
    for items in ([item for item in rounded if item not in ends], ends):
        sources = [rounded[item] for item in items]
        tile = (TILE, tall), lambda g, s: (g, 0)
        sources += [] if done is None else [(done, *tile)]
        (done,) = call(
            "place_pairs",
            functools.partial(place_body, items, n, col_n, done is not None),
            scalars,
            sources,
            [((columns, tall), bf16, *tile)],
            grid=-(-columns // TILE),
        )
    return done.T


def solution(mesh):
    in_specs = (P("row", "depth"), P("depth", "row", "col"), P("row"), P("depth"))
    out_specs = P(("row", "depth"), "col")
    return jax.shard_map(local, mesh=mesh, in_specs=in_specs, out_specs=out_specs, check_vma=False)
```

```python
import functools

import jax
import jax.numpy as jnp
import numpy as np
from jax import lax
from jax.experimental import pallas as pl
from jax.experimental.pallas import tpu as pltpu
from jax.sharding import PartitionSpec as P

OCC = 100
TOP = 32000.0
STEPS = 256.0
CORES = 2
TILE = 1264
LANES = 128
VMEM_BYTES = 32 * 2**20


def dot_nt(a, b):
    return lax.dot_general(a, b, (((1,), (1,)), ((), ())), preferred_element_type=jnp.float32)


def dot_nn(a, b):
    return lax.dot_general(a, b, (((1,), (0,)), ((), ())), preferred_element_type=jnp.float32)


def divide(value, by):
    whole = jnp.floor((value.astype(jnp.float32) + 0.5) * (1.0 / by)).astype(jnp.int32)
    return whole, value - whole * by


def inside_columns(place, n, z):
    apart, i = divide(place, n)
    j = i + apart + 1
    j = jnp.where(j >= n, j - n, j)
    valid = place < n * (n - 1) // 2
    return jnp.where(valid, i * OCC + z * n + j, -1), jnp.where(valid, j * OCC + z * n + i, -1)


def pair_columns(place, n, z, other, mine):
    half = (n * n + 1) // 2
    first = jnp.logical_xor(z < other, jnp.logical_not(mine))
    count = jnp.where(first, half, n * n - half)
    q, m = divide(place + jnp.where(first, 0, half), n)
    a = jnp.where(z < other, q, m)
    b = jnp.where(z < other, m, q)
    return jnp.where(place < count, a * OCC + other * n + b, -1)


def encode(values):
    largest = jnp.maximum(jnp.max(jnp.abs(values), axis=0, keepdims=True), 1e-30)
    code = jnp.floor(jnp.log2(TOP / largest) * STEPS)
    coded = jnp.round(values * jnp.exp2(code * (1.0 / STEPS)))
    rows = lax.broadcasted_iota(jnp.int32, values.shape, 0)
    coded = jnp.where(rows == values.shape[0] - 1, code, coded)
    return coded.astype(jnp.int32).astype(jnp.int16)


def decode(coded):
    values = coded.astype(jnp.int32).astype(jnp.float32)
    rows = lax.broadcasted_iota(jnp.int32, values.shape, 0)
    last = rows == values.shape[0] - 1
    code = jnp.sum(jnp.where(last, values, 0.0), axis=0, keepdims=True)
    return jnp.where(last, 0.0, values * jnp.exp2(code * (-1.0 / STEPS)))


def call(name, body, scalars, inputs, outputs, grid=None):
    arrays = [entry[0] if isinstance(entry, tuple) else entry for entry in inputs]
    shapes = [jax.ShapeDtypeStruct(entry[0], entry[1]) for entry in outputs]
    if grid is None:
        in_specs = [pl.BlockSpec(memory_space=pltpu.SMEM)] + [pl.BlockSpec(memory_space=pltpu.VMEM)] * len(arrays)
        specs = dict(in_specs=in_specs, out_specs=[pl.BlockSpec(memory_space=pltpu.VMEM)] * len(shapes))
    else:
        in_specs, out_specs = [], []
        for entry, array in zip(inputs, arrays):
            block, index = entry[1:] if isinstance(entry, tuple) else (array.shape, lambda g, s, rank=array.ndim: (0,) * rank)
            in_specs.append(pl.BlockSpec(block, index))
        for entry in outputs:
            out_specs.append(pl.BlockSpec(*entry[2:]))
        specs = dict(
            grid_spec=pltpu.PrefetchScalarGridSpec(
                num_scalar_prefetch=1, grid=(grid,), in_specs=in_specs, out_specs=out_specs
            )
        )
    return pl.pallas_call(
        body,
        name=name,
        out_shape=shapes,
        compiler_params=pltpu.CompilerParams(vmem_limit_bytes=VMEM_BYTES),
        cost_estimate=pl.CostEstimate(flops=1, bytes_accessed=1, transcendentals=0),
        **specs,
    )(scalars, *arrays)


def masked_rows(by, row_n, sub, k_here, s_ref, ab_ref, cd_ref, v_ref):
    x, y, core = s_ref[0], s_ref[2], s_ref[3]
    rows, cd_here = v_ref.shape
    tall = rows // 4
    q, m = divide(lax.broadcasted_iota(jnp.int32, (k_here, 1), 0), sub)
    wanted = q * (sub * row_n) + lax.rem(x - by + row_n, row_n) * sub + m
    square = (LANES, LANES)
    diagonal = lax.broadcasted_iota(jnp.int32, square, 0) == lax.broadcasted_iota(jnp.int32, square, 1)
    cd_labels = cd_ref[...].astype(jnp.float32)
    cd = jnp.concatenate([cd_labels[k : k + 1] for k in range(cd_here // LANES)], axis=1)
    strips = tall // LANES
    blocks = []
    for other_core in (1, 0):
        for other_y in (1, 0):
            block = lax.rem(y + other_y, 2) * CORES + lax.rem(core + other_core, CORES)
            for strip in range(strips):
                labels = ab_ref[pl.ds(block * strips + strip, 1), :].astype(jnp.float32)
                ab = jnp.sum(jnp.where(diagonal, labels, 0.0), axis=1, keepdims=True)
                start = pl.multiple_of(block * tall + strip * LANES, LANES)
                v = v_ref[pl.ds(start, LANES), :].astype(jnp.float32)
                blocks.append(jnp.where(ab == cd, v, 0.0).astype(jnp.bfloat16))
    return dot_nt(jnp.concatenate(blocks, axis=0), one_hot_rows(wanted, cd_here)).astype(jnp.bfloat16)


def mask_body(by, row_n, sub, s_ref, ab_ref, cd_ref, v_ref, out_ref):
    out_ref[...] = masked_rows(by, row_n, sub, out_ref.shape[1], s_ref, ab_ref, cd_ref, v_ref)


def one_hot_rows(columns, width):
    lanes = lax.broadcasted_iota(jnp.int32, (columns.shape[0], width), 1)
    return jnp.where(lanes == columns, 1.0, 0.0).astype(jnp.bfloat16)


def send_body(order, n, col_n, s_ref, t_ref, flat_ref, *out_refs):
    columns, wide = t_ref.shape[-1], flat_ref.shape[1]
    last = wide - LANES
    flat_ref[:, last:] = jnp.zeros((flat_ref.shape[0], LANES), flat_ref.dtype)
    flat_ref[:, :columns] = t_ref[...].reshape(-1, columns)
    z = s_ref[1]
    place = lax.broadcasted_iota(jnp.int32, (out_refs[0].shape[0], 1), 0)
    chunk = out_refs[0].shape[0]
    wanted = [pair_columns(place, n, z, lax.rem(z - r + col_n, col_n), False) for r in order]
    picked = dot_nt(one_hot_rows(jnp.concatenate(wanted, axis=0), flat_ref.shape[1]), flat_ref[...]).astype(jnp.bfloat16)
    for k, out_ref in enumerate(out_refs):
        out_ref[...] = picked[k * chunk : (k + 1) * chunk]


def keep_body(order, n, col_n, row_n, sub, s_ref, flat_ref, ab_ref, cd_ref, v_ref, both_ref, kept_ref):
    z = s_ref[1]
    half, k_here = kept_ref.shape
    pairs = both_ref.shape[0] - half
    place = lax.broadcasted_iota(jnp.int32, (pairs // (len(order) + 1), 1), 0)
    inside, turned = inside_columns(place, n, z)
    picks = [inside if r == 0 else pair_columns(place, n, z, lax.rem(z + r, col_n), True) for r in order] + [turned]
    picked = dot_nt(one_hot_rows(jnp.concatenate(picks, axis=0), flat_ref.shape[1]), flat_ref[...])
    both_ref[:pairs] = picked.astype(jnp.bfloat16)
    masked = masked_rows(0, row_n, sub, k_here, s_ref, ab_ref, cd_ref, v_ref)
    both_ref[pairs:] = masked[:half]
    kept_ref[...] = masked[half:]


def sum_body(first, count, groups, way, s_ref, own_here, own_there, *refs):
    away, refs = refs[: 2 * count], refs[2 * count :]
    keeps, passes, outs = refs[:groups], refs[groups : 2 * groups - 1], refs[2 * groups - 1 :]
    high, tall = outs[-1].shape[-2:]
    tall = tall // 2 if way == "x" else tall
    chunk = high // count
    pairs = own_here.shape[0] - 2 * tall

    def rows(ref):
        return ref[pairs - chunk : pairs] if ref.shape[0] > chunk else ref[...]

    mine = slice(first * chunk, (first + count) * chunk)
    tr = jnp.concatenate([rows(ref) for ref in away[:count]], axis=0)
    tro = jnp.concatenate([rows(ref) for ref in away[count:]], axis=0)
    left = jnp.concatenate([own_here[mine], own_there[mine], tr, tro], axis=1)
    for g in reversed(range(groups)):
        start = keeps[g].shape[0] - 2 * tall
        a = keeps[g][start:]
        b = own_there[pairs:] if g == 0 else passes[g - 1][: 2 * tall]
        total = dot_nt(left, jnp.concatenate([a, b, -a, -b], axis=1))
        if way == "y":
            outs[0][g] = encode(total[:, :tall])
            outs[1][g] = total[:, tall:]
        elif way == "x":
            if g == 0:
                outs[-1][...] = total
            else:
                outs[g - 1][...] = encode(total)
        else:
            outs[2 * g][...] = encode(total[:, :tall])
            outs[2 * g + 1][...] = total[:, tall:] if g == 0 else encode(total[:, tall:])


def add_y_body(s_ref, kept_ref, coded_ref, own_ref, *out_refs):
    for g in range(kept_ref.shape[0]):
        total = kept_ref[g] + decode(coded_ref[g])
        if g == 0:
            own_ref[...] = total
        else:
            out_refs[g - 1][...] = encode(total)


def add_x_body(s_ref, kept_ref, *refs):
    coded_ref, own_ref = refs[-2:]
    total = kept_ref[...]
    for ref in refs[:-2]:
        total = total + decode(ref[...])
    tall = own_ref.shape[1]
    coded_ref[...] = encode(total[:, :tall])
    own_ref[...] = total[:, tall:]


def round_body(count, s_ref, kept_ref, *refs):
    total = kept_ref[...]
    for ref in refs[:-count]:
        total = total + decode(ref[...])
    rounded = total.astype(jnp.bfloat16)
    chunk = rounded.shape[0] // count
    for k, out_ref in enumerate(refs[-count:]):
        out_ref[...] = rounded[k * chunk : (k + 1) * chunk]


def place_body(items, n, col_n, before, s_ref, *refs):
    out_ref = refs[-1]
    z = s_ref[1]
    chunk = refs[0].shape[0]
    place = lax.broadcasted_iota(jnp.int32, (1, chunk), 1)
    at = lax.broadcasted_iota(jnp.int32, (out_ref.shape[0], chunk), 0) + pl.program_id(0) * out_ref.shape[0]
    signs = []
    for r, mine in items:
        if r == 0:
            inside, turned = inside_columns(place, n, z)
            sign = jnp.where(at == inside, 1.0, jnp.where(at == turned, -1.0, 0.0))
        elif mine:
            sign = jnp.where(at == pair_columns(place, n, z, lax.rem(z + r, col_n), True), 1.0, 0.0)
        else:
            sign = jnp.where(at == pair_columns(place, n, z, lax.rem(z - r + col_n, col_n), False), -1.0, 0.0)
        signs.append(sign.astype(jnp.bfloat16))
    values = jnp.concatenate([ref[...] for ref in refs[: len(items)]], axis=0)
    total = dot_nn(jnp.concatenate(signs, axis=1), values)
    if before:
        total = total + refs[-2][...].astype(jnp.float32)
    out_ref[...] = total.astype(jnp.bfloat16)


def local(integrals, amplitudes, ab_irrep, cd_irrep):
    row_n, col_n, depth_n = lax.axis_size("row"), lax.axis_size("col"), lax.axis_size("depth")
    x, z, d = lax.axis_index("row"), lax.axis_index("col"), lax.axis_index("depth")
    y, core = d // CORES, d % CORES
    rows, cd_here = integrals.shape
    blocks, sub, columns = amplitudes.shape
    k_here = blocks * sub
    tall = rows // depth_n
    n = OCC // col_n
    chunk = -(-((n * n + 1) // 2 + 1) // 16) * 16
    far = col_n // 2
    near = [r for r in range(1, col_n) if r != far]
    order = [0] + near + [far]
    bf16, i16, f32 = jnp.bfloat16, jnp.int16, jnp.float32

    def shift(array, axis, by):
        count = lax.axis_size(axis)
        return lax.ppermute(array, axis, [(i, (i + by) % count) for i in range(count)])

    def other_core(array):
        return lax.ppermute(array, "depth", [(i, i ^ 1) for i in range(depth_n)])

    def other_y(array):
        return lax.ppermute(array, "depth", [(i, i ^ 2) for i in range(depth_n)])

    def across(array, by):
        pairs = [(i * depth_n + j, (i + by) % row_n * depth_n + (j ^ 2)) for i in range(row_n) for j in range(depth_n)]
        return lax.ppermute(array, ("row", "depth"), pairs)

    def after(values, *earlier):
        return lax.optimization_barrier((values, earlier))[0]

    scalars = jnp.stack([x, z, y, core]).astype(jnp.int32)
    ab_row, cd_row = ab_irrep.reshape(-1, LANES), cd_irrep.reshape(-1, LANES)

    kept = [None] * row_n
    gone = scalars
    for by in range(1, row_n):
        (gone,) = call(
            "mask_integrals",
            functools.partial(mask_body, by, row_n, sub),
            scalars,
            [ab_row, cd_row, integrals],
            [((rows, k_here), bf16)],
        )
        kept[by] = shift(gone, "row", -by)

    amplitudes, _ = lax.optimization_barrier((amplitudes, gone))
    sent_order = near + [far]
    flat, *sent = call(
        "send_columns",
        functools.partial(send_body, sent_order, n, col_n),
        scalars,
        [amplitudes],
        [((k_here, -(-columns // LANES) * LANES), bf16)] + [((chunk, k_here), bf16)] * len(sent_order),
    )
    away = {r: shift(s, "col", -r) for r, s in zip(near, sent)}

    both, kept[0] = call(
        "keep_columns",
        functools.partial(keep_body, order, n, col_n, row_n, sub),
        scalars,
        [flat, ab_row, cd_row, integrals],
        [(((col_n + 1) * chunk + 2 * tall, k_here), bf16), ((2 * tall, k_here), bf16)],
    )
    far_sent, away = lax.optimization_barrier((sent[-1], away))
    behind, kept[1:], *arrived = lax.optimization_barrier((both, kept[1:], *[away[r] for r in near]))
    away_there = {r: other_core(a) for r, a in zip(near, arrived)}
    both_there = other_core(behind)
    away[far] = shift(far_sent, "col", -far)
    passed = [other_core(a) for a in kept[1:]]

    crossed, added, rounded = {}, {}, {}

    def sum_pairs(group, way):
        first, count = order.index(group[0]), len(group)
        high = count * chunk
        if way == "y":
            shapes = [((row_n, high, tall), i16), ((row_n, high, tall), f32)]
        elif way == "x":
            shapes = [((high, 2 * tall), i16)] * (row_n - 1) + [((high, 2 * tall), f32)]
        else:
            shapes = [((high, tall), i16), ((high, tall), f32)] + [((high, tall), i16)] * (2 * row_n - 2)
        here = [both if r == 0 else away[r] for r in group]
        there = [both_there if r == 0 else away_there[r] for r in group]
        sums = call(
            "sum_pairs",
            functools.partial(sum_body, first, count, row_n, way),
            scalars,
            [both, both_there] + here + there + kept + passed,
            shapes,
        )
        if way == "y":
            crossed[group] = [sums[1], other_y(sums[0])]
        elif way == "x":
            crossed[group] = [sums[-1]] + [shift(value, "row", by + 1) for by, value in enumerate(sums[:-1])]
        else:
            crossed[group] = [sums[1], other_y(sums[0])]
            for by in range(1, row_n):
                crossed[group] += [across(sums[2 * by], by), shift(sums[2 * by + 1], "row", by)]
        return sums

    def add_pairs(group, way):
        high = len(group) * chunk
        if way == "y":
            own_sum, *coded = call(
                "add_other_y",
                add_y_body,
                scalars,
                crossed[group],
                [((high, tall), f32)] + [((high, tall), i16)] * (row_n - 1),
            )
            added[group] = [own_sum] + [shift(value, "row", by + 1) for by, value in enumerate(coded)]
        else:
            coded, own_sum = call(
                "add_other_x", add_x_body, scalars, crossed[group], [((high, tall), i16), ((high, tall), f32)]
            )
            added[group] = [own_sum, other_y(coded)]
        return own_sum

    def round_pairs(group, sums):
        mine = call(
            "round_pairs",
            functools.partial(round_body, len(group)),
            scalars,
            sums,
            [((chunk, tall), bf16)] * len(group),
        )
        for r, value in zip(group, mine):
            rounded[r, True] = value
            if r:
                rounded[r, False] = shift(value, "col", r)
        return mine

    y_group, x_group, last = (0, *near[:1]), tuple(near[1:]), (far,)
    sums = sum_pairs(x_group, "x")
    kept[0] = after(kept[0], sums)
    sums = sum_pairs(y_group, "y")
    early = add_pairs(x_group, "x")
    away[far] = after(away[far], early, sums)
    away_there[far] = other_core(away[far])
    sums = sum_pairs(last, "direct")
    round_pairs(x_group, after(added[x_group], sums))
    early = round_pairs(last, after(crossed[last], [rounded[r, False] for r in x_group]))
    crossed[y_group] = after(crossed[y_group], early)
    add_pairs(y_group, "y")
    round_pairs(y_group, added[y_group])

    done = None
    ends = [(r, False) for r in near[:1]]
    for items in ([item for item in rounded if item not in ends], ends):
        sources = [rounded[item] for item in items]
        tile = (TILE, tall), lambda g, s: (g, 0)
        sources += [] if done is None else [(done, *tile)]
        (done,) = call(
            "place_pairs",
            functools.partial(place_body, items, n, col_n, done is not None),
            scalars,
            sources,
            [((columns, tall), bf16, *tile)],
            grid=-(-columns // TILE),
        )
    return done.T


def solution(mesh):
    in_specs = (P("row", "depth"), P("depth", "row", "col"), P("row"), P("depth"))
    out_specs = P(("row", "depth"), "col")
    return jax.shard_map(local, mesh=mesh, in_specs=in_specs, out_specs=out_specs, check_vma=False)
```

```python
import functools

import jax
import jax.numpy as jnp
import numpy as np
from jax import lax
from jax.experimental import pallas as pl
from jax.experimental.pallas import tpu as pltpu
from jax.sharding import PartitionSpec as P

OCC = 100
TOP = 32000.0
STEPS = 256.0
CORES = 2
TILE = 1264
LANES = 128
VMEM_BYTES = 32 * 2**20


def dot_nt(a, b):
    return lax.dot_general(a, b, (((1,), (1,)), ((), ())), preferred_element_type=jnp.float32)


def dot_nn(a, b):
    return lax.dot_general(a, b, (((1,), (0,)), ((), ())), preferred_element_type=jnp.float32)


def divide(value, by):
    whole = jnp.floor((value.astype(jnp.float32) + 0.5) * (1.0 / by)).astype(jnp.int32)
    return whole, value - whole * by


def inside_columns(place, n, z):
    apart, i = divide(place, n)
    j = i + apart + 1
    j = jnp.where(j >= n, j - n, j)
    valid = place < n * (n - 1) // 2
    return jnp.where(valid, i * OCC + z * n + j, -1), jnp.where(valid, j * OCC + z * n + i, -1)


def pair_columns(place, n, z, other, mine):
    half = (n * n + 1) // 2
    first = jnp.logical_xor(z < other, jnp.logical_not(mine))
    count = jnp.where(first, half, n * n - half)
    q, m = divide(place + jnp.where(first, 0, half), n)
    a = jnp.where(z < other, q, m)
    b = jnp.where(z < other, m, q)
    return jnp.where(place < count, a * OCC + other * n + b, -1)


def encode(values):
    largest = jnp.maximum(jnp.max(jnp.abs(values), axis=0, keepdims=True), 1e-30)
    code = jnp.floor(jnp.log2(TOP / largest) * STEPS)
    coded = jnp.round(values * jnp.exp2(code * (1.0 / STEPS)))
    rows = lax.broadcasted_iota(jnp.int32, values.shape, 0)
    coded = jnp.where(rows == values.shape[0] - 1, code, coded)
    return coded.astype(jnp.int32).astype(jnp.int16)


def decode(coded):
    values = coded.astype(jnp.int32).astype(jnp.float32)
    rows = lax.broadcasted_iota(jnp.int32, values.shape, 0)
    last = rows == values.shape[0] - 1
    code = jnp.sum(jnp.where(last, values, 0.0), axis=0, keepdims=True)
    return jnp.where(last, 0.0, values * jnp.exp2(code * (-1.0 / STEPS)))


def call(name, body, scalars, inputs, outputs, grid=None):
    arrays = [entry[0] if isinstance(entry, tuple) else entry for entry in inputs]
    shapes = [jax.ShapeDtypeStruct(entry[0], entry[1]) for entry in outputs]
    if grid is None:
        in_specs = [pl.BlockSpec(memory_space=pltpu.SMEM)] + [pl.BlockSpec(memory_space=pltpu.VMEM)] * len(arrays)
        specs = dict(in_specs=in_specs, out_specs=[pl.BlockSpec(memory_space=pltpu.VMEM)] * len(shapes))
    else:
        in_specs, out_specs = [], []
        for entry, array in zip(inputs, arrays):
            block, index = entry[1:] if isinstance(entry, tuple) else (array.shape, lambda g, s, rank=array.ndim: (0,) * rank)
            in_specs.append(pl.BlockSpec(block, index))
        for entry in outputs:
            out_specs.append(pl.BlockSpec(*entry[2:]))
        specs = dict(
            grid_spec=pltpu.PrefetchScalarGridSpec(
                num_scalar_prefetch=1, grid=(grid,), in_specs=in_specs, out_specs=out_specs
            )
        )
    return pl.pallas_call(
        body,
        name=name,
        out_shape=shapes,
        compiler_params=pltpu.CompilerParams(vmem_limit_bytes=VMEM_BYTES),
        cost_estimate=pl.CostEstimate(flops=1, bytes_accessed=1, transcendentals=0),
        **specs,
    )(scalars, *arrays)


def masked_rows(by, row_n, sub, k_here, s_ref, ab_ref, cd_ref, v_ref):
    x, y, core = s_ref[0], s_ref[2], s_ref[3]
    rows, cd_here = v_ref.shape
    tall = rows // 4
    q, m = divide(lax.broadcasted_iota(jnp.int32, (k_here, 1), 0), sub)
    wanted = q * (sub * row_n) + lax.rem(x - by + row_n, row_n) * sub + m
    square = (LANES, LANES)
    diagonal = lax.broadcasted_iota(jnp.int32, square, 0) == lax.broadcasted_iota(jnp.int32, square, 1)
    cd_labels = cd_ref[...].astype(jnp.float32)
    cd = jnp.concatenate([cd_labels[k : k + 1] for k in range(cd_here // LANES)], axis=1)
    strips = tall // LANES
    blocks = []
    for other_core in (1, 0):
        for other_y in (1, 0):
            block = lax.rem(y + other_y, 2) * CORES + lax.rem(core + other_core, CORES)
            for strip in range(strips):
                labels = ab_ref[pl.ds(block * strips + strip, 1), :].astype(jnp.float32)
                ab = jnp.sum(jnp.where(diagonal, labels, 0.0), axis=1, keepdims=True)
                start = pl.multiple_of(block * tall + strip * LANES, LANES)
                v = v_ref[pl.ds(start, LANES), :].astype(jnp.float32)
                blocks.append(jnp.where(ab == cd, v, 0.0).astype(jnp.bfloat16))
    return dot_nt(jnp.concatenate(blocks, axis=0), one_hot_rows(wanted, cd_here)).astype(jnp.bfloat16)


def mask_body(by, row_n, sub, s_ref, ab_ref, cd_ref, v_ref, out_ref):
    out_ref[...] = masked_rows(by, row_n, sub, out_ref.shape[1], s_ref, ab_ref, cd_ref, v_ref)


def one_hot_rows(columns, width):
    lanes = lax.broadcasted_iota(jnp.int32, (columns.shape[0], width), 1)
    return jnp.where(lanes == columns, 1.0, 0.0).astype(jnp.bfloat16)


def send_body(order, n, col_n, s_ref, t_ref, flat_ref, *out_refs):
    columns, wide = t_ref.shape[-1], flat_ref.shape[1]
    last = wide - LANES
    flat_ref[:, last:] = jnp.zeros((flat_ref.shape[0], LANES), flat_ref.dtype)
    flat_ref[:, :columns] = t_ref[...].reshape(-1, columns)
    z = s_ref[1]
    place = lax.broadcasted_iota(jnp.int32, (out_refs[0].shape[0], 1), 0)
    chunk = out_refs[0].shape[0]
    wanted = [pair_columns(place, n, z, lax.rem(z - r + col_n, col_n), False) for r in order]
    picked = dot_nt(one_hot_rows(jnp.concatenate(wanted, axis=0), flat_ref.shape[1]), flat_ref[...]).astype(jnp.bfloat16)
    for k, out_ref in enumerate(out_refs):
        out_ref[...] = picked[k * chunk : (k + 1) * chunk]


def keep_body(order, n, col_n, row_n, sub, s_ref, flat_ref, ab_ref, cd_ref, v_ref, both_ref, kept_ref):
    z = s_ref[1]
    half, k_here = kept_ref.shape
    pairs = both_ref.shape[0] - half
    place = lax.broadcasted_iota(jnp.int32, (pairs // (len(order) + 1), 1), 0)
    inside, turned = inside_columns(place, n, z)
    picks = [inside if r == 0 else pair_columns(place, n, z, lax.rem(z + r, col_n), True) for r in order] + [turned]
    picked = dot_nt(one_hot_rows(jnp.concatenate(picks, axis=0), flat_ref.shape[1]), flat_ref[...])
    both_ref[:pairs] = picked.astype(jnp.bfloat16)
    masked = masked_rows(0, row_n, sub, k_here, s_ref, ab_ref, cd_ref, v_ref)
    both_ref[pairs:] = masked[:half]
    kept_ref[...] = masked[half:]


def sum_body(first, count, groups, way, s_ref, own_here, own_there, *refs):
    away, refs = refs[: 2 * count], refs[2 * count :]
    keeps, passes, outs = refs[:groups], refs[groups : 2 * groups - 1], refs[2 * groups - 1 :]
    high, tall = outs[-1].shape[-2:]
    tall = tall // 2 if way == "x" else tall
    chunk = high // count
    pairs = own_here.shape[0] - 2 * tall

    def rows(ref):
        return ref[pairs - chunk : pairs] if ref.shape[0] > chunk else ref[...]

    mine = slice(first * chunk, (first + count) * chunk)
    tr = jnp.concatenate([rows(ref) for ref in away[:count]], axis=0)
    tro = jnp.concatenate([rows(ref) for ref in away[count:]], axis=0)
    left = jnp.concatenate([own_here[mine], own_there[mine], tr, tro], axis=1)
    for g in reversed(range(groups)):
        start = keeps[g].shape[0] - 2 * tall
        a = keeps[g][start:]
        b = own_there[pairs:] if g == 0 else passes[g - 1][: 2 * tall]
        total = dot_nt(left, jnp.concatenate([a, b, -a, -b], axis=1))
        if way == "y":
            outs[0][g] = encode(total[:, :tall])
            outs[1][g] = total[:, tall:]
        elif way == "x":
            if g == 0:
                outs[-1][...] = total
            else:
                outs[g - 1][...] = encode(total)
        else:
            outs[2 * g][...] = encode(total[:, :tall])
            outs[2 * g + 1][...] = total[:, tall:] if g == 0 else encode(total[:, tall:])


def add_y_body(s_ref, kept_ref, coded_ref, own_ref, *out_refs):
    for g in range(kept_ref.shape[0]):
        total = kept_ref[g] + decode(coded_ref[g])
        if g == 0:
            own_ref[...] = total
        else:
            out_refs[g - 1][...] = encode(total)


def add_x_body(s_ref, kept_ref, *refs):
    coded_ref, own_ref = refs[-2:]
    total = kept_ref[...]
    for ref in refs[:-2]:
        total = total + decode(ref[...])
    tall = own_ref.shape[1]
    coded_ref[...] = encode(total[:, :tall])
    own_ref[...] = total[:, tall:]


def round_body(count, s_ref, kept_ref, *refs):
    total = kept_ref[...]
    for ref in refs[:-count]:
        total = total + decode(ref[...])
    rounded = total.astype(jnp.bfloat16)
    chunk = rounded.shape[0] // count
    for k, out_ref in enumerate(refs[-count:]):
        out_ref[...] = rounded[k * chunk : (k + 1) * chunk]


def place_body(items, n, col_n, before, s_ref, *refs):
    out_ref = refs[-1]
    z = s_ref[1]
    chunk = refs[0].shape[0]
    place = lax.broadcasted_iota(jnp.int32, (1, chunk), 1)
    at = lax.broadcasted_iota(jnp.int32, (out_ref.shape[0], chunk), 0) + pl.program_id(0) * out_ref.shape[0]
    signs = []
    for r, mine in items:
        if r == 0:
            inside, turned = inside_columns(place, n, z)
            sign = jnp.where(at == inside, 1.0, jnp.where(at == turned, -1.0, 0.0))
        elif mine:
            sign = jnp.where(at == pair_columns(place, n, z, lax.rem(z + r, col_n), True), 1.0, 0.0)
        else:
            sign = jnp.where(at == pair_columns(place, n, z, lax.rem(z - r + col_n, col_n), False), -1.0, 0.0)
        signs.append(sign.astype(jnp.bfloat16))
    values = jnp.concatenate([ref[...] for ref in refs[: len(items)]], axis=0)
    total = dot_nn(jnp.concatenate(signs, axis=1), values)
    if before:
        total = total + refs[-2][...].astype(jnp.float32)
    out_ref[...] = total.astype(jnp.bfloat16)


def local(integrals, amplitudes, ab_irrep, cd_irrep):
    row_n, col_n, depth_n = lax.axis_size("row"), lax.axis_size("col"), lax.axis_size("depth")
    x, z, d = lax.axis_index("row"), lax.axis_index("col"), lax.axis_index("depth")
    y, core = d // CORES, d % CORES
    rows, cd_here = integrals.shape
    blocks, sub, columns = amplitudes.shape
    k_here = blocks * sub
    tall = rows // depth_n
    n = OCC // col_n
    chunk = -(-((n * n + 1) // 2 + 1) // 16) * 16
    far = col_n // 2
    near = [r for r in range(1, col_n) if r != far]
    order = [0] + near + [far]
    bf16, i16, f32 = jnp.bfloat16, jnp.int16, jnp.float32

    def shift(array, axis, by):
        count = lax.axis_size(axis)
        return lax.ppermute(array, axis, [(i, (i + by) % count) for i in range(count)])

    def other_core(array):
        return lax.ppermute(array, "depth", [(i, i ^ 1) for i in range(depth_n)])

    def other_y(array):
        return lax.ppermute(array, "depth", [(i, i ^ 2) for i in range(depth_n)])

    def across(array, by):
        pairs = [(i * depth_n + j, (i + by) % row_n * depth_n + (j ^ 2)) for i in range(row_n) for j in range(depth_n)]
        return lax.ppermute(array, ("row", "depth"), pairs)

    def after(values, *earlier):
        return lax.optimization_barrier((values, earlier))[0]

    scalars = jnp.stack([x, z, y, core]).astype(jnp.int32)
    ab_row, cd_row = ab_irrep.reshape(-1, LANES), cd_irrep.reshape(-1, LANES)

    kept = [None] * row_n
    gone = scalars
    for by in range(1, row_n):
        (gone,) = call(
            "mask_integrals",
            functools.partial(mask_body, by, row_n, sub),
            scalars,
            [ab_row, cd_row, integrals],
            [((rows, k_here), bf16)],
        )
        kept[by] = shift(gone, "row", -by)

    amplitudes, _ = lax.optimization_barrier((amplitudes, gone))
    sent_order = near + [far]
    flat, *sent = call(
        "send_columns",
        functools.partial(send_body, sent_order, n, col_n),
        scalars,
        [amplitudes],
        [((k_here, -(-columns // LANES) * LANES), bf16)] + [((chunk, k_here), bf16)] * len(sent_order),
    )
    away = {r: shift(s, "col", -r) for r, s in zip(near, sent)}

    both, kept[0] = call(
        "keep_columns",
        functools.partial(keep_body, order, n, col_n, row_n, sub),
        scalars,
        [flat, ab_row, cd_row, integrals],
        [(((col_n + 1) * chunk + 2 * tall, k_here), bf16), ((2 * tall, k_here), bf16)],
    )
    far_sent, away = lax.optimization_barrier((sent[-1], away))
    behind, kept[1:], *arrived = lax.optimization_barrier((both, kept[1:], *[away[r] for r in near]))
    away_there = {r: other_core(a) for r, a in zip(near, arrived)}
    both_there = other_core(behind)
    away[far] = shift(far_sent, "col", -far)
    passed = [other_core(a) for a in kept[1:]]

    crossed, added, rounded = {}, {}, {}

    def sum_pairs(group, way):
        first, count = order.index(group[0]), len(group)
        high = count * chunk
        if way == "y":
            shapes = [((row_n, high, tall), i16), ((row_n, high, tall), f32)]
        elif way == "x":
            shapes = [((high, 2 * tall), i16)] * (row_n - 1) + [((high, 2 * tall), f32)]
        else:
            shapes = [((high, tall), i16), ((high, tall), f32)] + [((high, tall), i16)] * (2 * row_n - 2)
        here = [both if r == 0 else away[r] for r in group]
        there = [both_there if r == 0 else away_there[r] for r in group]
        sums = call(
            "sum_pairs",
            functools.partial(sum_body, first, count, row_n, way),
            scalars,
            [both, both_there] + here + there + kept + passed,
            shapes,
        )
        if way == "y":
            crossed[group] = [sums[1], other_y(sums[0])]
        elif way == "x":
            crossed[group] = [sums[-1]] + [shift(value, "row", by + 1) for by, value in enumerate(sums[:-1])]
        else:
            crossed[group] = [sums[1], other_y(sums[0])]
            for by in range(1, row_n):
                crossed[group] += [across(sums[2 * by], by), shift(sums[2 * by + 1], "row", by)]
        return sums

    def add_pairs(group, way):
        high = len(group) * chunk
        if way == "y":
            own_sum, *coded = call(
                "add_other_y",
                add_y_body,
                scalars,
                crossed[group],
                [((high, tall), f32)] + [((high, tall), i16)] * (row_n - 1),
            )
            added[group] = [own_sum] + [shift(value, "row", by + 1) for by, value in enumerate(coded)]
        else:
            coded, own_sum = call(
                "add_other_x", add_x_body, scalars, crossed[group], [((high, tall), i16), ((high, tall), f32)]
            )
            added[group] = [own_sum, other_y(coded)]
        return own_sum

    def round_pairs(group, sums):
        mine = call(
            "round_pairs",
            functools.partial(round_body, len(group)),
            scalars,
            sums,
            [((chunk, tall), bf16)] * len(group),
        )
        for r, value in zip(group, mine):
            rounded[r, True] = value
            if r:
                rounded[r, False] = shift(value, "col", r)
        return mine

    y_group, x_group, last = (0, *near[:1]), tuple(near[1:]), (far,)
    sum_pairs(x_group, "x")
    sums = sum_pairs(y_group, "y")
    early = add_pairs(x_group, "x")
    away[far] = after(away[far], early, sums)
    away_there[far] = other_core(away[far])
    sums = sum_pairs(last, "direct")
    round_pairs(x_group, after(added[x_group], sums))
    add_pairs(y_group, "y")
    early = round_pairs(y_group, added[y_group])
    round_pairs(last, after(crossed[last], early, [rounded[r, False] for r in x_group]))

    done = None
    ends = [(far, False)]
    for items in ([item for item in rounded if item not in ends], ends):
        sources = [rounded[item] for item in items]
        tile = (TILE, tall), lambda g, s: (g, 0)
        sources += [] if done is None else [(done, *tile)]
        (done,) = call(
            "place_pairs",
            functools.partial(place_body, items, n, col_n, done is not None),
            scalars,
            sources,
            [((columns, tall), bf16, *tile)],
            grid=-(-columns // TILE),
        )
    return done.T


def solution(mesh):
    in_specs = (P("row", "depth"), P("depth", "row", "col"), P("row"), P("depth"))
    out_specs = P(("row", "depth"), "col")
    return jax.shard_map(local, mesh=mesh, in_specs=in_specs, out_specs=out_specs, check_vma=False)
```

```python
import functools

import jax
import jax.numpy as jnp
import numpy as np
from jax import lax
from jax.experimental import pallas as pl
from jax.experimental.pallas import tpu as pltpu
from jax.sharding import PartitionSpec as P

OCC = 100
TOP = 32000.0
STEPS = 256.0
CORES = 2
TILE = 1264
LANES = 128
VMEM_BYTES = 32 * 2**20


def dot_nt(a, b):
    return lax.dot_general(a, b, (((1,), (1,)), ((), ())), preferred_element_type=jnp.float32)


def dot_nn(a, b):
    return lax.dot_general(a, b, (((1,), (0,)), ((), ())), preferred_element_type=jnp.float32)


def divide(value, by):
    whole = jnp.floor((value.astype(jnp.float32) + 0.5) * (1.0 / by)).astype(jnp.int32)
    return whole, value - whole * by


def inside_columns(place, n, z):
    apart, i = divide(place, n)
    j = i + apart + 1
    j = jnp.where(j >= n, j - n, j)
    valid = place < n * (n - 1) // 2
    return jnp.where(valid, i * OCC + z * n + j, -1), jnp.where(valid, j * OCC + z * n + i, -1)


def pair_columns(place, n, z, other, mine):
    half = (n * n + 1) // 2
    first = jnp.logical_xor(z < other, jnp.logical_not(mine))
    count = jnp.where(first, half, n * n - half)
    q, m = divide(place + jnp.where(first, 0, half), n)
    a = jnp.where(z < other, q, m)
    b = jnp.where(z < other, m, q)
    return jnp.where(place < count, a * OCC + other * n + b, -1)


def encode(values):
    largest = jnp.maximum(jnp.max(jnp.abs(values), axis=0, keepdims=True), 1e-30)
    code = jnp.floor(jnp.log2(TOP / largest) * STEPS)
    coded = jnp.round(values * jnp.exp2(code * (1.0 / STEPS)))
    rows = lax.broadcasted_iota(jnp.int32, values.shape, 0)
    coded = jnp.where(rows == values.shape[0] - 1, code, coded)
    return coded.astype(jnp.int32).astype(jnp.int16)


def decode(coded):
    values = coded.astype(jnp.int32).astype(jnp.float32)
    rows = lax.broadcasted_iota(jnp.int32, values.shape, 0)
    last = rows == values.shape[0] - 1
    code = jnp.sum(jnp.where(last, values, 0.0), axis=0, keepdims=True)
    return jnp.where(last, 0.0, values * jnp.exp2(code * (-1.0 / STEPS)))


def call(name, body, scalars, inputs, outputs, grid=None):
    arrays = [entry[0] if isinstance(entry, tuple) else entry for entry in inputs]
    shapes = [jax.ShapeDtypeStruct(entry[0], entry[1]) for entry in outputs]
    if grid is None:
        in_specs = [pl.BlockSpec(memory_space=pltpu.SMEM)] + [pl.BlockSpec(memory_space=pltpu.VMEM)] * len(arrays)
        specs = dict(in_specs=in_specs, out_specs=[pl.BlockSpec(memory_space=pltpu.VMEM)] * len(shapes))
    else:
        in_specs, out_specs = [], []
        for entry, array in zip(inputs, arrays):
            block, index = entry[1:] if isinstance(entry, tuple) else (array.shape, lambda g, s, rank=array.ndim: (0,) * rank)
            in_specs.append(pl.BlockSpec(block, index))
        for entry in outputs:
            out_specs.append(pl.BlockSpec(*entry[2:]))
        specs = dict(
            grid_spec=pltpu.PrefetchScalarGridSpec(
                num_scalar_prefetch=1, grid=(grid,), in_specs=in_specs, out_specs=out_specs
            )
        )
    return pl.pallas_call(
        body,
        name=name,
        out_shape=shapes,
        compiler_params=pltpu.CompilerParams(vmem_limit_bytes=VMEM_BYTES),
        cost_estimate=pl.CostEstimate(flops=1, bytes_accessed=1, transcendentals=0),
        **specs,
    )(scalars, *arrays)


def masked_rows(by, row_n, sub, k_here, s_ref, ab_ref, cd_ref, v_ref):
    x, y, core = s_ref[0], s_ref[2], s_ref[3]
    rows, cd_here = v_ref.shape
    tall = rows // 4
    q, m = divide(lax.broadcasted_iota(jnp.int32, (k_here, 1), 0), sub)
    wanted = q * (sub * row_n) + lax.rem(x - by + row_n, row_n) * sub + m
    square = (LANES, LANES)
    diagonal = lax.broadcasted_iota(jnp.int32, square, 0) == lax.broadcasted_iota(jnp.int32, square, 1)
    cd_labels = cd_ref[...].astype(jnp.float32)
    cd = jnp.concatenate([cd_labels[k : k + 1] for k in range(cd_here // LANES)], axis=1)
    strips = tall // LANES
    blocks = []
    for other_core in (1, 0):
        for other_y in (1, 0):
            block = lax.rem(y + other_y, 2) * CORES + lax.rem(core + other_core, CORES)
            for strip in range(strips):
                labels = ab_ref[pl.ds(block * strips + strip, 1), :].astype(jnp.float32)
                ab = jnp.sum(jnp.where(diagonal, labels, 0.0), axis=1, keepdims=True)
                start = pl.multiple_of(block * tall + strip * LANES, LANES)
                v = v_ref[pl.ds(start, LANES), :].astype(jnp.float32)
                blocks.append(jnp.where(ab == cd, v, 0.0).astype(jnp.bfloat16))
    return dot_nt(jnp.concatenate(blocks, axis=0), one_hot_rows(wanted, cd_here)).astype(jnp.bfloat16)


def mask_body(by, row_n, sub, s_ref, ab_ref, cd_ref, v_ref, out_ref):
    out_ref[...] = masked_rows(by, row_n, sub, out_ref.shape[1], s_ref, ab_ref, cd_ref, v_ref)


def one_hot_rows(columns, width):
    lanes = lax.broadcasted_iota(jnp.int32, (columns.shape[0], width), 1)
    return jnp.where(lanes == columns, 1.0, 0.0).astype(jnp.bfloat16)


def send_body(order, n, col_n, s_ref, t_ref, flat_ref, *out_refs):
    columns, wide = t_ref.shape[-1], flat_ref.shape[1]
    last = wide - LANES
    flat_ref[:, last:] = jnp.zeros((flat_ref.shape[0], LANES), flat_ref.dtype)
    flat_ref[:, :columns] = t_ref[...].reshape(-1, columns)
    z = s_ref[1]
    place = lax.broadcasted_iota(jnp.int32, (out_refs[0].shape[0], 1), 0)
    chunk = out_refs[0].shape[0]
    wanted = [pair_columns(place, n, z, lax.rem(z - r + col_n, col_n), False) for r in order]
    picked = dot_nt(one_hot_rows(jnp.concatenate(wanted, axis=0), flat_ref.shape[1]), flat_ref[...]).astype(jnp.bfloat16)
    for k, out_ref in enumerate(out_refs):
        out_ref[...] = picked[k * chunk : (k + 1) * chunk]


def keep_body(order, n, col_n, row_n, sub, s_ref, flat_ref, ab_ref, cd_ref, v_ref, both_ref, kept_ref):
    z = s_ref[1]
    half, k_here = kept_ref.shape
    pairs = both_ref.shape[0] - half
    place = lax.broadcasted_iota(jnp.int32, (pairs // (len(order) + 1), 1), 0)
    inside, turned = inside_columns(place, n, z)
    picks = [inside if r == 0 else pair_columns(place, n, z, lax.rem(z + r, col_n), True) for r in order] + [turned]
    picked = dot_nt(one_hot_rows(jnp.concatenate(picks, axis=0), flat_ref.shape[1]), flat_ref[...])
    both_ref[:pairs] = picked.astype(jnp.bfloat16)
    masked = masked_rows(0, row_n, sub, k_here, s_ref, ab_ref, cd_ref, v_ref)
    both_ref[pairs:] = masked[:half]
    kept_ref[...] = masked[half:]


def sum_body(first, count, groups, way, s_ref, own_here, own_there, *refs):
    away, refs = refs[: 2 * count], refs[2 * count :]
    keeps, passes, outs = refs[:groups], refs[groups : 2 * groups - 1], refs[2 * groups - 1 :]
    high, tall = outs[-1].shape[-2:]
    tall = tall // 2 if way == "x" else tall
    chunk = high // count
    pairs = own_here.shape[0] - 2 * tall

    def rows(ref):
        return ref[pairs - chunk : pairs] if ref.shape[0] > chunk else ref[...]

    mine = slice(first * chunk, (first + count) * chunk)
    tr = jnp.concatenate([rows(ref) for ref in away[:count]], axis=0)
    tro = jnp.concatenate([rows(ref) for ref in away[count:]], axis=0)
    left = jnp.concatenate([own_here[mine], own_there[mine], tr, tro], axis=1)
    for g in reversed(range(groups)):
        start = keeps[g].shape[0] - 2 * tall
        a = keeps[g][start:]
        b = own_there[pairs:] if g == 0 else passes[g - 1][: 2 * tall]
        total = dot_nt(left, jnp.concatenate([a, b, -a, -b], axis=1))
        if way == "y":
            outs[0][g] = encode(total[:, :tall])
            outs[1][g] = total[:, tall:]
        elif way == "x":
            if g == 0:
                outs[-1][...] = total
            else:
                outs[g - 1][...] = encode(total)
        else:
            outs[2 * g][...] = encode(total[:, :tall])
            outs[2 * g + 1][...] = total[:, tall:] if g == 0 else encode(total[:, tall:])


def add_y_body(s_ref, kept_ref, coded_ref, own_ref, *out_refs):
    for g in range(kept_ref.shape[0]):
        total = kept_ref[g] + decode(coded_ref[g])
        if g == 0:
            own_ref[...] = total
        else:
            out_refs[g - 1][...] = encode(total)


def add_x_body(s_ref, kept_ref, *refs):
    coded_ref, own_ref = refs[-2:]
    total = kept_ref[...]
    for ref in refs[:-2]:
        total = total + decode(ref[...])
    tall = own_ref.shape[1]
    coded_ref[...] = encode(total[:, :tall])
    own_ref[...] = total[:, tall:]


def round_body(count, s_ref, kept_ref, *refs):
    total = kept_ref[...]
    for ref in refs[:-count]:
        total = total + decode(ref[...])
    rounded = total.astype(jnp.bfloat16)
    chunk = rounded.shape[0] // count
    for k, out_ref in enumerate(refs[-count:]):
        out_ref[...] = rounded[k * chunk : (k + 1) * chunk]


def place_body(items, n, col_n, before, s_ref, *refs):
    out_ref = refs[-1]
    z = s_ref[1]
    chunk = refs[0].shape[0]
    place = lax.broadcasted_iota(jnp.int32, (1, chunk), 1)
    at = lax.broadcasted_iota(jnp.int32, (out_ref.shape[0], chunk), 0) + pl.program_id(0) * out_ref.shape[0]
    signs = []
    for r, mine in items:
        if r == 0:
            inside, turned = inside_columns(place, n, z)
            sign = jnp.where(at == inside, 1.0, jnp.where(at == turned, -1.0, 0.0))
        elif mine:
            sign = jnp.where(at == pair_columns(place, n, z, lax.rem(z + r, col_n), True), 1.0, 0.0)
        else:
            sign = jnp.where(at == pair_columns(place, n, z, lax.rem(z - r + col_n, col_n), False), -1.0, 0.0)
        signs.append(sign.astype(jnp.bfloat16))
    values = jnp.concatenate([ref[...] for ref in refs[: len(items)]], axis=0)
    total = dot_nn(jnp.concatenate(signs, axis=1), values)
    if before:
        total = total + refs[-2][...].astype(jnp.float32)
    out_ref[...] = total.astype(jnp.bfloat16)


def local(integrals, amplitudes, ab_irrep, cd_irrep):
    row_n, col_n, depth_n = lax.axis_size("row"), lax.axis_size("col"), lax.axis_size("depth")
    x, z, d = lax.axis_index("row"), lax.axis_index("col"), lax.axis_index("depth")
    y, core = d // CORES, d % CORES
    rows, cd_here = integrals.shape
    blocks, sub, columns = amplitudes.shape
    k_here = blocks * sub
    tall = rows // depth_n
    n = OCC // col_n
    chunk = -(-((n * n + 1) // 2 + 1) // 16) * 16
    far = col_n // 2
    near = [r for r in range(1, col_n) if r != far]
    order = [0] + near + [far]
    bf16, i16, f32 = jnp.bfloat16, jnp.int16, jnp.float32

    def shift(array, axis, by):
        count = lax.axis_size(axis)
        return lax.ppermute(array, axis, [(i, (i + by) % count) for i in range(count)])

    def other_core(array):
        return lax.ppermute(array, "depth", [(i, i ^ 1) for i in range(depth_n)])

    def other_y(array):
        return lax.ppermute(array, "depth", [(i, i ^ 2) for i in range(depth_n)])

    def across(array, by):
        pairs = [(i * depth_n + j, (i + by) % row_n * depth_n + (j ^ 2)) for i in range(row_n) for j in range(depth_n)]
        return lax.ppermute(array, ("row", "depth"), pairs)

    def after(values, *earlier):
        return lax.optimization_barrier((values, earlier))[0]

    scalars = jnp.stack([x, z, y, core]).astype(jnp.int32)
    ab_row, cd_row = ab_irrep.reshape(-1, LANES), cd_irrep.reshape(-1, LANES)

    kept = [None] * row_n
    gone = scalars
    for by in range(1, row_n):
        (gone,) = call(
            "mask_integrals",
            functools.partial(mask_body, by, row_n, sub),
            scalars,
            [ab_row, cd_row, integrals],
            [((rows, k_here), bf16)],
        )
        kept[by] = shift(gone, "row", -by)

    amplitudes, _ = lax.optimization_barrier((amplitudes, gone))
    sent_order = near + [far]
    flat, *sent = call(
        "send_columns",
        functools.partial(send_body, sent_order, n, col_n),
        scalars,
        [amplitudes],
        [((k_here, -(-columns // LANES) * LANES), bf16)] + [((chunk, k_here), bf16)] * len(sent_order),
    )
    away = {r: shift(s, "col", -r) for r, s in zip(near, sent)}

    both, kept[0] = call(
        "keep_columns",
        functools.partial(keep_body, order, n, col_n, row_n, sub),
        scalars,
        [flat, ab_row, cd_row, integrals],
        [(((col_n + 1) * chunk + 2 * tall, k_here), bf16), ((2 * tall, k_here), bf16)],
    )
    far_sent, away = lax.optimization_barrier((sent[-1], away))
    behind, kept[1:], *arrived = lax.optimization_barrier((both, kept[1:], *[away[r] for r in near]))
    away_there = {r: other_core(a) for r, a in zip(near, arrived)}
    both_there = other_core(behind)
    away[far] = shift(far_sent, "col", -far)
    passed = [other_core(a) for a in kept[1:]]

    crossed, added, rounded = {}, {}, {}

    def sum_pairs(group, way):
        first, count = order.index(group[0]), len(group)
        high = count * chunk
        if way == "y":
            shapes = [((row_n, high, tall), i16), ((row_n, high, tall), f32)]
        elif way == "x":
            shapes = [((high, 2 * tall), i16)] * (row_n - 1) + [((high, 2 * tall), f32)]
        else:
            shapes = [((high, tall), i16), ((high, tall), f32)] + [((high, tall), i16)] * (2 * row_n - 2)
        here = [both if r == 0 else away[r] for r in group]
        there = [both_there if r == 0 else away_there[r] for r in group]
        sums = call(
            "sum_pairs",
            functools.partial(sum_body, first, count, row_n, way),
            scalars,
            [both, both_there] + here + there + kept + passed,
            shapes,
        )
        if way == "y":
            crossed[group] = [sums[1], other_y(sums[0])]
        elif way == "x":
            crossed[group] = [sums[-1]] + [shift(value, "row", by + 1) for by, value in enumerate(sums[:-1])]
        else:
            crossed[group] = [sums[1], other_y(sums[0])]
            for by in range(1, row_n):
                crossed[group] += [across(sums[2 * by], by), shift(sums[2 * by + 1], "row", by)]
        return sums

    def add_pairs(group, way):
        high = len(group) * chunk
        if way == "y":
            own_sum, *coded = call(
                "add_other_y",
                add_y_body,
                scalars,
                crossed[group],
                [((high, tall), f32)] + [((high, tall), i16)] * (row_n - 1),
            )
            added[group] = [own_sum] + [shift(value, "row", by + 1) for by, value in enumerate(coded)]
        else:
            coded, own_sum = call(
                "add_other_x", add_x_body, scalars, crossed[group], [((high, tall), i16), ((high, tall), f32)]
            )
            added[group] = [own_sum, coded]
        return own_sum

    def round_pairs(group, sums):
        mine = call(
            "round_pairs",
            functools.partial(round_body, len(group)),
            scalars,
            sums,
            [((chunk, tall), bf16)] * len(group),
        )
        for r, value in zip(group, mine):
            rounded[r, True] = value
            if r:
                rounded[r, False] = shift(value, "col", r)
        return mine

    y_group, x_group, last = (0, *near[:1]), tuple(near[1:]), (far,)
    sum_pairs(x_group, "x")
    sums = sum_pairs(y_group, "y")
    early = add_pairs(x_group, "x")
    away[far] = after(away[far], early, sums)
    away_there[far] = other_core(away[far])
    sums = sum_pairs(last, "direct")
    own_sum, coded = after(added[x_group], sums)
    added[x_group] = [own_sum, other_y(coded)]
    add_pairs(y_group, "y")
    early = round_pairs(y_group, added[y_group])
    round_pairs(x_group, added[x_group])
    round_pairs(last, after(crossed[last], early, rounded[x_group[0], True]))

    done = None
    ends = [(far, False)]
    for items in ([item for item in rounded if item not in ends], ends):
        sources = [rounded[item] for item in items]
        tile = (TILE, tall), lambda g, s: (g, 0)
        sources += [] if done is None else [(done, *tile)]
        (done,) = call(
            "place_pairs",
            functools.partial(place_body, items, n, col_n, done is not None),
            scalars,
            sources,
            [((columns, tall), bf16, *tile)],
            grid=-(-columns // TILE),
        )
    return done.T


def solution(mesh):
    in_specs = (P("row", "depth"), P("depth", "row", "col"), P("row"), P("depth"))
    out_specs = P(("row", "depth"), "col")
    return jax.shard_map(local, mesh=mesh, in_specs=in_specs, out_specs=out_specs, check_vma=False)
```

```python
import functools

import jax
import jax.numpy as jnp
import numpy as np
from jax import lax
from jax.experimental import pallas as pl
from jax.experimental.pallas import tpu as pltpu
from jax.sharding import PartitionSpec as P

OCC = 100
TOP = 32000.0
STEPS = 256.0
CORES = 2
TILE = 1264
LANES = 128
VMEM_BYTES = 32 * 2**20


def dot_nt(a, b):
    return lax.dot_general(a, b, (((1,), (1,)), ((), ())), preferred_element_type=jnp.float32)


def dot_nn(a, b):
    return lax.dot_general(a, b, (((1,), (0,)), ((), ())), preferred_element_type=jnp.float32)


def divide(value, by):
    whole = jnp.floor((value.astype(jnp.float32) + 0.5) * (1.0 / by)).astype(jnp.int32)
    return whole, value - whole * by


def inside_columns(place, n, z):
    apart, i = divide(place, n)
    j = i + apart + 1
    j = jnp.where(j >= n, j - n, j)
    valid = place < n * (n - 1) // 2
    return jnp.where(valid, i * OCC + z * n + j, -1), jnp.where(valid, j * OCC + z * n + i, -1)


def pair_columns(place, n, z, other, mine):
    half = (n * n + 1) // 2
    first = jnp.logical_xor(z < other, jnp.logical_not(mine))
    count = jnp.where(first, half, n * n - half)
    q, m = divide(place + jnp.where(first, 0, half), n)
    a = jnp.where(z < other, q, m)
    b = jnp.where(z < other, m, q)
    return jnp.where(place < count, a * OCC + other * n + b, -1)


def encode(values):
    largest = jnp.maximum(jnp.max(jnp.abs(values), axis=0, keepdims=True), 1e-30)
    code = jnp.floor(jnp.log2(TOP / largest) * STEPS)
    coded = jnp.round(values * jnp.exp2(code * (1.0 / STEPS)))
    rows = lax.broadcasted_iota(jnp.int32, values.shape, 0)
    coded = jnp.where(rows == values.shape[0] - 1, code, coded)
    return coded.astype(jnp.int32).astype(jnp.int16)


def decode(coded):
    values = coded.astype(jnp.int32).astype(jnp.float32)
    rows = lax.broadcasted_iota(jnp.int32, values.shape, 0)
    last = rows == values.shape[0] - 1
    code = jnp.sum(jnp.where(last, values, 0.0), axis=0, keepdims=True)
    return jnp.where(last, 0.0, values * jnp.exp2(code * (-1.0 / STEPS)))


def call(name, body, scalars, inputs, outputs, grid=None):
    arrays = [entry[0] if isinstance(entry, tuple) else entry for entry in inputs]
    shapes = [jax.ShapeDtypeStruct(entry[0], entry[1]) for entry in outputs]
    if grid is None:
        in_specs = [pl.BlockSpec(memory_space=pltpu.SMEM)] + [pl.BlockSpec(memory_space=pltpu.VMEM)] * len(arrays)
        specs = dict(in_specs=in_specs, out_specs=[pl.BlockSpec(memory_space=pltpu.VMEM)] * len(shapes))
    else:
        in_specs, out_specs = [], []
        for entry, array in zip(inputs, arrays):
            block, index = entry[1:] if isinstance(entry, tuple) else (array.shape, lambda g, s, rank=array.ndim: (0,) * rank)
            in_specs.append(pl.BlockSpec(block, index))
        for entry in outputs:
            out_specs.append(pl.BlockSpec(*entry[2:]))
        specs = dict(
            grid_spec=pltpu.PrefetchScalarGridSpec(
                num_scalar_prefetch=1, grid=(grid,), in_specs=in_specs, out_specs=out_specs
            )
        )
    return pl.pallas_call(
        body,
        name=name,
        out_shape=shapes,
        compiler_params=pltpu.CompilerParams(vmem_limit_bytes=VMEM_BYTES),
        cost_estimate=pl.CostEstimate(flops=1, bytes_accessed=1, transcendentals=0),
        **specs,
    )(scalars, *arrays)


def masked_rows(by, row_n, sub, k_here, s_ref, ab_ref, cd_ref, v_ref):
    x, y, core = s_ref[0], s_ref[2], s_ref[3]
    rows, cd_here = v_ref.shape
    tall = rows // 4
    q, m = divide(lax.broadcasted_iota(jnp.int32, (k_here, 1), 0), sub)
    wanted = q * (sub * row_n) + lax.rem(x - by + row_n, row_n) * sub + m
    square = (LANES, LANES)
    diagonal = lax.broadcasted_iota(jnp.int32, square, 0) == lax.broadcasted_iota(jnp.int32, square, 1)
    cd_labels = cd_ref[...].astype(jnp.float32)
    cd = jnp.concatenate([cd_labels[k : k + 1] for k in range(cd_here // LANES)], axis=1)
    strips = tall // LANES
    blocks = []
    for other_core in (1, 0):
        for other_y in (1, 0):
            block = lax.rem(y + other_y, 2) * CORES + lax.rem(core + other_core, CORES)
            for strip in range(strips):
                labels = ab_ref[pl.ds(block * strips + strip, 1), :].astype(jnp.float32)
                ab = jnp.sum(jnp.where(diagonal, labels, 0.0), axis=1, keepdims=True)
                start = pl.multiple_of(block * tall + strip * LANES, LANES)
                v = v_ref[pl.ds(start, LANES), :].astype(jnp.float32)
                blocks.append(jnp.where(ab == cd, v, 0.0).astype(jnp.bfloat16))
    return dot_nt(jnp.concatenate(blocks, axis=0), one_hot_rows(wanted, cd_here)).astype(jnp.bfloat16)


def mask_body(by, row_n, sub, s_ref, ab_ref, cd_ref, v_ref, pass_ref, keep_ref):
    masked = masked_rows(by, row_n, sub, keep_ref.shape[1], s_ref, ab_ref, cd_ref, v_ref)
    pass_ref[...] = masked[: pass_ref.shape[0]]
    keep_ref[...] = masked[pass_ref.shape[0] :]


def one_hot_rows(columns, width):
    lanes = lax.broadcasted_iota(jnp.int32, (columns.shape[0], width), 1)
    return jnp.where(lanes == columns, 1.0, 0.0).astype(jnp.bfloat16)


def send_body(order, n, col_n, s_ref, t_ref, flat_ref, *out_refs):
    columns, wide = t_ref.shape[-1], flat_ref.shape[1]
    last = wide - LANES
    flat_ref[:, last:] = jnp.zeros((flat_ref.shape[0], LANES), flat_ref.dtype)
    flat_ref[:, :columns] = t_ref[...].reshape(-1, columns)
    z = s_ref[1]
    place = lax.broadcasted_iota(jnp.int32, (out_refs[0].shape[0], 1), 0)
    chunk = out_refs[0].shape[0]
    wanted = [pair_columns(place, n, z, lax.rem(z - r + col_n, col_n), False) for r in order]
    picked = dot_nt(one_hot_rows(jnp.concatenate(wanted, axis=0), flat_ref.shape[1]), flat_ref[...]).astype(jnp.bfloat16)
    for k, out_ref in enumerate(out_refs):
        out_ref[...] = picked[k * chunk : (k + 1) * chunk]


def keep_body(order, n, col_n, row_n, sub, s_ref, flat_ref, ab_ref, cd_ref, v_ref, both_ref, kept_ref):
    z = s_ref[1]
    half, k_here = kept_ref.shape
    pairs = both_ref.shape[0] - half
    place = lax.broadcasted_iota(jnp.int32, (pairs // (len(order) + 1), 1), 0)
    inside, turned = inside_columns(place, n, z)
    picks = [inside if r == 0 else pair_columns(place, n, z, lax.rem(z + r, col_n), True) for r in order] + [turned]
    picked = dot_nt(one_hot_rows(jnp.concatenate(picks, axis=0), flat_ref.shape[1]), flat_ref[...])
    both_ref[:pairs] = picked.astype(jnp.bfloat16)
    masked = masked_rows(0, row_n, sub, k_here, s_ref, ab_ref, cd_ref, v_ref)
    both_ref[pairs:] = masked[:half]
    kept_ref[...] = masked[half:]


def sum_body(first, count, groups, way, s_ref, own_here, own_there, *refs):
    away, refs = refs[: 2 * count], refs[2 * count :]
    keeps, passes, outs = refs[:groups], refs[groups : 2 * groups - 1], refs[2 * groups - 1 :]
    high, tall = outs[-1].shape[-2:]
    tall = tall // 2 if way == "x" else tall
    chunk = high // count
    pairs = own_here.shape[0] - 2 * tall

    def rows(ref):
        return ref[pairs - chunk : pairs] if ref.shape[0] > chunk else ref[...]

    mine = slice(first * chunk, (first + count) * chunk)
    tr = jnp.concatenate([rows(ref) for ref in away[:count]], axis=0)
    tro = jnp.concatenate([rows(ref) for ref in away[count:]], axis=0)
    left = jnp.concatenate([own_here[mine], own_there[mine], tr, tro], axis=1)
    for g in reversed(range(groups)):
        start = keeps[g].shape[0] - 2 * tall
        a = keeps[g][start:]
        b = own_there[pairs:] if g == 0 else passes[g - 1][: 2 * tall]
        total = dot_nt(left, jnp.concatenate([a, b, -a, -b], axis=1))
        if way == "y":
            outs[0][g] = encode(total[:, :tall])
            outs[1][g] = total[:, tall:]
        elif way == "x":
            if g == 0:
                outs[-1][...] = total
            else:
                outs[g - 1][...] = encode(total)
        else:
            outs[2 * g][...] = encode(total[:, :tall])
            outs[2 * g + 1][...] = total[:, tall:] if g == 0 else encode(total[:, tall:])


def add_y_body(s_ref, kept_ref, coded_ref, own_ref, *out_refs):
    for g in range(kept_ref.shape[0]):
        total = kept_ref[g] + decode(coded_ref[g])
        if g == 0:
            own_ref[...] = total
        else:
            out_refs[g - 1][...] = encode(total)


def add_x_body(s_ref, kept_ref, *refs):
    coded_ref, own_ref = refs[-2:]
    total = kept_ref[...]
    for ref in refs[:-2]:
        total = total + decode(ref[...])
    tall = own_ref.shape[1]
    coded_ref[...] = encode(total[:, :tall])
    own_ref[...] = total[:, tall:]


def round_body(count, s_ref, kept_ref, *refs):
    total = kept_ref[...]
    for ref in refs[:-count]:
        total = total + decode(ref[...])
    rounded = total.astype(jnp.bfloat16)
    chunk = rounded.shape[0] // count
    for k, out_ref in enumerate(refs[-count:]):
        out_ref[...] = rounded[k * chunk : (k + 1) * chunk]


def place_body(items, n, col_n, before, s_ref, *refs):
    out_ref = refs[-1]
    z = s_ref[1]
    chunk = refs[0].shape[0]
    place = lax.broadcasted_iota(jnp.int32, (1, chunk), 1)
    at = lax.broadcasted_iota(jnp.int32, (out_ref.shape[0], chunk), 0) + pl.program_id(0) * out_ref.shape[0]
    signs = []
    for r, mine in items:
        if r == 0:
            inside, turned = inside_columns(place, n, z)
            sign = jnp.where(at == inside, 1.0, jnp.where(at == turned, -1.0, 0.0))
        elif mine:
            sign = jnp.where(at == pair_columns(place, n, z, lax.rem(z + r, col_n), True), 1.0, 0.0)
        else:
            sign = jnp.where(at == pair_columns(place, n, z, lax.rem(z - r + col_n, col_n), False), -1.0, 0.0)
        signs.append(sign.astype(jnp.bfloat16))
    values = jnp.concatenate([ref[...] for ref in refs[: len(items)]], axis=0)
    total = dot_nn(jnp.concatenate(signs, axis=1), values)
    if before:
        total = total + refs[-2][...].astype(jnp.float32)
    out_ref[...] = total.astype(jnp.bfloat16)


def local(integrals, amplitudes, ab_irrep, cd_irrep):
    row_n, col_n, depth_n = lax.axis_size("row"), lax.axis_size("col"), lax.axis_size("depth")
    x, z, d = lax.axis_index("row"), lax.axis_index("col"), lax.axis_index("depth")
    y, core = d // CORES, d % CORES
    rows, cd_here = integrals.shape
    blocks, sub, columns = amplitudes.shape
    k_here = blocks * sub
    tall = rows // depth_n
    n = OCC // col_n
    chunk = -(-((n * n + 1) // 2 + 1) // 16) * 16
    far = col_n // 2
    near = [r for r in range(1, col_n) if r != far]
    order = [0] + near + [far]
    bf16, i16, f32 = jnp.bfloat16, jnp.int16, jnp.float32

    def shift(array, axis, by):
        count = lax.axis_size(axis)
        return lax.ppermute(array, axis, [(i, (i + by) % count) for i in range(count)])

    def other_core(array):
        return lax.ppermute(array, "depth", [(i, i ^ 1) for i in range(depth_n)])

    def other_y(array):
        return lax.ppermute(array, "depth", [(i, i ^ 2) for i in range(depth_n)])

    def across(array, by):
        pairs = [(i * depth_n + j, (i + by) % row_n * depth_n + (j ^ 2)) for i in range(row_n) for j in range(depth_n)]
        return lax.ppermute(array, ("row", "depth"), pairs)

    def after(values, *earlier):
        return lax.optimization_barrier((values, earlier))[0]

    scalars = jnp.stack([x, z, y, core]).astype(jnp.int32)
    ab_row, cd_row = ab_irrep.reshape(-1, LANES), cd_irrep.reshape(-1, LANES)

    kept, passed = [None] * row_n, [None] * row_n
    stay = scalars
    for by in range(1, row_n):
        gone, stay = call(
            "mask_integrals",
            functools.partial(mask_body, by, row_n, sub),
            scalars,
            [ab_row, cd_row, integrals],
            [((2 * tall, k_here), bf16)] * 2,
        )
        passed[by], kept[by] = shift(gone, "row", -by), shift(stay, "row", -by)

    amplitudes, _ = lax.optimization_barrier((amplitudes, stay))
    sent_order = near + [far]
    flat, *sent = call(
        "send_columns",
        functools.partial(send_body, sent_order, n, col_n),
        scalars,
        [amplitudes],
        [((k_here, -(-columns // LANES) * LANES), bf16)] + [((chunk, k_here), bf16)] * len(sent_order),
    )
    away = {r: shift(s, "col", -r) for r, s in zip(near, sent)}

    both, kept[0] = call(
        "keep_columns",
        functools.partial(keep_body, order, n, col_n, row_n, sub),
        scalars,
        [flat, ab_row, cd_row, integrals],
        [(((col_n + 1) * chunk + 2 * tall, k_here), bf16), ((2 * tall, k_here), bf16)],
    )
    far_sent, away = lax.optimization_barrier((sent[-1], away))
    arrived = lax.optimization_barrier((both, kept[1:], passed[1:], *[away[r] for r in near]))
    behind, kept[1:], passed, *arrived = arrived
    away_there = {r: other_core(a) for r, a in zip(near, arrived)}
    both_there = other_core(behind)
    away[far] = shift(far_sent, "col", -far)
    passed = [other_core(a) for a in passed]

    crossed, added, rounded = {}, {}, {}

    def sum_pairs(group, way):
        first, count = order.index(group[0]), len(group)
        high = count * chunk
        if way == "y":
            shapes = [((row_n, high, tall), i16), ((row_n, high, tall), f32)]
        elif way == "x":
            shapes = [((high, 2 * tall), i16)] * (row_n - 1) + [((high, 2 * tall), f32)]
        else:
            shapes = [((high, tall), i16), ((high, tall), f32)] + [((high, tall), i16)] * (2 * row_n - 2)
        here = [both if r == 0 else away[r] for r in group]
        there = [both_there if r == 0 else away_there[r] for r in group]
        sums = call(
            "sum_pairs",
            functools.partial(sum_body, first, count, row_n, way),
            scalars,
            [both, both_there] + here + there + kept + passed,
            shapes,
        )
        if way == "y":
            crossed[group] = [sums[1], other_y(sums[0])]
        elif way == "x":
            crossed[group] = [sums[-1]] + [shift(value, "row", by + 1) for by, value in enumerate(sums[:-1])]
        else:
            crossed[group] = [sums[1], other_y(sums[0])]
            for by in range(1, row_n):
                crossed[group] += [across(sums[2 * by], by), shift(sums[2 * by + 1], "row", by)]
        return sums

    def add_pairs(group, way):
        high = len(group) * chunk
        if way == "y":
            own_sum, *coded = call(
                "add_other_y",
                add_y_body,
                scalars,
                crossed[group],
                [((high, tall), f32)] + [((high, tall), i16)] * (row_n - 1),
            )
            added[group] = [own_sum] + [shift(value, "row", by + 1) for by, value in enumerate(coded)]
        else:
            coded, own_sum = call(
                "add_other_x", add_x_body, scalars, crossed[group], [((high, tall), i16), ((high, tall), f32)]
            )
            added[group] = [own_sum, other_y(coded)]
        return own_sum

    def round_pairs(group, sums):
        mine = call(
            "round_pairs",
            functools.partial(round_body, len(group)),
            scalars,
            sums,
            [((chunk, tall), bf16)] * len(group),
        )
        for r, value in zip(group, mine):
            rounded[r, True] = value
            if r:
                rounded[r, False] = shift(value, "col", r)
        return mine

    y_group, x_group, last = (0, *near[:1]), tuple(near[1:]), (far,)
    sum_pairs(x_group, "x")
    sums = sum_pairs(y_group, "y")
    early = add_pairs(x_group, "x")
    away[far] = after(away[far], early, sums)
    away_there[far] = other_core(away[far])
    sums = sum_pairs(last, "direct")
    round_pairs(x_group, after(added[x_group], sums))
    add_pairs(y_group, "y")
    early = round_pairs(y_group, added[y_group])
    round_pairs(last, after(crossed[last], early, [rounded[r, False] for r in x_group]))

    done = None
    ends = [(far, False)]
    for items in ([item for item in rounded if item not in ends], ends):
        sources = [rounded[item] for item in items]
        tile = (TILE, tall), lambda g, s: (g, 0)
        sources += [] if done is None else [(done, *tile)]
        (done,) = call(
            "place_pairs",
            functools.partial(place_body, items, n, col_n, done is not None),
            scalars,
            sources,
            [((columns, tall), bf16, *tile)],
            grid=-(-columns // TILE),
        )
    return done.T


def solution(mesh):
    in_specs = (P("row", "depth"), P("depth", "row", "col"), P("row"), P("depth"))
    out_specs = P(("row", "depth"), "col")
    return jax.shard_map(local, mesh=mesh, in_specs=in_specs, out_specs=out_specs, check_vma=False)
```

```python
import functools

import jax
import jax.numpy as jnp
import numpy as np
from jax import lax
from jax.experimental import pallas as pl
from jax.experimental.pallas import tpu as pltpu
from jax.sharding import PartitionSpec as P

OCC = 100
TOP = 32000.0
STEPS = 256.0
CORES = 2
TILE = 1264
LANES = 128
VMEM_BYTES = 32 * 2**20


def dot_nt(a, b):
    return lax.dot_general(a, b, (((1,), (1,)), ((), ())), preferred_element_type=jnp.float32)


def dot_nn(a, b):
    return lax.dot_general(a, b, (((1,), (0,)), ((), ())), preferred_element_type=jnp.float32)


def divide(value, by):
    whole = jnp.floor((value.astype(jnp.float32) + 0.5) * (1.0 / by)).astype(jnp.int32)
    return whole, value - whole * by


def inside_columns(place, n, z):
    apart, i = divide(place, n)
    j = i + apart + 1
    j = jnp.where(j >= n, j - n, j)
    valid = place < n * (n - 1) // 2
    return jnp.where(valid, i * OCC + z * n + j, -1), jnp.where(valid, j * OCC + z * n + i, -1)


def pair_columns(place, n, z, other, mine):
    half = (n * n + 1) // 2
    first = jnp.logical_xor(z < other, jnp.logical_not(mine))
    count = jnp.where(first, half, n * n - half)
    q, m = divide(place + jnp.where(first, 0, half), n)
    a = jnp.where(z < other, q, m)
    b = jnp.where(z < other, m, q)
    return jnp.where(place < count, a * OCC + other * n + b, -1)


def encode(values):
    largest = jnp.maximum(jnp.max(jnp.abs(values), axis=0, keepdims=True), 1e-30)
    code = jnp.floor(jnp.log2(TOP / largest) * STEPS)
    coded = jnp.round(values * jnp.exp2(code * (1.0 / STEPS)))
    rows = lax.broadcasted_iota(jnp.int32, values.shape, 0)
    coded = jnp.where(rows == values.shape[0] - 1, code, coded)
    return coded.astype(jnp.int32).astype(jnp.int16)


def decode(coded):
    values = coded.astype(jnp.int32).astype(jnp.float32)
    rows = lax.broadcasted_iota(jnp.int32, values.shape, 0)
    last = rows == values.shape[0] - 1
    code = jnp.sum(jnp.where(last, values, 0.0), axis=0, keepdims=True)
    return jnp.where(last, 0.0, values * jnp.exp2(code * (-1.0 / STEPS)))


def call(name, body, scalars, inputs, outputs, grid=None):
    arrays = [entry[0] if isinstance(entry, tuple) else entry for entry in inputs]
    shapes = [jax.ShapeDtypeStruct(entry[0], entry[1]) for entry in outputs]
    if grid is None:
        in_specs = [pl.BlockSpec(memory_space=pltpu.SMEM)] + [pl.BlockSpec(memory_space=pltpu.VMEM)] * len(arrays)
        specs = dict(in_specs=in_specs, out_specs=[pl.BlockSpec(memory_space=pltpu.VMEM)] * len(shapes))
    else:
        in_specs, out_specs = [], []
        for entry, array in zip(inputs, arrays):
            block, index = entry[1:] if isinstance(entry, tuple) else (array.shape, lambda g, s, rank=array.ndim: (0,) * rank)
            in_specs.append(pl.BlockSpec(block, index))
        for entry in outputs:
            out_specs.append(pl.BlockSpec(*entry[2:]))
        specs = dict(
            grid_spec=pltpu.PrefetchScalarGridSpec(
                num_scalar_prefetch=1, grid=(grid,), in_specs=in_specs, out_specs=out_specs
            )
        )
    return pl.pallas_call(
        body,
        name=name,
        out_shape=shapes,
        compiler_params=pltpu.CompilerParams(vmem_limit_bytes=VMEM_BYTES),
        cost_estimate=pl.CostEstimate(flops=1, bytes_accessed=1, transcendentals=0),
        **specs,
    )(scalars, *arrays)


def masked_rows(by, row_n, sub, k_here, s_ref, ab_ref, cd_ref, v_ref):
    x, y, core = s_ref[0], s_ref[2], s_ref[3]
    rows, cd_here = v_ref.shape
    tall = rows // 4
    q, m = divide(lax.broadcasted_iota(jnp.int32, (k_here, 1), 0), sub)
    wanted = q * (sub * row_n) + lax.rem(x - by + row_n, row_n) * sub + m
    square = (LANES, LANES)
    diagonal = lax.broadcasted_iota(jnp.int32, square, 0) == lax.broadcasted_iota(jnp.int32, square, 1)
    cd_labels = cd_ref[...].astype(jnp.float32)
    cd = jnp.concatenate([cd_labels[k : k + 1] for k in range(cd_here // LANES)], axis=1)
    strips = tall // LANES
    blocks = []
    for other_core in (1, 0):
        for other_y in (1, 0):
            block = lax.rem(y + other_y, 2) * CORES + lax.rem(core + other_core, CORES)
            for strip in range(strips):
                labels = ab_ref[pl.ds(block * strips + strip, 1), :].astype(jnp.float32)
                ab = jnp.sum(jnp.where(diagonal, labels, 0.0), axis=1, keepdims=True)
                start = pl.multiple_of(block * tall + strip * LANES, LANES)
                v = v_ref[pl.ds(start, LANES), :].astype(jnp.float32)
                blocks.append(jnp.where(ab == cd, v, 0.0).astype(jnp.bfloat16))
    return dot_nt(jnp.concatenate(blocks, axis=0), one_hot_rows(wanted, cd_here)).astype(jnp.bfloat16)


def mask_body(by, row_n, sub, s_ref, ab_ref, cd_ref, v_ref, pass_ref, keep_ref):
    masked = masked_rows(by, row_n, sub, keep_ref.shape[1], s_ref, ab_ref, cd_ref, v_ref)
    pass_ref[...] = masked[: pass_ref.shape[0]]
    keep_ref[...] = masked[pass_ref.shape[0] :]


def one_hot_rows(columns, width):
    lanes = lax.broadcasted_iota(jnp.int32, (columns.shape[0], width), 1)
    return jnp.where(lanes == columns, 1.0, 0.0).astype(jnp.bfloat16)


def send_body(order, n, col_n, s_ref, t_ref, flat_ref, *out_refs):
    columns, wide = t_ref.shape[-1], flat_ref.shape[1]
    last = wide - LANES
    flat_ref[:, last:] = jnp.zeros((flat_ref.shape[0], LANES), flat_ref.dtype)
    flat_ref[:, :columns] = t_ref[...].reshape(-1, columns)
    z = s_ref[1]
    place = lax.broadcasted_iota(jnp.int32, (out_refs[0].shape[0], 1), 0)
    chunk = out_refs[0].shape[0]
    wanted = [pair_columns(place, n, z, lax.rem(z - r + col_n, col_n), False) for r in order]
    picked = dot_nt(one_hot_rows(jnp.concatenate(wanted, axis=0), flat_ref.shape[1]), flat_ref[...]).astype(jnp.bfloat16)
    for k, out_ref in enumerate(out_refs):
        out_ref[...] = picked[k * chunk : (k + 1) * chunk]


def keep_body(order, n, col_n, row_n, sub, s_ref, flat_ref, ab_ref, cd_ref, v_ref, both_ref, kept_ref, far_ref):
    z = s_ref[1]
    half, k_here = kept_ref.shape
    pairs = both_ref.shape[0] - half
    place = lax.broadcasted_iota(jnp.int32, (pairs // (len(order) + 1), 1), 0)
    inside, turned = inside_columns(place, n, z)
    picks = [inside if r == 0 else pair_columns(place, n, z, lax.rem(z + r, col_n), True) for r in order] + [turned]
    picks.append(pair_columns(place, n, z, lax.rem(z - order[-1] + col_n, col_n), False))
    picked = dot_nt(one_hot_rows(jnp.concatenate(picks, axis=0), flat_ref.shape[1]), flat_ref[...])
    both_ref[:pairs] = picked[:pairs].astype(jnp.bfloat16)
    far_ref[...] = picked[pairs:].astype(jnp.bfloat16)
    masked = masked_rows(0, row_n, sub, k_here, s_ref, ab_ref, cd_ref, v_ref)
    both_ref[pairs:] = masked[:half]
    kept_ref[...] = masked[half:]


def sum_body(first, count, groups, way, s_ref, own_here, own_there, *refs):
    away, refs = refs[: 2 * count], refs[2 * count :]
    keeps, passes, outs = refs[:groups], refs[groups : 2 * groups - 1], refs[2 * groups - 1 :]
    high, tall = outs[-1].shape[-2:]
    tall = tall // 2 if way == "x" else tall
    chunk = high // count
    pairs = own_here.shape[0] - 2 * tall

    def rows(ref):
        return ref[pairs - chunk : pairs] if ref.shape[0] > chunk else ref[...]

    mine = slice(first * chunk, (first + count) * chunk)
    tr = jnp.concatenate([rows(ref) for ref in away[:count]], axis=0)
    tro = jnp.concatenate([rows(ref) for ref in away[count:]], axis=0)
    left = jnp.concatenate([own_here[mine], own_there[mine], tr, tro], axis=1)
    for g in reversed(range(groups)):
        start = keeps[g].shape[0] - 2 * tall
        a = keeps[g][start:]
        b = own_there[pairs:] if g == 0 else passes[g - 1][: 2 * tall]
        total = dot_nt(left, jnp.concatenate([a, b, -a, -b], axis=1))
        if way == "y":
            outs[0][g] = encode(total[:, :tall])
            outs[1][g] = total[:, tall:]
        elif way == "x":
            if g == 0:
                outs[-1][...] = total
            else:
                outs[g - 1][...] = encode(total)
        else:
            outs[2 * g][...] = encode(total[:, :tall])
            outs[2 * g + 1][...] = total[:, tall:] if g == 0 else encode(total[:, tall:])


def add_y_body(s_ref, kept_ref, coded_ref, own_ref, *out_refs):
    for g in range(kept_ref.shape[0]):
        total = kept_ref[g] + decode(coded_ref[g])
        if g == 0:
            own_ref[...] = total
        else:
            out_refs[g - 1][...] = encode(total)


def add_x_body(s_ref, kept_ref, *refs):
    coded_ref, own_ref = refs[-2:]
    total = kept_ref[...]
    for ref in refs[:-2]:
        total = total + decode(ref[...])
    tall = own_ref.shape[1]
    coded_ref[...] = encode(total[:, :tall])
    own_ref[...] = total[:, tall:]


def round_body(count, s_ref, kept_ref, *refs):
    total = kept_ref[...]
    for ref in refs[:-count]:
        total = total + decode(ref[...])
    rounded = total.astype(jnp.bfloat16)
    chunk = rounded.shape[0] // count
    for k, out_ref in enumerate(refs[-count:]):
        out_ref[...] = rounded[k * chunk : (k + 1) * chunk]


def place_body(items, n, col_n, before, s_ref, *refs):
    out_ref = refs[-1]
    z = s_ref[1]
    chunk = refs[0].shape[0]
    place = lax.broadcasted_iota(jnp.int32, (1, chunk), 1)
    at = lax.broadcasted_iota(jnp.int32, (out_ref.shape[0], chunk), 0) + pl.program_id(0) * out_ref.shape[0]
    signs = []
    for r, mine in items:
        if r == 0:
            inside, turned = inside_columns(place, n, z)
            sign = jnp.where(at == inside, 1.0, jnp.where(at == turned, -1.0, 0.0))
        elif mine:
            sign = jnp.where(at == pair_columns(place, n, z, lax.rem(z + r, col_n), True), 1.0, 0.0)
        else:
            sign = jnp.where(at == pair_columns(place, n, z, lax.rem(z - r + col_n, col_n), False), -1.0, 0.0)
        signs.append(sign.astype(jnp.bfloat16))
    values = jnp.concatenate([ref[...] for ref in refs[: len(items)]], axis=0)
    total = dot_nn(jnp.concatenate(signs, axis=1), values)
    if before:
        total = total + refs[-2][...].astype(jnp.float32)
    out_ref[...] = total.astype(jnp.bfloat16)


def local(integrals, amplitudes, ab_irrep, cd_irrep):
    row_n, col_n, depth_n = lax.axis_size("row"), lax.axis_size("col"), lax.axis_size("depth")
    x, z, d = lax.axis_index("row"), lax.axis_index("col"), lax.axis_index("depth")
    y, core = d // CORES, d % CORES
    rows, cd_here = integrals.shape
    blocks, sub, columns = amplitudes.shape
    k_here = blocks * sub
    tall = rows // depth_n
    n = OCC // col_n
    chunk = -(-((n * n + 1) // 2 + 1) // 16) * 16
    far = col_n // 2
    near = [r for r in range(1, col_n) if r != far]
    order = [0] + near + [far]
    bf16, i16, f32 = jnp.bfloat16, jnp.int16, jnp.float32

    def shift(array, axis, by):
        count = lax.axis_size(axis)
        return lax.ppermute(array, axis, [(i, (i + by) % count) for i in range(count)])

    def other_core(array):
        return lax.ppermute(array, "depth", [(i, i ^ 1) for i in range(depth_n)])

    def other_y(array):
        return lax.ppermute(array, "depth", [(i, i ^ 2) for i in range(depth_n)])

    def across(array, by):
        pairs = [(i * depth_n + j, (i + by) % row_n * depth_n + (j ^ 2)) for i in range(row_n) for j in range(depth_n)]
        return lax.ppermute(array, ("row", "depth"), pairs)

    def after(values, *earlier):
        return lax.optimization_barrier((values, earlier))[0]

    scalars = jnp.stack([x, z, y, core]).astype(jnp.int32)
    ab_row, cd_row = ab_irrep.reshape(-1, LANES), cd_irrep.reshape(-1, LANES)

    kept, passed = [None] * row_n, [None] * row_n
    stay = scalars
    for by in range(1, row_n):
        gone, stay = call(
            "mask_integrals",
            functools.partial(mask_body, by, row_n, sub),
            scalars,
            [ab_row, cd_row, integrals],
            [((2 * tall, k_here), bf16)] * 2,
        )
        passed[by], kept[by] = shift(gone, "row", -by), shift(stay, "row", -by)

    amplitudes, _ = lax.optimization_barrier((amplitudes, stay))
    sent_order = near
    flat, *sent = call(
        "send_columns",
        functools.partial(send_body, sent_order, n, col_n),
        scalars,
        [amplitudes],
        [((k_here, -(-columns // LANES) * LANES), bf16)] + [((chunk, k_here), bf16)] * len(near),
    )
    away = {r: shift(s, "col", -r) for r, s in zip(near, sent)}

    both, kept[0], far_sent = call(
        "keep_columns",
        functools.partial(keep_body, order, n, col_n, row_n, sub),
        scalars,
        [flat, ab_row, cd_row, integrals],
        [(((col_n + 1) * chunk + 2 * tall, k_here), bf16), ((2 * tall, k_here), bf16), ((chunk, k_here), bf16)],
    )
    far_sent, away = lax.optimization_barrier((far_sent, away))
    arrived = lax.optimization_barrier((both, kept[1:], passed[1:], *[away[r] for r in near]))
    behind, kept[1:], passed, *arrived = arrived
    away_there = {r: other_core(a) for r, a in zip(near, arrived)}
    both_there = other_core(behind)
    away[far] = shift(far_sent, "col", -far)
    passed = [other_core(a) for a in passed]

    crossed, added, rounded = {}, {}, {}

    def sum_pairs(group, way):
        first, count = order.index(group[0]), len(group)
        high = count * chunk
        if way == "y":
            shapes = [((row_n, high, tall), i16), ((row_n, high, tall), f32)]
        elif way == "x":
            shapes = [((high, 2 * tall), i16)] * (row_n - 1) + [((high, 2 * tall), f32)]
        else:
            shapes = [((high, tall), i16), ((high, tall), f32)] + [((high, tall), i16)] * (2 * row_n - 2)
        here = [both if r == 0 else away[r] for r in group]
        there = [both_there if r == 0 else away_there[r] for r in group]
        sums = call(
            "sum_pairs",
            functools.partial(sum_body, first, count, row_n, way),
            scalars,
            [both, both_there] + here + there + kept + passed,
            shapes,
        )
        if way == "y":
            crossed[group] = [sums[1], other_y(sums[0])]
        elif way == "x":
            crossed[group] = [sums[-1]] + [shift(value, "row", by + 1) for by, value in enumerate(sums[:-1])]
        else:
            crossed[group] = [sums[1], other_y(sums[0])]
            for by in range(1, row_n):
                crossed[group] += [across(sums[2 * by], by), shift(sums[2 * by + 1], "row", by)]
        return sums

    def add_pairs(group, way):
        high = len(group) * chunk
        if way == "y":
            own_sum, *coded = call(
                "add_other_y",
                add_y_body,
                scalars,
                crossed[group],
                [((high, tall), f32)] + [((high, tall), i16)] * (row_n - 1),
            )
            added[group] = [own_sum] + [shift(value, "row", by + 1) for by, value in enumerate(coded)]
        else:
            coded, own_sum = call(
                "add_other_x", add_x_body, scalars, crossed[group], [((high, tall), i16), ((high, tall), f32)]
            )
            added[group] = [own_sum, other_y(coded)]
        return own_sum

    def round_pairs(group, sums):
        mine = call(
            "round_pairs",
            functools.partial(round_body, len(group)),
            scalars,
            sums,
            [((chunk, tall), bf16)] * len(group),
        )
        for r, value in zip(group, mine):
            rounded[r, True] = value
            if r:
                rounded[r, False] = shift(value, "col", r)
        return mine

    y_group, x_group, last = (0, *near[:1]), tuple(near[1:]), (far,)
    sum_pairs(x_group, "x")
    sums = sum_pairs(y_group, "y")
    early = add_pairs(x_group, "x")
    away[far] = after(away[far], early, sums)
    away_there[far] = other_core(away[far])
    sums = sum_pairs(last, "direct")
    round_pairs(x_group, after(added[x_group], sums))
    add_pairs(y_group, "y")
    early = round_pairs(y_group, added[y_group])
    round_pairs(last, after(crossed[last], early, [rounded[r, False] for r in x_group]))

    done = None
    ends = [(far, False)]
    for items in ([item for item in rounded if item not in ends], ends):
        sources = [rounded[item] for item in items]
        tile = (TILE, tall), lambda g, s: (g, 0)
        sources += [] if done is None else [(done, *tile)]
        (done,) = call(
            "place_pairs",
            functools.partial(place_body, items, n, col_n, done is not None),
            scalars,
            sources,
            [((columns, tall), bf16, *tile)],
            grid=-(-columns // TILE),
        )
    return done.T


def solution(mesh):
    in_specs = (P("row", "depth"), P("depth", "row", "col"), P("row"), P("depth"))
    out_specs = P(("row", "depth"), "col")
    return jax.shard_map(local, mesh=mesh, in_specs=in_specs, out_specs=out_specs, check_vma=False)
```
